128 devices in a mesh: rows: 8 (over y_hi, z), cent: 16 (over y_lo, x, core).
Axes of the slice: x: 4, y: 4 (y_hi: 2, y_lo: 2; y = y_hi * 2 + y_lo), z: 4, core: 2. Of those that a mesh axis runs over, the one named last changes fastest.
Arguments:
- train_rows: float32 [32768, 64], P('rows'), may hold values from -6 to 6
- centre_index: int32 [16384], P('cent'), may hold values from 0 to 32767
- precond: bfloat16 [16384, 16384], P('cent', 'rows'), as said below
- coefficients: float32 [16384, 128], P(('rows', 'cent')), may hold values from -6 to 6
- residual: float32 [16384, 128], P(('rows', 'cent')), may hold values from -6 to 6
- direction: float32 [16384, 128], P(('rows', 'cent')), may hold values from -6 to 6
Outputs:
- coef_next: float32 [16384, 128], P(('rows', 'cent'))
- residual_next: float32 [16384, 128], P(('rows', 'cent'))
- direction_next: float32 [16384, 128], P(('rows', 'cent'))
The draws below stay inside these ranges and needn't reach their ends.
Inputs may be any that keep to these rules, and one draw needn't show every extreme that they name: precond is zero below its diagonal.
All inputs are finite; a program needn't handle non-finite values.
Results may differ from the reference program's by a relative error of at most 0.0047.
Values may be sent and summed in bfloat16 or wider, within the bound.
No kernel may reach another device: no remote copies, remote signals or barrier semaphores. Data moves between devices by JAX's collectives and lax.ppermute only.
A program may use at most 64 MiB of HBM per device.

```python
import math
import jax
import jax.numpy as jnp
from jax import lax

ROWS_DEV = 4096
CENTRES = 16384
FEAT = 64
OUTS = 128
TRAIN = 32768


def draw_precond(key, part):
    first, second = jax.random.split(jax.random.fold_in(key, 11))
    upper_part = jax.random.normal(first, (CENTRES, CENTRES), jnp.float32) * CENTRES ** (-0.5)
    diag_vals = jnp.exp(jax.random.uniform(second, (CENTRES,), jnp.float32, math.log(0.5), math.log(2.0)))
    row_ids = jnp.arange(CENTRES)[:, None]
    col_ids = jnp.arange(CENTRES)[None, :]
    matrix = jnp.where(col_ids > row_ids, upper_part, 0.0) + jnp.where(col_ids == row_ids, diag_vals[:, None], 0.0)
    return matrix.astype(jnp.bfloat16)


def draw_train_rows(key, part):
    subkeys = jax.random.split(jax.random.fold_in(key, 23), 4)
    groups = max(TRAIN // 64, 2)
    member = jax.random.randint(subkeys[0], (TRAIN,), 0, groups)
    cluster_mean = 1.2 * jax.random.normal(subkeys[1], (groups, FEAT), jnp.float32)
    spread = jnp.full((groups, 1), 0.5, jnp.float32)
    jitter = jax.random.normal(subkeys[3], (TRAIN, FEAT), jnp.float32)
    points = cluster_mean[member] + spread[member] * jitter
    return jnp.clip(points, -6.0, 6.0)


def plant(entries, own_key, least, top_value):
    spot = [jax.random.randint(jax.random.fold_in(own_key, axis), (), 0, length) for axis, length in enumerate(entries.shape)]
    longest = entries.shape.index(max(entries.shape))
    beside = spot[:longest] + [(spot[longest] + 1) % entries.shape[longest]] + spot[longest + 1:]
    return entries.at[tuple(spot)].set(least).at[tuple(beside)].set(top_value)


def levels(own_key, dims, cuts, low, high):
    def one(axis_at, blocks):
        heights = jax.random.uniform(jax.random.fold_in(jax.random.fold_in(own_key, 6), axis_at), (blocks,), jnp.float32, low / len(cuts), high / len(cuts))
        return jnp.repeat(jnp.exp(heights), dims[axis_at] // blocks).reshape((-1,) + (1,) * (len(dims) - axis_at - 1))

    gain = one(*cuts[0])
    for cut in cuts[1:]:
        gain = gain * one(*cut)
    return gain


def scatter_about(own_key, dims, deviation, most, shards=(), held_as=jnp.bfloat16):
    values = deviation * jax.random.normal(own_key, dims, jnp.float32)
    if shards:
        values = values * levels(own_key, dims, shards, -0.22, 0.18)
    return jnp.clip(values, -most, most).astype(held_as)


def setup_inputs(seed: int = 0) -> dict:
    key_of = jax.random.split(jax.random.key(seed), 7)
    return {
        "train_rows": draw_train_rows(jax.random.fold_in(key_of[6], 71), 0),
        "centre_index": plant(jax.random.randint(key_of[1], (CENTRES,), 0, TRAIN), jax.random.fold_in(key_of[1], 1), 0, TRAIN - 1).astype(jnp.int32),
        "precond": draw_precond(jax.random.fold_in(key_of[6], 71), 0),
        "coefficients": scatter_about(key_of[3], (CENTRES, OUTS), 1.0, 6.0, ((0, 128),), jnp.float32),
        "residual": scatter_about(key_of[4], (CENTRES, OUTS), 1.0, 6.0, ((0, 128),), jnp.float32),
        "direction": scatter_about(key_of[5], (CENTRES, OUTS), 1.0, 6.0, ((0, 128),), jnp.float32),
    }


ridge_weight = 0.1


def kernel_tile(block_rows, centres):
    row_sq = jnp.sum(block_rows * block_rows, axis=1)
    cen_sq = jnp.sum(centres * centres, axis=1)
    cross = jnp.dot(block_rows, centres.T, precision=lax.Precision.HIGHEST, preferred_element_type=jnp.float32)
    distance = row_sq[:, None] + cen_sq[None, :] - 2.0 * cross
    return jnp.exp(-(2.0 / FEAT) * distance).astype(jnp.bfloat16)


def reference(train_rows, centre_index, precond, coefficients, residual, direction):
    centres = train_rows[centre_index.astype(jnp.int32)]
    block_size = min(ROWS_DEV, 1024)
    row_blocks = train_rows.reshape(TRAIN // block_size, block_size, FEAT)
    dir_low = direction.astype(jnp.bfloat16)
    coef_field = jnp.dot(precond, dir_low, preferred_element_type=jnp.float32).astype(jnp.bfloat16)

    def forward(block_rows):
        return jnp.dot(kernel_tile(block_rows, centres), coef_field, preferred_element_type=jnp.float32).astype(jnp.bfloat16)

    fitted = lax.map(forward, row_blocks)

    def accumulate(total, pair):
        block_rows, fitted_block = pair
        tile = kernel_tile(block_rows, centres)
        return total + lax.dot_general(tile, fitted_block, (((0,), (0,)), ((), ())), preferred_element_type=jnp.float32), None

    grad, unused = lax.scan(accumulate, jnp.zeros((CENTRES, OUTS), jnp.float32), (row_blocks, fitted))
    grad_low = (grad * (float(TRAIN) ** -0.5)).astype(jnp.bfloat16)
    image = lax.dot_general(precond, grad_low, (((0,), (0,)), ((), ())), preferred_element_type=jnp.float32)
    image = image + ridge_weight * direction
    norm_old = jnp.sum(residual * residual)
    curvature = jnp.sum(direction * image)
    step_size = norm_old / curvature
    coef_next = coefficients + step_size * direction
    residual_next = residual - step_size * image
    norm_new = jnp.sum(residual_next * residual_next)
    direction_next = residual_next + (norm_new / norm_old) * direction
    return coef_next, residual_next, direction_next
```

```python
import math

import jax
import jax.numpy as jnp
import numpy as np
from jax import lax
from jax.experimental import pallas as pl
from jax.experimental.pallas import tpu as pltpu
from jax.sharding import Mesh
from jax.sharding import PartitionSpec as P

FEAT = 64
OUTS = 128
ridge_weight = 0.1
F32, BF16 = jnp.float32, jnp.bfloat16

FINE = (("yh", 2), ("z", 4), ("yl", 2), ("x", 4), ("core", 2))
ROWS = ("yh", "z")
CHIPS = ("yl", "x")
CENT = ("yl", "x", "core")
FEATURE_SCALE = math.sqrt(2.0 * (2.0 / FEAT) * math.log2(math.e))
SWAP = [(0, 1), (1, 0)]


def pieces(value, count):
    out = []
    for _ in range(count):
        top = lax.reduce_precision(value, 8, 7)
        out.append(top.astype(BF16))
        value = value - top
    return out


def half_norm(high, mid):
    value = high.astype(F32) + mid.astype(F32)
    return pieces(-0.5 * jnp.sum(value * value, axis=1, keepdims=True), 3)


def row_operand(high, mid):
    n = high.shape[0]
    ones = jnp.ones((n, 3), BF16)
    return jnp.concatenate([high, high, mid, *half_norm(high, mid), ones, jnp.zeros((n, 58), BF16)], axis=1)


def centre_operand(high, mid):
    n = high.shape[0]
    ones = jnp.ones((n, 3), BF16)
    return jnp.concatenate([high, mid, high, ones, *half_norm(high, mid), jnp.zeros((n, 58), BF16)], axis=1)


def params(**more):
    return pltpu.CompilerParams(vmem_limit_bytes=48 * 1024 * 1024, **more)


def tile_kernel(rows_ref, cen_ref, coef_ref, tile_ref, fit_ref):
    power = lax.dot_general(rows_ref[...], cen_ref[...], (((1,), (1,)), ((), ())), preferred_element_type=F32)
    tile = jnp.exp2(power).astype(BF16)
    tile_ref[...] = tile
    fit_ref[...] = jnp.dot(tile, coef_ref[...], preferred_element_type=F32).astype(BF16)


def tile_forward(rows_op, cen_op, coef, block=512):
    n, m = rows_op.shape[0], cen_op.shape[0]
    return pl.pallas_call(
        tile_kernel,
        grid=(n // block,),
        in_specs=[
            pl.BlockSpec((block, 256), lambda i: (i, 0)),
            pl.BlockSpec((m, 256), lambda i: (0, 0)),
            pl.BlockSpec((m, OUTS), lambda i: (0, 0)),
        ],
        out_specs=[pl.BlockSpec((block, m), lambda i: (i, 0)), pl.BlockSpec((block, OUTS), lambda i: (i, 0))],
        out_shape=[jax.ShapeDtypeStruct((n, m), BF16), jax.ShapeDtypeStruct((n, OUTS), BF16)],
        compiler_params=params(),
        name="tile_forward",
    )(rows_op, cen_op, coef)


def back_kernel(tile_ref, fit_ref, grad_ref, total_ref):
    step = pl.program_id(0)

    @pl.when(step == 0)
    def _():
        total_ref[...] = jnp.zeros_like(total_ref)

    total_ref[...] += jnp.dot(fit_ref[...].T, tile_ref[...], preferred_element_type=F32)

    @pl.when(step == pl.num_programs(0) - 1)
    def _():
        grad_ref[...] = total_ref[...].T.astype(BF16)


def backward(tile, fitted, block=512):
    n, m = tile.shape
    return pl.pallas_call(
        back_kernel,
        grid=(n // block,),
        in_specs=[pl.BlockSpec((block, m), lambda i: (i, 0)), pl.BlockSpec((block, OUTS), lambda i: (i, 0))],
        out_specs=pl.BlockSpec((m, OUTS), lambda i: (0, 0)),
        out_shape=jax.ShapeDtypeStruct((m, OUTS), BF16),
        scratch_shapes=[pltpu.VMEM((OUTS, m), F32)],
        compiler_params=params(),
        name="tile_backward",
    )(tile, fitted)


def field_kernel(pre_ref, dir_ref, out_ref):
    out_ref[...] = jnp.dot(pre_ref[...], dir_ref[...], preferred_element_type=F32).astype(BF16)


def field(precond, dir_all, block=256):
    n, m = precond.shape
    return pl.pallas_call(
        field_kernel,
        grid=(n // block,),
        in_specs=[pl.BlockSpec((block, m), lambda i: (i, 0)), pl.BlockSpec((m, OUTS), lambda i: (0, 0))],
        out_specs=pl.BlockSpec((block, OUTS), lambda i: (i, 0)),
        out_shape=jax.ShapeDtypeStruct((n, OUTS), BF16),
        compiler_params=params(),
        name="precond_forward",
    )(precond, dir_all)


def image_kernel(pre_ref, grad_ref, out_ref):
    part = jnp.dot(grad_ref[...].T, pre_ref[...], preferred_element_type=F32)
    out_ref[...] = part.T.astype(BF16)


def image_part(precond, grad, block=512):
    n, m = precond.shape
    return pl.pallas_call(
        image_kernel,
        grid=(m // block,),
        in_specs=[pl.BlockSpec((n, block), lambda i: (0, i)), pl.BlockSpec((n, OUTS), lambda i: (0, 0))],
        out_specs=pl.BlockSpec((block, OUTS), lambda i: (i, 0)),
        out_shape=jax.ShapeDtypeStruct((m, OUTS), BF16),
        compiler_params=params(),
        name="precond_backward",
    )(precond, grad)


def spread(part, axes):
    return lax.all_to_all(part, axes, 0, 0, tiled=True)


def gathered(part, axes):
    count = math.prod(lax.axis_size(axis) for axis in axes)
    return spread(jnp.broadcast_to(part[None], (count, *part.shape)), axes)


def summed(parts):
    return jnp.sum(parts.astype(F32), axis=0)


def core_halves(part, axis):
    me = lax.axis_index("core")
    mine = lax.dynamic_index_in_dim(part, me, axis, keepdims=False)
    other = lax.dynamic_index_in_dim(part, 1 - me, axis, keepdims=False)
    came = lax.ppermute(other, "core", SWAP)
    return mine.astype(F32) + came.astype(F32)


def core_both(part):
    first = lax.axis_index("core") == 0
    came = lax.ppermute(part, "core", SWAP)
    return jnp.stack([jnp.where(first, part, came), jnp.where(first, came, part)])


def on_device(train_rows, centre_index, precond, coefficients, residual, direction):
    rows_here = train_rows.shape[0]
    cen_here = centre_index.shape[0]
    row_devices = lax.axis_size("yh") * lax.axis_size("z")
    cen_devices = lax.axis_size("yl") * lax.axis_size("x") * lax.axis_size("core")
    start_row = lax.axis_index(ROWS) * rows_here

    offset = centre_index - start_row
    inside = (offset >= 0) & (offset < rows_here)
    picked = train_rows[jnp.clip(offset, 0, rows_here - 1)]
    picked = jnp.where(inside[:, None], picked, 0.0)
    both = jnp.concatenate(pieces(picked * FEATURE_SCALE, 2), axis=1)
    mine = summed(spread(both.reshape(row_devices, cen_here // row_devices, 2 * FEAT), ROWS)).astype(BF16)

    dir_all = gathered(direction.astype(BF16), CENT).reshape(-1, OUTS)
    part = field(precond, dir_all).reshape(row_devices, cen_here // row_devices, OUTS)
    load = jnp.concatenate([part, jnp.broadcast_to(mine[None], (row_devices, *mine.shape))], axis=1)
    got = spread(load, ROWS)
    share = cen_here // row_devices
    features = got[:, share:].reshape(cen_here, 2 * FEAT)
    coef_mine = summed(got[:, :share]).astype(BF16)
    coef_field = gathered(coef_mine, ROWS).reshape(cen_here, OUTS)

    rows_op = row_operand(*pieces(train_rows * FEATURE_SCALE, 2))
    cen_op = centre_operand(features[:, :FEAT], features[:, FEAT:])
    tile, fit_part = tile_forward(rows_op, cen_op, coef_field)

    share = rows_here // cen_devices
    half = core_halves(fit_part.reshape(2, cen_devices // 2, share, OUTS), 0).astype(BF16)
    fit_mine = summed(spread(half, CHIPS)).astype(BF16)
    fitted = core_both(gathered(fit_mine, CHIPS)).reshape(rows_here, OUTS)

    grad_part = backward(tile, fitted).reshape(row_devices, cen_here // row_devices, OUTS)
    grad_mine = summed(spread(grad_part, ROWS)) * float(rows_here * row_devices) ** (-0.5)
    grad_low = gathered(grad_mine.astype(BF16), ROWS).reshape(cen_here, OUTS)

    part = image_part(precond, grad_low)
    half = core_halves(part.reshape(cen_devices // 2, 2, direction.shape[0], OUTS), 1).astype(BF16)
    image = summed(spread(half, CHIPS)) + ridge_weight * direction

    top = jnp.max(jnp.abs(image))
    top = jnp.where(top > 0, top, 1.0)
    scaled = image / top
    numbers = [jnp.sum(residual * residual), jnp.sum(direction * image), jnp.sum(residual * scaled), jnp.sum(scaled * scaled), top]
    lane = lax.broadcasted_iota(jnp.int32, (8, 128), 0)
    packed = jnp.zeros((8, 128), F32)
    for place, number in enumerate(numbers):
        packed = jnp.where(lane == place, number, packed)

    def combine(parts):
        tops = parts[:, 4:5]
        most = jnp.max(tops, axis=0, keepdims=True)
        ratio = tops / most
        plain = jnp.sum(parts[:, 0:2], axis=0)
        cross = jnp.sum(parts[:, 2:3] * ratio, axis=0)
        square = jnp.sum(parts[:, 3:4] * ratio * ratio, axis=0)
        return jnp.concatenate([plain, cross, square, most[0], jnp.zeros((3, 128), F32)], axis=0)

    packed = combine(gathered(packed, CENT))
    packed = combine(gathered(packed, ROWS))
    norm_old, curvature, cross, square, most = (packed[place, 0] for place in range(5))
    step_size = norm_old / curvature
    reach = step_size * most
    norm_new = norm_old - 2.0 * reach * cross + reach * reach * square
    coef_next = coefficients + step_size * direction
    residual_next = residual - step_size * image
    direction_next = residual_next + norm_new / norm_old * direction
    return (coef_next, residual_next, direction_next)


def solution(mesh):
    fine = Mesh(np.asarray(mesh.devices).reshape([size for _, size in FINE]), [name for name, _ in FINE])
    every = P((*ROWS, *CENT), None)
    return jax.shard_map(
        on_device,
        mesh=fine,
        in_specs=(P(ROWS, None), P(CENT), P(CENT, ROWS), every, every, every),
        out_specs=(every, every, every),
        check_vma=False,
    )
```

```python
import math

import jax
import jax.numpy as jnp
import numpy as np
from jax import lax
from jax.experimental import pallas as pl
from jax.experimental.pallas import tpu as pltpu
from jax.sharding import Mesh
from jax.sharding import PartitionSpec as P

FEAT = 64
OUTS = 128
ridge_weight = 0.1
F32, BF16 = jnp.float32, jnp.bfloat16

FINE = (("yh", 2), ("z", 4), ("yl", 2), ("x", 4), ("core", 2))
ROWS = ("yh", "z")
CHIPS = ("yl", "x")
CENT = ("yl", "x", "core")
FEATURE_SCALE = math.sqrt(2.0 * (2.0 / FEAT) * math.log2(math.e))
SWAP = [(0, 1), (1, 0)]


def params(limit=48):
    return pltpu.CompilerParams(vmem_limit_bytes=limit * 1024 * 1024)


def cost(flops, nbytes, exps=0):
    return pl.CostEstimate(flops=flops, bytes_accessed=nbytes, transcendentals=exps)


def split_pieces(value, count):
    out = []
    for _ in range(count):
        top = value.astype(BF16)
        out.append(top)
        value = value - top.astype(F32)
    return out


def operand(high, mid, row_side):
    n = high.shape[1]
    value = high.astype(F32) + mid.astype(F32)
    norm = -0.5 * jnp.sum(value * value, axis=0, keepdims=True)
    line = lax.broadcasted_iota(jnp.int32, (FEAT, n), 0)
    tail = jnp.zeros((FEAT, n), F32)
    first_norm, first_one = (0, 3) if row_side else (3, 0)
    for place, piece in enumerate(split_pieces(norm, 3)):
        tail = jnp.where(line == first_norm + place, piece.astype(F32), tail)
    tail = jnp.where((line >= first_one) & (line < first_one + 3), 1.0, tail).astype(BF16)
    middle = (high, mid) if row_side else (mid, high)
    return jnp.concatenate([high, *middle, tail], axis=0)


def pick_kernel(start_ref, index_ref, feat_ref, out_ref, total_ref):
    step = pl.program_id(0)
    block = feat_ref.shape[1]

    @pl.when(step == 0)
    def _():
        total_ref[...] = jnp.zeros_like(total_ref)

    table = jnp.concatenate(split_pieces(feat_ref[...] * FEATURE_SCALE, 2), axis=0)
    wanted = index_ref[...] - (start_ref[0] + step * block)
    place = lax.broadcasted_iota(jnp.int32, (block, wanted.shape[1]), 0)
    choice = jnp.where(place == wanted, 1.0, 0.0).astype(BF16)
    total_ref[...] += jnp.dot(table, choice, preferred_element_type=F32)

    @pl.when(step == pl.num_programs(0) - 1)
    def _():
        for j in range(out_ref.shape[0]):
            width = out_ref.shape[2]
            out_ref[j] = total_ref[:, j * width : (j + 1) * width].astype(BF16)


def pick(start, index, feat, parts, block=512):
    depth, n = feat.shape
    m = index.shape[1]
    return pl.pallas_call(
        pick_kernel,
        grid=(n // block,),
        in_specs=[
            pl.BlockSpec(memory_space=pltpu.SMEM),
            pl.BlockSpec((1, m), lambda i: (0, 0)),
            pl.BlockSpec((depth, block), lambda i: (0, i)),
        ],
        out_specs=pl.BlockSpec((parts, 2 * depth, m // parts), lambda i: (0, 0, 0)),
        out_shape=jax.ShapeDtypeStruct((parts, 2 * depth, m // parts), BF16),
        scratch_shapes=[pltpu.VMEM((2 * depth, m), F32)],
        compiler_params=params(),
        cost_estimate=cost(2 * n * m * 128 * 4, n * depth * 4),
        name="pick_centres",
    )(start, index, feat)


def prepare_kernel(feat_ref, out_ref):
    high, mid = split_pieces(feat_ref[...] * FEATURE_SCALE, 2)
    out_ref[...] = operand(high, mid, True).T


def prepare_rows(feat, block=1024):
    depth, n = feat.shape
    return pl.pallas_call(
        prepare_kernel,
        grid=(n // block,),
        in_specs=[pl.BlockSpec((depth, block), lambda i: (0, i))],
        out_specs=pl.BlockSpec((block, 256), lambda i: (i, 0)),
        out_shape=jax.ShapeDtypeStruct((n, 256), BF16),
        compiler_params=params(),
        cost_estimate=cost(n * 2**20 // 2, n * 1024),
        name="prepare_rows",
    )(feat)


def tile_kernel(rows_ref, got_ref, tile_ref, cen_ref):
    @pl.when(pl.program_id(0) == 0)
    def _():
        width = got_ref.shape[2]
        for j in range(got_ref.shape[0]):
            both = got_ref[j, got_ref.shape[1] - 2 * FEAT :]
            cen_ref[:, j * width : (j + 1) * width] = operand(both[:FEAT], both[FEAT:], False)

    power = jnp.dot(rows_ref[...], cen_ref[...], preferred_element_type=F32)
    tile_ref[...] = jnp.exp2(power).astype(BF16)


def make_tile(rows_op, got, block=512):
    n = rows_op.shape[0]
    m = got.shape[0] * got.shape[2]
    return pl.pallas_call(
        tile_kernel,
        grid=(n // block,),
        in_specs=[pl.BlockSpec((block, 256), lambda i: (i, 0)), pl.BlockSpec(got.shape, lambda i: (0, 0, 0))],
        out_specs=pl.BlockSpec((block, m), lambda i: (i, 0)),
        out_shape=jax.ShapeDtypeStruct((n, m), BF16),
        scratch_shapes=[pltpu.VMEM((256, m), BF16)],
        compiler_params=params(),
        cost_estimate=cost(2 * n * m * 256, 2 * n * m, n * m),
        name="kernel_tile",
    )(rows_op, got)


def forward_kernel(tile_ref, coef_ref, fit_ref):
    fit_ref[...] = jnp.dot(tile_ref[...], coef_ref[...], preferred_element_type=F32)


def forward(tile, coef, block=512):
    n, m = tile.shape
    return pl.pallas_call(
        forward_kernel,
        grid=(n // block,),
        in_specs=[pl.BlockSpec((block, m), lambda i: (i, 0)), pl.BlockSpec((m, OUTS), lambda i: (0, 0))],
        out_specs=pl.BlockSpec((block, OUTS), lambda i: (i, 0)),
        out_shape=jax.ShapeDtypeStruct((n, OUTS), F32),
        compiler_params=params(),
        cost_estimate=cost(2 * n * m * OUTS, 2 * n * m),
        name="tile_forward",
    )(tile, coef)


def back_kernel(tile_ref, fit_ref, grad_ref, total_ref):
    step = pl.program_id(0)

    @pl.when(step == 0)
    def _():
        total_ref[...] = jnp.zeros_like(total_ref)

    total_ref[...] += jnp.dot(fit_ref[...].T, tile_ref[...], preferred_element_type=F32)

    @pl.when(step == pl.num_programs(0) - 1)
    def _():
        grad_ref[...] = total_ref[...].T.astype(BF16)


def backward(tile, fitted, block=512):
    n, m = tile.shape
    return pl.pallas_call(
        back_kernel,
        grid=(n // block,),
        in_specs=[pl.BlockSpec((block, m), lambda i: (i, 0)), pl.BlockSpec((block, OUTS), lambda i: (i, 0))],
        out_specs=pl.BlockSpec((m, OUTS), lambda i: (0, 0)),
        out_shape=jax.ShapeDtypeStruct((m, OUTS), BF16),
        scratch_shapes=[pltpu.VMEM((OUTS, m), F32)],
        compiler_params=params(),
        cost_estimate=cost(2 * n * m * OUTS, 2 * n * m),
        name="tile_backward",
    )(tile, fitted)


def field_kernel(pre_ref, dir_ref, feat_ref, out_ref):
    width = out_ref.shape[1] - 2 * FEAT
    part = jnp.dot(pre_ref[...], dir_ref[...], preferred_element_type=F32).astype(BF16)
    features = jnp.sum(feat_ref[...].astype(F32), axis=0).astype(BF16)
    for j in range(out_ref.shape[0]):
        out_ref[j, :width] = part[j * width : (j + 1) * width]
        out_ref[j, width:] = features


def field(precond, dir_all, feat_parts, block=256):
    n, m = precond.shape
    parts = feat_parts.shape[0]
    share = n // parts
    return pl.pallas_call(
        field_kernel,
        grid=(n // block,),
        in_specs=[
            pl.BlockSpec((block, m), lambda i: (i, 0)),
            pl.BlockSpec((m, OUTS), lambda i: (0, 0)),
            pl.BlockSpec(feat_parts.shape, lambda i: (0, 0, 0)),
        ],
        out_specs=pl.BlockSpec((block // share, share + 2 * FEAT, OUTS), lambda i: (i, 0, 0)),
        out_shape=jax.ShapeDtypeStruct((parts, share + 2 * FEAT, OUTS), BF16),
        compiler_params=params(60),
        cost_estimate=cost(2 * n * m * OUTS, 2 * n * m),
        name="precond_forward",
    )(precond, dir_all, feat_parts)


def image_kernel(pre_ref, grad_ref, out_ref):
    part = jnp.dot(grad_ref[...].T, pre_ref[...], preferred_element_type=F32).T
    chips, width = out_ref.shape[1:3]
    for chip in range(chips):
        for core in range(2):
            first = (chip * 2 + core) * width
            out_ref[core, chip] = part[first : first + width]


def image_part(precond, grad, share, block=512):
    n, m = precond.shape
    return pl.pallas_call(
        image_kernel,
        grid=(m // block,),
        in_specs=[pl.BlockSpec((n, block), lambda i: (0, i)), pl.BlockSpec((n, OUTS), lambda i: (0, 0))],
        out_specs=pl.BlockSpec((2, block // share // 2, share, OUTS), lambda i: (0, i, 0, 0)),
        out_shape=jax.ShapeDtypeStruct((2, m // share // 2, share, OUTS), F32),
        compiler_params=params(),
        cost_estimate=cost(2 * n * m * OUTS, 2 * n * m),
        name="precond_backward",
    )(precond, grad)


def numbers_kernel(part_ref, dir_ref, res_ref, image_ref, out_ref):
    direction, residual = dir_ref[...], res_ref[...]
    image = jnp.sum(part_ref[...].astype(F32), axis=0) + ridge_weight * direction
    image_ref[...] = image
    top = jnp.max(jnp.max(jnp.abs(image), axis=0, keepdims=True), axis=1, keepdims=True)
    top = jnp.where(top > 0, top, 1.0)
    scaled = image / top

    def total(value):
        return jnp.sum(jnp.sum(value, axis=0, keepdims=True), axis=1, keepdims=True)

    numbers = [total(residual * residual), total(direction * image), total(residual * scaled), total(scaled * scaled), top]
    lane = lax.broadcasted_iota(jnp.int32, (1, 128), 1)
    packed = jnp.zeros((1, 128), F32)
    for place, number in enumerate(numbers):
        packed = jnp.where(lane == place, number, packed)
    out_ref[...] = jnp.broadcast_to(packed, out_ref.shape)


def numbers(parts, direction, residual, devices):
    shape = jax.ShapeDtypeStruct(direction.shape, F32)
    return pl.pallas_call(
        numbers_kernel,
        out_shape=[shape, jax.ShapeDtypeStruct((devices, 128), F32)],
        compiler_params=params(),
        name="image_numbers",
    )(parts, direction, residual)


def finish_kernel(all_ref, image_ref, coef_ref, res_ref, dir_ref, coef_out, res_out, dir_out):
    every = all_ref[...]
    lane = lax.broadcasted_iota(jnp.int32, every.shape, 1)

    def column(place):
        return jnp.sum(jnp.where(lane == place, every, 0.0), axis=1, keepdims=True)

    tops = column(4)
    most = jnp.max(tops, axis=0, keepdims=True)
    ratio = tops / most
    norm_old = jnp.sum(column(0), axis=0, keepdims=True)
    curvature = jnp.sum(column(1), axis=0, keepdims=True)
    cross = jnp.sum(column(2) * ratio, axis=0, keepdims=True)
    square = jnp.sum(column(3) * ratio * ratio, axis=0, keepdims=True)
    step_size = norm_old / curvature
    reach = step_size * most
    norm_new = norm_old - 2.0 * reach * cross + reach * reach * square
    direction = dir_ref[...]
    coef_out[...] = coef_ref[...] + step_size * direction
    residual_next = res_ref[...] - step_size * image_ref[...]
    res_out[...] = residual_next
    dir_out[...] = residual_next + norm_new / norm_old * direction


def finish(every, image, coefficients, residual, direction):
    shape = jax.ShapeDtypeStruct(direction.shape, F32)
    return pl.pallas_call(
        finish_kernel,
        out_shape=[shape, shape, shape],
        compiler_params=params(),
        name="finish",
    )(every, image, coefficients, residual, direction)


def spread(part, axes):
    return lax.all_to_all(part, axes, 0, 0, tiled=True)


def gathered(part, axes):
    count = math.prod(lax.axis_size(axis) for axis in axes)
    return spread(jnp.broadcast_to(part[None], (count, *part.shape)), axes)


def summed(parts):
    return jnp.sum(parts.astype(F32), axis=0)


def core_halves(part, send):
    me = lax.axis_index("core")
    mine = lax.dynamic_index_in_dim(part, me, 0, keepdims=False)
    other = lax.dynamic_index_in_dim(part, 1 - me, 0, keepdims=False)
    came = lax.ppermute(other.astype(send), "core", SWAP)
    return (mine + came.astype(F32)).astype(BF16)


def core_both(part):
    first = lax.axis_index("core") == 0
    came = lax.ppermute(part, "core", SWAP)
    return jnp.stack([jnp.where(first, part, came), jnp.where(first, came, part)])


def on_device(train_rows, centre_index, precond, coefficients, residual, direction):
    rows_here = train_rows.shape[0]
    cen_here = centre_index.shape[0]
    row_devices = lax.axis_size("yh") * lax.axis_size("z")
    cen_devices = lax.axis_size("yl") * lax.axis_size("x") * lax.axis_size("core")
    start_row = (lax.axis_index(ROWS) * rows_here).astype(jnp.int32)
    share = cen_here // row_devices

    dir_all = gathered(direction.astype(BF16), CENT).reshape(-1, OUTS)

    feat = train_rows.T
    feat_parts = spread(pick(start_row[None], centre_index[None], feat, row_devices), ROWS)
    rows_op = prepare_rows(feat)

    got = spread(field(precond, dir_all, feat_parts), ROWS)
    coef_mine = summed(got[:, :share]).astype(BF16)
    coef_field = gathered(coef_mine, ROWS).reshape(cen_here, OUTS)
    tile = make_tile(rows_op, got)
    fit_part = forward(tile, coef_field)

    half = core_halves(fit_part.reshape(2, cen_devices // 2, rows_here // cen_devices, OUTS), BF16)
    fit_mine = summed(spread(half, CHIPS)).astype(BF16)
    fitted = core_both(gathered(fit_mine, CHIPS)).reshape(rows_here, OUTS)

    grad_part = backward(tile, fitted).reshape(row_devices, share, OUTS)
    grad_mine = summed(spread(grad_part, ROWS)) * float(rows_here * row_devices) ** (-0.5)
    grad_low = gathered(grad_mine.astype(BF16), ROWS).reshape(cen_here, OUTS)

    half = core_halves(image_part(precond, grad_low, direction.shape[0]), F32)
    image, row = numbers(spread(half, CHIPS), direction, residual, row_devices * cen_devices)
    every = spread(row, (*ROWS, *CENT))
    return tuple(finish(every, image, coefficients, residual, direction))


def solution(mesh):
    fine = Mesh(np.asarray(mesh.devices).reshape([size for _, size in FINE]), [name for name, _ in FINE])
    every = P((*ROWS, *CENT), None)
    return jax.shard_map(
        on_device,
        mesh=fine,
        in_specs=(P(ROWS, None), P(CENT), P(CENT, ROWS), every, every, every),
        out_specs=(every, every, every),
        check_vma=False,
    )
```

```python
import math

import jax
import jax.numpy as jnp
import numpy as np
from jax import lax
from jax.experimental import pallas as pl
from jax.experimental.pallas import tpu as pltpu
from jax.sharding import Mesh
from jax.sharding import PartitionSpec as P

FEAT = 64
OUTS = 128
ridge_weight = 0.1
F32, BF16 = jnp.float32, jnp.bfloat16

FINE = (("yh", 2), ("z", 4), ("yl", 2), ("x", 4), ("core", 2))
ROWS = ("yh", "z")
CHIPS = ("yl", "x")
CENT = ("yl", "x", "core")
FEATURE_SCALE = math.sqrt(2.0 * (2.0 / FEAT) * math.log2(math.e))
SWAP = [(0, 1), (1, 0)]


def params(limit=16):
    return pltpu.CompilerParams(vmem_limit_bytes=limit * 1024 * 1024)


def cost(flops, nbytes, exps=0):
    return pl.CostEstimate(flops=flops, bytes_accessed=nbytes, transcendentals=exps)


def split_pieces(value, count):
    out = []
    for _ in range(count):
        top = value.astype(BF16)
        out.append(top)
        value = value - top.astype(F32)
    return out


def operand(high, mid, row_side):
    n = high.shape[1]
    value = high.astype(F32) + mid.astype(F32)
    norm = -0.5 * jnp.sum(value * value, axis=0, keepdims=True)
    line = lax.broadcasted_iota(jnp.int32, (FEAT, n), 0)
    tail = jnp.zeros((FEAT, n), F32)
    first_norm, first_one = (0, 3) if row_side else (3, 0)
    for place, piece in enumerate(split_pieces(norm, 3)):
        tail = jnp.where(line == first_norm + place, piece.astype(F32), tail)
    tail = jnp.where((line >= first_one) & (line < first_one + 3), 1.0, tail).astype(BF16)
    middle = (high, mid) if row_side else (mid, high)
    return jnp.concatenate([high, *middle, tail], axis=0)


def pick_kernel(start_ref, index_ref, feat_ref, out_ref, total_ref):
    step = pl.program_id(0)
    block = feat_ref.shape[1]

    @pl.when(step == 0)
    def _():
        total_ref[...] = jnp.zeros_like(total_ref)

    table = jnp.concatenate(split_pieces(feat_ref[...] * FEATURE_SCALE, 2), axis=0)
    wanted = index_ref[...] - (start_ref[0] + step * block)
    place = lax.broadcasted_iota(jnp.int32, (block, wanted.shape[1]), 0)
    choice = jnp.where(place == wanted, 1.0, 0.0).astype(BF16)
    total_ref[...] += jnp.dot(table, choice, preferred_element_type=F32)

    @pl.when(step == pl.num_programs(0) - 1)
    def _():
        for j in range(out_ref.shape[0]):
            width = out_ref.shape[2]
            out_ref[j] = total_ref[:, j * width : (j + 1) * width].astype(BF16)


def pick(start, index, feat, parts, block=512):
    depth, n = feat.shape
    m = index.shape[1]
    return pl.pallas_call(
        pick_kernel,
        grid=(n // block,),
        in_specs=[
            pl.BlockSpec(memory_space=pltpu.SMEM),
            pl.BlockSpec((1, m), lambda i: (0, 0)),
            pl.BlockSpec((depth, block), lambda i: (0, i)),
        ],
        out_specs=pl.BlockSpec((parts, 2 * depth, m // parts), lambda i: (0, 0, 0)),
        out_shape=jax.ShapeDtypeStruct((parts, 2 * depth, m // parts), BF16),
        scratch_shapes=[pltpu.VMEM((2 * depth, m), F32)],
        compiler_params=params(),
        cost_estimate=cost(2 * n * m * 128 * 4, n * depth * 4),
        name="pick_centres",
    )(start, index, feat)


def prepare_kernel(feat_ref, out_ref):
    high, mid = split_pieces(feat_ref[...] * FEATURE_SCALE, 2)
    out_ref[...] = operand(high, mid, True).T


def prepare_rows(feat, block=1024):
    depth, n = feat.shape
    return pl.pallas_call(
        prepare_kernel,
        grid=(n // block,),
        in_specs=[pl.BlockSpec((depth, block), lambda i: (0, i))],
        out_specs=pl.BlockSpec((block, 256), lambda i: (i, 0)),
        out_shape=jax.ShapeDtypeStruct((n, 256), BF16),
        compiler_params=params(60),
        cost_estimate=cost(n * 2**20 // 2, n * 1024),
        name="prepare_rows",
    )(feat)


VMEM = pl.BlockSpec(memory_space=pltpu.VMEM)
SMEM = pl.BlockSpec(memory_space=pltpu.SMEM)
HBM = pl.BlockSpec(memory_space=pltpu.HBM)


def tile_kernel(rows_ref, got_ref, tile_ref, fit_ref, cen_ref, coef_ref):
    @pl.when(pl.program_id(0) == 0)
    def _():
        parts, depth, width = got_ref.shape
        share = depth - 2 * FEAT
        for j in range(parts):
            both = got_ref[j, share:]
            cen_ref[:, j * width : (j + 1) * width] = operand(both[:FEAT], both[FEAT:], False)
            coef_ref[j * share : (j + 1) * share] = got_ref[j, :share]

    power = jnp.dot(rows_ref[...], cen_ref[...], preferred_element_type=F32)
    tile = jnp.exp2(power).astype(BF16)
    tile_ref[...] = tile
    fit_ref[...] = jnp.dot(tile, coef_ref[...], preferred_element_type=F32)


def tile_forward(rows_op, got, block=512):
    n = rows_op.shape[0]
    parts, depth, width = got.shape
    m = parts * width
    return pl.pallas_call(
        tile_kernel,
        grid=(n // block,),
        in_specs=[pl.BlockSpec((block, 256), lambda i: (i, 0)), pl.BlockSpec(got.shape, lambda i: (0, 0, 0))],
        out_specs=[pl.BlockSpec((block, m), lambda i: (i, 0)), pl.BlockSpec((block, OUTS), lambda i: (i, 0))],
        out_shape=[jax.ShapeDtypeStruct((n, m), BF16), jax.ShapeDtypeStruct((n, OUTS), F32)],
        scratch_shapes=[pltpu.VMEM((256, m), BF16), pltpu.VMEM((parts * (depth - 2 * FEAT), OUTS), BF16)],
        compiler_params=params(56),
        cost_estimate=cost(2 * n * m * 384, 2 * n * m, n * m),
        name="tile_forward",
    )(rows_op, got)


def back_kernel(me_ref, tile_ref, mine_ref, came_ref, grad_ref, tile_here, fit_ref, total_ref, sems):
    blocks = sems.shape[0]
    block = tile_ref.shape[0] // blocks
    copies = [
        pltpu.make_async_copy(tile_ref.at[pl.ds(j * block, block)], tile_here.at[pl.ds(j * block, block)], sems.at[j])
        for j in range(blocks)
    ]
    for copy in copies:
        copy.start()
    me = me_ref[0]
    parts, share, _ = mine_ref.shape
    half = parts * share
    for j in range(parts):
        fit_ref[:, pl.ds(pl.multiple_of(me * half + j * share, share), share)] = mine_ref[j].T
        fit_ref[:, pl.ds(pl.multiple_of((1 - me) * half + j * share, share), share)] = came_ref[j].T
    for j in range(blocks):
        copies[j].wait()
        here = slice(j * block, (j + 1) * block)
        part = jnp.dot(fit_ref[:, here], tile_here[here], preferred_element_type=F32)
        if j == 0:
            total_ref[...] = part
        else:
            total_ref[...] += part
    grad_ref[...] = total_ref[...].T.astype(BF16)


def backward(me, tile, mine, came, blocks=8):
    n, m = tile.shape
    return pl.pallas_call(
        back_kernel,
        in_specs=[SMEM, HBM, VMEM, VMEM],
        out_specs=VMEM,
        out_shape=jax.ShapeDtypeStruct((m, OUTS), BF16),
        scratch_shapes=[
            pltpu.VMEM((n, m), BF16),
            pltpu.VMEM((OUTS, n), BF16),
            pltpu.VMEM((OUTS, m), F32),
            pltpu.SemaphoreType.DMA((blocks,)),
        ],
        compiler_params=params(53),
        cost_estimate=cost(2 * n * m * OUTS, 2 * n * m),
        name="tile_backward",
    )(me, tile, mine, came)


def field_kernel(me_ref, pre_ref, mine_ref, came_ref, feat_ref, out_ref, pre_here, dir_here, sems):
    parts = out_ref.shape[0]
    width = out_ref.shape[1] - 2 * FEAT
    copies = [
        pltpu.make_async_copy(pre_ref.at[pl.ds(j * width, width)], pre_here.at[pl.ds(j * width, width)], sems.at[j])
        for j in range(parts)
    ]
    for copy in copies:
        copy.start()
    me = me_ref[0]
    chips, share, _ = mine_ref.shape
    for j in range(chips):
        dir_here[pl.ds(pl.multiple_of((2 * j + me) * share, share), share)] = mine_ref[j]
        dir_here[pl.ds(pl.multiple_of((2 * j + 1 - me) * share, share), share)] = came_ref[j]
    for j in range(parts):
        out_ref[j, width:] = feat_ref[j]
    for j in range(parts):
        copies[j].wait()
        part = jnp.dot(pre_here[j * width : (j + 1) * width], dir_here[...], preferred_element_type=F32)
        out_ref[j, :width] = part.astype(BF16)


def field(me, precond, mine, came, feat_parts):
    n, m = precond.shape
    parts = feat_parts.shape[0]
    return pl.pallas_call(
        field_kernel,
        in_specs=[SMEM, HBM, VMEM, VMEM, VMEM],
        out_specs=VMEM,
        out_shape=jax.ShapeDtypeStruct((parts, n // parts + 2 * FEAT, OUTS), BF16),
        scratch_shapes=[pltpu.VMEM((n, m), BF16), pltpu.VMEM((m, OUTS), BF16), pltpu.SemaphoreType.DMA((parts,))],
        compiler_params=params(57),
        cost_estimate=cost(2 * n * m * OUTS, 2 * n * m),
        name="precond_forward",
    )(me, precond, mine, came, feat_parts)


def image_kernel(pre_ref, grad_ref, out_ref):
    part = jnp.dot(grad_ref[...].T, pre_ref[...], preferred_element_type=F32).T
    chips, width = out_ref.shape[1:3]
    for chip in range(chips):
        for core in range(2):
            first = (chip * 2 + core) * width
            out_ref[core, chip] = part[first : first + width]


def image_part(precond, grad, share, block=512):
    n, m = precond.shape
    return pl.pallas_call(
        image_kernel,
        grid=(m // block,),
        in_specs=[pl.BlockSpec((n, block), lambda i: (0, i)), pl.BlockSpec((n, OUTS), lambda i: (0, 0))],
        out_specs=pl.BlockSpec((2, block // share // 2, share, OUTS), lambda i: (0, i, 0, 0)),
        out_shape=jax.ShapeDtypeStruct((2, m // share // 2, share, OUTS), F32),
        compiler_params=params(),
        cost_estimate=cost(2 * n * m * OUTS, 2 * n * m),
        name="precond_backward",
    )(precond, grad)


def numbers_kernel(part_ref, dir_ref, res_ref, image_ref, out_ref):
    direction, residual = dir_ref[...], res_ref[...]
    image = jnp.sum(part_ref[...].astype(F32), axis=0) + ridge_weight * direction
    image_ref[...] = image
    top = jnp.max(jnp.max(jnp.abs(image), axis=0, keepdims=True), axis=1, keepdims=True)
    top = jnp.where(top > 0, top, 1.0)
    scaled = image / top

    def total(value):
        return jnp.sum(jnp.sum(value, axis=0, keepdims=True), axis=1, keepdims=True)

    numbers = [total(residual * residual), total(direction * image), total(residual * scaled), total(scaled * scaled), top]
    lane = lax.broadcasted_iota(jnp.int32, (1, 128), 1)
    packed = jnp.zeros((1, 128), F32)
    for place, number in enumerate(numbers):
        packed = jnp.where(lane == place, number, packed)
    out_ref[...] = jnp.broadcast_to(packed, out_ref.shape)


def numbers(parts, direction, residual, devices):
    shape = jax.ShapeDtypeStruct(direction.shape, F32)
    return pl.pallas_call(
        numbers_kernel,
        out_shape=[shape, jax.ShapeDtypeStruct((devices, 128), F32)],
        compiler_params=params(),
        name="image_numbers",
    )(parts, direction, residual)


def finish_kernel(all_ref, image_ref, coef_ref, res_ref, dir_ref, coef_out, res_out, dir_out):
    every = all_ref[...]
    lane = lax.broadcasted_iota(jnp.int32, every.shape, 1)

    def column(place):
        return jnp.sum(jnp.where(lane == place, every, 0.0), axis=1, keepdims=True)

    tops = column(4)
    most = jnp.max(tops, axis=0, keepdims=True)
    ratio = tops / most
    norm_old = jnp.sum(column(0), axis=0, keepdims=True)
    curvature = jnp.sum(column(1), axis=0, keepdims=True)
    cross = jnp.sum(column(2) * ratio, axis=0, keepdims=True)
    square = jnp.sum(column(3) * ratio * ratio, axis=0, keepdims=True)
    step_size = norm_old / curvature
    reach = step_size * most
    norm_new = norm_old - 2.0 * reach * cross + reach * reach * square
    direction = dir_ref[...]
    coef_out[...] = coef_ref[...] + step_size * direction
    residual_next = res_ref[...] - step_size * image_ref[...]
    res_out[...] = residual_next
    dir_out[...] = residual_next + norm_new / norm_old * direction


def finish(every, image, coefficients, residual, direction):
    shape = jax.ShapeDtypeStruct(direction.shape, F32)
    return pl.pallas_call(
        finish_kernel,
        out_shape=[shape, shape, shape],
        compiler_params=params(),
        name="finish",
    )(every, image, coefficients, residual, direction)


def spread(part, axes):
    return lax.all_to_all(part, axes, 0, 0, tiled=True)


def gathered(part, axes):
    count = math.prod(lax.axis_size(axis) for axis in axes)
    return spread(jnp.broadcast_to(part[None], (count, *part.shape)), axes)


def summed(parts):
    return jnp.sum(parts.astype(F32), axis=0)


def core_halves(part, send):
    me = lax.axis_index("core")
    mine = lax.dynamic_index_in_dim(part, me, 0, keepdims=False)
    other = lax.dynamic_index_in_dim(part, 1 - me, 0, keepdims=False)
    came = lax.ppermute(other.astype(send), "core", SWAP)
    return (mine + came.astype(F32)).astype(BF16)


def on_device(train_rows, centre_index, precond, coefficients, residual, direction):
    rows_here = train_rows.shape[0]
    cen_here = centre_index.shape[0]
    row_devices = lax.axis_size("yh") * lax.axis_size("z")
    cen_devices = lax.axis_size("yl") * lax.axis_size("x") * lax.axis_size("core")
    me = lax.axis_index("core").astype(jnp.int32)[None]
    start_row = (lax.axis_index(ROWS) * rows_here).astype(jnp.int32)
    share = cen_here // row_devices

    dir_mine = gathered(direction.astype(BF16), CHIPS)
    feat = train_rows.T
    picked = pick(start_row[None], centre_index[None], feat, row_devices)
    dir_mine, picked = lax.optimization_barrier((dir_mine, picked))
    dir_came = lax.ppermute(dir_mine, "core", SWAP)
    rows_op = prepare_rows(feat)
    parts = spread(field(me, precond, dir_mine, dir_came, picked), ROWS)
    got = gathered(summed(parts).astype(BF16), ROWS)
    tile, fit_part = tile_forward(rows_op, got)

    half = core_halves(fit_part.reshape(2, cen_devices // 2, rows_here // cen_devices, OUTS), BF16)
    fit_mine = gathered(summed(spread(half, CHIPS)).astype(BF16), CHIPS)
    fit_came = lax.ppermute(fit_mine, "core", SWAP)

    grad_part = backward(me, tile, fit_mine, fit_came).reshape(row_devices, share, OUTS)
    grad_mine = summed(spread(grad_part, ROWS)) * float(rows_here * row_devices) ** (-0.5)
    grad_low = gathered(grad_mine.astype(BF16), ROWS).reshape(cen_here, OUTS)

    half = core_halves(image_part(precond, grad_low, direction.shape[0]), F32)
    image, row = numbers(spread(half, CHIPS), direction, residual, row_devices * cen_devices)
    every = spread(row, (*ROWS, *CENT))
    return tuple(finish(every, image, coefficients, residual, direction))


def solution(mesh):
    fine = Mesh(np.asarray(mesh.devices).reshape([size for _, size in FINE]), [name for name, _ in FINE])
    every = P((*ROWS, *CENT), None)
    return jax.shard_map(
        on_device,
        mesh=fine,
        in_specs=(P(ROWS, None), P(CENT), P(CENT, ROWS), every, every, every),
        out_specs=(every, every, every),
        check_vma=False,
    )
```

```python
import functools
import math

import jax
import jax.numpy as jnp
import numpy as np
from jax import lax
from jax.experimental import pallas as pl
from jax.experimental.pallas import tpu as pltpu
from jax.sharding import Mesh
from jax.sharding import PartitionSpec as P

FEAT = 64
OUTS = 128
ridge_weight = 0.1
F32, BF16 = jnp.float32, jnp.bfloat16

FINE = (("yh", 2), ("z", 4), ("yl", 2), ("x", 4), ("core", 2))
ROWS = ("yh", "z")
CHIPS = ("yl", "x")
CENT = ("yl", "x", "core")
FEATURE_SCALE = math.sqrt(2.0 * (2.0 / FEAT) * math.log2(math.e))
SWAP = [(0, 1), (1, 0)]


def params(limit=16):
    return pltpu.CompilerParams(vmem_limit_bytes=limit * 1024 * 1024)


def cost(flops, nbytes, exps=0):
    return pl.CostEstimate(flops=flops, bytes_accessed=nbytes, transcendentals=exps)


def in_hbm(value):
    return pltpu.with_memory_space_constraint(value, pltpu.HBM)


def split_pieces(value, count):
    out = []
    for _ in range(count):
        top = value.astype(BF16)
        out.append(top)
        value = value - top.astype(F32)
    return out


def operand(high, mid, row_side):
    n = high.shape[1]
    value = high.astype(F32) + mid.astype(F32)
    norm = -0.5 * jnp.sum(value * value, axis=0, keepdims=True)
    line = lax.broadcasted_iota(jnp.int32, (FEAT, n), 0)
    tail = jnp.zeros((FEAT, n), F32)
    first_norm, first_one = (0, 3) if row_side else (3, 0)
    for place, piece in enumerate(split_pieces(norm, 3)):
        tail = jnp.where(line == first_norm + place, piece.astype(F32), tail)
    tail = jnp.where((line >= first_one) & (line < first_one + 3), 1.0, tail).astype(BF16)
    middle = (high, mid) if row_side else (mid, high)
    return jnp.concatenate([high, *middle, tail], axis=0)


def pick_kernel(start_ref, index_ref, feat_ref, out_ref, total_ref):
    step = pl.program_id(0)
    block = feat_ref.shape[1]

    @pl.when(step == 0)
    def _():
        total_ref[...] = jnp.zeros_like(total_ref)

    table = jnp.concatenate(split_pieces(feat_ref[...] * FEATURE_SCALE, 2), axis=0)
    wanted = index_ref[...] - (start_ref[0] + step * block)
    place = lax.broadcasted_iota(jnp.int32, (block, wanted.shape[1]), 0)
    choice = jnp.where(place == wanted, 1.0, 0.0).astype(BF16)
    total_ref[...] += jnp.dot(table, choice, preferred_element_type=F32)

    @pl.when(step == pl.num_programs(0) - 1)
    def _():
        for j in range(out_ref.shape[0]):
            width = out_ref.shape[2]
            out_ref[j] = total_ref[:, j * width : (j + 1) * width].astype(BF16)


def pick(start, index, feat, parts, block=512):
    depth, n = feat.shape
    m = index.shape[1]
    return pl.pallas_call(
        pick_kernel,
        grid=(n // block,),
        in_specs=[
            pl.BlockSpec(memory_space=pltpu.SMEM),
            pl.BlockSpec((1, m), lambda i: (0, 0)),
            pl.BlockSpec((depth, block), lambda i: (0, i)),
        ],
        out_specs=pl.BlockSpec((parts, 2 * depth, m // parts), lambda i: (0, 0, 0)),
        out_shape=jax.ShapeDtypeStruct((parts, 2 * depth, m // parts), BF16),
        scratch_shapes=[pltpu.VMEM((2 * depth, m), F32)],
        compiler_params=params(),
        cost_estimate=cost(2 * n * m * 128 * 4, n * depth * 4),
        name="pick_centres",
    )(start, index, feat)


def prepare_kernel(me_ref, feat_ref, out_ref):
    high, mid = split_pieces(feat_ref[...] * FEATURE_SCALE, 2)
    out_ref[...] = operand(high, mid, True).T


def prepare_rows(me, feat, block=1024):
    depth, n = feat.shape
    blocks = n // block
    half = blocks // 2
    return pl.pallas_call(
        prepare_kernel,
        grid_spec=pltpu.PrefetchScalarGridSpec(
            num_scalar_prefetch=1,
            grid=(blocks,),
            in_specs=[pl.BlockSpec((depth, block), lambda i, me: (0, (i + half * (1 - me[0])) % blocks))],
            out_specs=pl.BlockSpec((block, 256), lambda i, me: (i, 0)),
        ),
        out_shape=pltpu.HBM((n, 256), BF16),
        compiler_params=params(),
        cost_estimate=cost(n * 2**20 // 2, n * 1024),
        name="prepare_rows",
    )(me, feat)


def send_kernel(dir_ref, out_ref):
    out_ref[...] = jnp.broadcast_to(dir_ref[...].astype(BF16)[None], out_ref.shape)


def copies_of(direction, count):
    return pl.pallas_call(
        send_kernel,
        out_shape=jax.ShapeDtypeStruct((count, *direction.shape), BF16),
        compiler_params=params(),
        name="direction_copies",
    )(direction)


VMEM = pl.BlockSpec(memory_space=pltpu.VMEM)
SMEM = pl.BlockSpec(memory_space=pltpu.SMEM)
HBM = pl.BlockSpec(memory_space=pltpu.HBM)


def centre_kernel(got_ref, cen_ref, coef_ref):
    parts, depth, width = got_ref.shape
    share = depth - 2 * FEAT
    for j in range(parts):
        both = got_ref[j, share:]
        cen_ref[:, j * width : (j + 1) * width] = operand(both[:FEAT], both[FEAT:], False)
        coef_ref[j * share : (j + 1) * share] = got_ref[j, :share]


def prepare_centres(got):
    parts, depth, width = got.shape
    return pl.pallas_call(
        centre_kernel,
        out_shape=[
            jax.ShapeDtypeStruct((256, parts * width), BF16),
            jax.ShapeDtypeStruct((parts * (depth - 2 * FEAT), OUTS), BF16),
        ],
        compiler_params=params(),
        name="prepare_centres",
    )(got)


def tile_kernel(rows_ref, cen_ref, coef_ref, tile_ref, fit_ref):
    power = jnp.dot(rows_ref[...], cen_ref[...], preferred_element_type=F32)
    tile = jnp.exp2(power).astype(BF16)
    tile_ref[...] = tile
    fit_ref[...] = jnp.dot(tile, coef_ref[...], preferred_element_type=F32).astype(fit_ref.dtype)


def tile_forward(rows_op, half, cen_op, coef, fit_type, block=512):
    n = rows_op.shape[0] // 2
    m = cen_op.shape[1]
    first = half * (n // block)
    return pl.pallas_call(
        tile_kernel,
        grid=(n // block,),
        in_specs=[
            pl.BlockSpec((block, 256), lambda i: (first + i, 0)),
            pl.BlockSpec(cen_op.shape, lambda i: (0, 0)),
            pl.BlockSpec(coef.shape, lambda i: (0, 0)),
        ],
        out_specs=[pl.BlockSpec((block, m), lambda i: (i, 0)), pl.BlockSpec((block, OUTS), lambda i: (i, 0))],
        out_shape=[pltpu.HBM((n, m), BF16), jax.ShapeDtypeStruct((n, OUTS), fit_type)],
        compiler_params=params(),
        cost_estimate=cost(2 * n * m * 384, 2 * n * m, n * m),
        name="tile_forward",
    )(in_hbm(rows_op), cen_op, coef)


def back_kernel(*refs, last):
    tile_ref, fit_ref, *before, out_ref, tile_here, turned, total_ref, sems = refs
    blocks = sems.shape[0]
    block = tile_ref.shape[0] // blocks
    copies = [
        pltpu.make_async_copy(tile_ref.at[pl.ds(j * block, block)], tile_here.at[pl.ds(j * block, block)], sems.at[j])
        for j in range(blocks)
    ]
    for copy in copies:
        copy.start()
    parts, share, _ = fit_ref.shape
    for j in range(parts):
        turned[:, j * share : (j + 1) * share] = fit_ref[j].T
    for j in range(blocks):
        copies[j].wait()
        here = slice(j * block, (j + 1) * block)
        part = jnp.dot(turned[:, here], tile_here[here], preferred_element_type=F32)
        if j or before:
            part += total_ref[...] if j else before[0][...]
        if j < blocks - 1:
            total_ref[...] = part
        elif last:
            out_ref[...] = part.T.astype(BF16)
        else:
            out_ref[...] = part


def backward(tile, fitted, before=None, blocks=4):
    n, m = tile.shape
    last = before is not None
    return pl.pallas_call(
        functools.partial(back_kernel, last=last),
        in_specs=[HBM, VMEM] + [VMEM] * last,
        out_specs=VMEM,
        out_shape=jax.ShapeDtypeStruct((m, OUTS), BF16) if last else jax.ShapeDtypeStruct((OUTS, m), F32),
        scratch_shapes=[
            pltpu.VMEM((n, m), BF16),
            pltpu.VMEM((OUTS, n), BF16),
            pltpu.VMEM((OUTS, m), F32),
            pltpu.SemaphoreType.DMA((blocks,)),
        ],
        compiler_params=params(),
        cost_estimate=cost(2 * n * m * OUTS, 2 * n * m),
        name="tile_backward",
    )(in_hbm(tile), fitted, *([before] if last else []))


def field_kernel(me_ref, pre_ref, mine_ref, came_ref, feat_ref, out_ref, pre_here, dir_here, sems):
    parts = out_ref.shape[0]
    width = out_ref.shape[1] - 2 * FEAT
    blocks = sems.shape[0]
    block = pre_ref.shape[0] // blocks
    copies = [
        pltpu.make_async_copy(pre_ref.at[pl.ds(j * block, block)], pre_here.at[pl.ds(j * block, block)], sems.at[j])
        for j in range(blocks)
    ]
    for copy in copies:
        copy.start()
    me = me_ref[0]
    chips, share, _ = mine_ref.shape
    for j in range(chips):
        dir_here[pl.ds(pl.multiple_of((2 * j + me) * share, share), share)] = mine_ref[j]
        dir_here[pl.ds(pl.multiple_of((2 * j + 1 - me) * share, share), share)] = came_ref[j]
    for j in range(parts):
        out_ref[j, width:] = feat_ref[j]
    for j in range(blocks):
        copies[j].wait()
        part = jnp.dot(pre_here[j * block : (j + 1) * block], dir_here[...], preferred_element_type=F32).astype(BF16)
        for k in range(block // width):
            out_ref[j * (block // width) + k, :width] = part[k * width : (k + 1) * width]


def field(me, precond, mine, came, feat_parts, blocks=4):
    n, m = precond.shape
    parts = feat_parts.shape[0]
    return pl.pallas_call(
        field_kernel,
        in_specs=[SMEM, HBM, VMEM, VMEM, VMEM],
        out_specs=VMEM,
        out_shape=jax.ShapeDtypeStruct((parts, n // parts + 2 * FEAT, OUTS), BF16),
        scratch_shapes=[pltpu.VMEM((n, m), BF16), pltpu.VMEM((m, OUTS), BF16), pltpu.SemaphoreType.DMA((blocks,))],
        compiler_params=params(),
        cost_estimate=cost(2 * n * m * OUTS, 2 * n * m),
        name="precond_forward",
    )(me, in_hbm(precond), mine, came, feat_parts)


def image_kernel(core_ref, pre_ref, grad_ref, out_ref, pre_here, sems):
    core = core_ref[0]
    chips, width, _ = out_ref.shape
    copies = [
        pltpu.make_async_copy(
            pre_ref.at[:, pl.ds(pl.multiple_of((2 * j + core) * width, width), width)],
            pre_here.at[j // 2, :, pl.ds(j % 2 * width, width)],
            sems.at[j],
        )
        for j in range(chips)
    ]
    for copy in copies:
        copy.start()
    grad = grad_ref[...].T
    for j in range(0, chips, 2):
        copies[j].wait()
        copies[j + 1].wait()
        part = jnp.dot(grad, pre_here[j // 2], preferred_element_type=F32).T
        out_ref[j] = part[:width]
        out_ref[j + 1] = part[width:]


def image_part(core, precond, grad, share):
    n, m = precond.shape
    chips = m // share // 2
    return pl.pallas_call(
        image_kernel,
        in_specs=[SMEM, HBM, VMEM],
        out_specs=VMEM,
        out_shape=jax.ShapeDtypeStruct((chips, share, OUTS), F32),
        scratch_shapes=[pltpu.VMEM((chips // 2, n, 2 * share), BF16), pltpu.SemaphoreType.DMA((chips,))],
        compiler_params=params(),
        cost_estimate=cost(n * m * OUTS, n * m),
        name="precond_backward",
    )(core, in_hbm(precond), grad)


def numbers_kernel(part_ref, dir_ref, res_ref, image_ref, out_ref):
    direction, residual = dir_ref[...], res_ref[...]
    image = jnp.sum(part_ref[...].astype(F32), axis=0) + ridge_weight * direction
    image_ref[...] = image
    top = jnp.max(jnp.max(jnp.abs(image), axis=0, keepdims=True), axis=1, keepdims=True)
    top = jnp.where(top > 0, top, 1.0)
    scaled = image / top

    def total(value):
        return jnp.sum(jnp.sum(value, axis=0, keepdims=True), axis=1, keepdims=True)

    numbers = [total(residual * residual), total(direction * image), total(residual * scaled), total(scaled * scaled), top]
    lane = lax.broadcasted_iota(jnp.int32, (1, 128), 1)
    packed = jnp.zeros((1, 128), F32)
    for place, number in enumerate(numbers):
        packed = jnp.where(lane == place, number, packed)
    out_ref[...] = jnp.broadcast_to(packed, out_ref.shape)


def numbers(parts, direction, residual, devices):
    shape = jax.ShapeDtypeStruct(direction.shape, F32)
    return pl.pallas_call(
        numbers_kernel,
        out_shape=[shape, jax.ShapeDtypeStruct((devices, 128), F32)],
        compiler_params=params(),
        name="image_numbers",
    )(parts, direction, residual)


def finish_kernel(all_ref, image_ref, coef_ref, res_ref, dir_ref, coef_out, res_out, dir_out):
    every = all_ref[...]
    lane = lax.broadcasted_iota(jnp.int32, every.shape, 1)

    def column(place):
        return jnp.sum(jnp.where(lane == place, every, 0.0), axis=1, keepdims=True)

    tops = column(4)
    most = jnp.max(tops, axis=0, keepdims=True)
    ratio = tops / most
    norm_old = jnp.sum(column(0), axis=0, keepdims=True)
    curvature = jnp.sum(column(1), axis=0, keepdims=True)
    cross = jnp.sum(column(2) * ratio, axis=0, keepdims=True)
    square = jnp.sum(column(3) * ratio * ratio, axis=0, keepdims=True)
    step_size = norm_old / curvature
    reach = step_size * most
    norm_new = norm_old - 2.0 * reach * cross + reach * reach * square
    direction = dir_ref[...]
    coef_out[...] = coef_ref[...] + step_size * direction
    residual_next = res_ref[...] - step_size * image_ref[...]
    res_out[...] = residual_next
    dir_out[...] = residual_next + norm_new / norm_old * direction


def finish(every, image, coefficients, residual, direction):
    shape = jax.ShapeDtypeStruct(direction.shape, F32)
    return pl.pallas_call(
        finish_kernel,
        out_shape=[shape, shape, shape],
        compiler_params=params(),
        name="finish",
    )(every, image, coefficients, residual, direction)


def spread(part, axes):
    return lax.all_to_all(part, axes, 0, 0, tiled=True)


def gathered(part, axes):
    count = math.prod(lax.axis_size(axis) for axis in axes)
    return spread(jnp.broadcast_to(part[None], (count, *part.shape)), axes)


def summed(parts):
    return jnp.sum(parts.astype(F32), axis=0)


def swapped(part):
    return lax.ppermute(part, "core", SWAP)


def on_device(train_rows, centre_index, precond, coefficients, residual, direction):
    rows_here = train_rows.shape[0]
    cen_here = centre_index.shape[0]
    row_devices = lax.axis_size("yh") * lax.axis_size("z")
    cen_devices = lax.axis_size("yl") * lax.axis_size("x") * lax.axis_size("core")
    me = lax.axis_index("core").astype(jnp.int32)[None]
    start_row = (lax.axis_index(ROWS) * rows_here).astype(jnp.int32)
    share = cen_here // row_devices

    other = 1 - me
    dir_mine = spread(copies_of(direction, cen_devices // 2), CHIPS)

    feat = train_rows.T
    picked = pick(start_row[None], centre_index[None], feat, row_devices)
    dir_mine, picked = lax.optimization_barrier((dir_mine, picked))
    rows_op = prepare_rows(me, feat)
    parts = spread(field(me, precond, dir_mine, swapped(dir_mine), picked), ROWS)
    got = gathered(summed(parts).astype(BF16), ROWS)
    cen_op, coef = prepare_centres(got)

    chips_shape = (cen_devices // 2, rows_here // cen_devices, OUTS)
    tile_other, fit_other = tile_forward(rows_op, 0, cen_op, coef, BF16)
    fit_came = swapped(fit_other)
    tile_mine, fit_mine = tile_forward(rows_op, 1, cen_op, coef, F32)
    fit_mine, fit_came = lax.optimization_barrier((fit_mine, fit_came))
    half = (fit_mine + fit_came.astype(F32)).astype(BF16).reshape(chips_shape)
    fitted = gathered(summed(spread(half, CHIPS)).astype(BF16), CHIPS)
    fitted_came = swapped(fitted)
    grad_mine = backward(tile_mine, fitted)
    grad_mine, fitted_came = lax.optimization_barrier((grad_mine, fitted_came))
    grad_part = backward(tile_other, fitted_came, grad_mine).reshape(row_devices, share, OUTS)

    grad_sum = summed(spread(grad_part, ROWS)) * float(rows_here * row_devices) ** (-0.5)
    grad_low = gathered(grad_sum.astype(BF16), ROWS).reshape(cen_here, OUTS)

    image_came = swapped(image_part(other, precond, grad_low, direction.shape[0]))
    image_mine = image_part(me, precond, grad_low, direction.shape[0])
    image_mine, image_came = lax.optimization_barrier((image_mine, image_came))
    half = (image_mine + image_came).astype(BF16)
    image, row = numbers(spread(half, CHIPS), direction, residual, row_devices * cen_devices)
    every = spread(row, (*ROWS, *CENT))
    return tuple(finish(every, image, coefficients, residual, direction))


def solution(mesh):
    fine = Mesh(np.asarray(mesh.devices).reshape([size for _, size in FINE]), [name for name, _ in FINE])
    every = P((*ROWS, *CENT), None)
    return jax.shard_map(
        on_device,
        mesh=fine,
        in_specs=(P(ROWS, None), P(CENT), P(CENT, ROWS), every, every, every),
        out_specs=(every, every, every),
        check_vma=False,
    )
```

```python
import functools
import math

import jax
import jax.numpy as jnp
import numpy as np
from jax import lax
from jax.experimental import pallas as pl
from jax.experimental.pallas import tpu as pltpu
from jax.sharding import Mesh
from jax.sharding import PartitionSpec as P

FEAT = 64
OUTS = 128
ridge_weight = 0.1
F32, BF16 = jnp.float32, jnp.bfloat16

FINE = (("yh", 2), ("z", 4), ("yl", 2), ("x", 4), ("core", 2))
ROWS = ("yh", "z")
CHIPS = ("yl", "x")
CENT = ("yl", "x", "core")
FEATURE_SCALE = math.sqrt(2.0 * (2.0 / FEAT) * math.log2(math.e))
SWAP = [(0, 1), (1, 0)]


def params(limit=16):
    return pltpu.CompilerParams(vmem_limit_bytes=limit * 1024 * 1024)


def cost(flops, nbytes, exps=0):
    return pl.CostEstimate(flops=flops, bytes_accessed=nbytes, transcendentals=exps)


def in_hbm(value):
    return pltpu.with_memory_space_constraint(value, pltpu.HBM)


def split_pieces(value, count):
    out = []
    for _ in range(count):
        top = value.astype(BF16)
        out.append(top)
        value = value - top.astype(F32)
    return out


def operand(high, mid, row_side):
    n = high.shape[1]
    value = high.astype(F32) + mid.astype(F32)
    norm = -0.5 * jnp.sum(value * value, axis=0, keepdims=True)
    line = lax.broadcasted_iota(jnp.int32, (FEAT, n), 0)
    tail = jnp.zeros((FEAT, n), F32)
    first_norm, first_one = (0, 3) if row_side else (3, 0)
    for place, piece in enumerate(split_pieces(norm, 3)):
        tail = jnp.where(line == first_norm + place, piece.astype(F32), tail)
    tail = jnp.where((line >= first_one) & (line < first_one + 3), 1.0, tail).astype(BF16)
    middle = (high, mid) if row_side else (mid, high)
    return jnp.concatenate([high, *middle, tail], axis=0)


def pick_kernel(start_ref, index_ref, feat_ref, out_ref, total_ref):
    step = pl.program_id(0)
    block = feat_ref.shape[1]

    @pl.when(step == 0)
    def _():
        total_ref[...] = jnp.zeros_like(total_ref)

    table = jnp.concatenate(split_pieces(feat_ref[...] * FEATURE_SCALE, 2), axis=0)
    wanted = index_ref[...] - (start_ref[0] + step * block)
    place = lax.broadcasted_iota(jnp.int32, (block, wanted.shape[1]), 0)
    choice = jnp.where(place == wanted, 1.0, 0.0).astype(BF16)
    total_ref[...] += jnp.dot(table, choice, preferred_element_type=F32)

    @pl.when(step == pl.num_programs(0) - 1)
    def _():
        for j in range(out_ref.shape[0]):
            width = out_ref.shape[2]
            out_ref[j] = total_ref[:, j * width : (j + 1) * width].astype(BF16)


def pick(start, index, feat, parts, block=512):
    depth, n = feat.shape
    m = index.shape[1]
    return pl.pallas_call(
        pick_kernel,
        grid=(n // block,),
        in_specs=[
            pl.BlockSpec(memory_space=pltpu.SMEM),
            pl.BlockSpec((1, m), lambda i: (0, 0)),
            pl.BlockSpec((depth, block), lambda i: (0, i)),
        ],
        out_specs=pl.BlockSpec((parts, 2 * depth, m // parts), lambda i: (0, 0, 0)),
        out_shape=jax.ShapeDtypeStruct((parts, 2 * depth, m // parts), BF16),
        scratch_shapes=[pltpu.VMEM((2 * depth, m), F32)],
        compiler_params=params(),
        cost_estimate=cost(2 * n * m * 128 * 4, n * depth * 4),
        name="pick_centres",
    )(start, index, feat)


def prepare_kernel(me_ref, feat_ref, out_ref):
    high, mid = split_pieces(feat_ref[...] * FEATURE_SCALE, 2)
    out_ref[...] = operand(high, mid, True).T


def prepare_rows(me, feat, block=1024):
    depth, n = feat.shape
    blocks = n // block
    half = blocks // 2
    return pl.pallas_call(
        prepare_kernel,
        grid_spec=pltpu.PrefetchScalarGridSpec(
            num_scalar_prefetch=1,
            grid=(blocks,),
            in_specs=[pl.BlockSpec((depth, block), lambda i, me: (0, (i + half * (1 - me[0])) % blocks))],
            out_specs=pl.BlockSpec((block, 256), lambda i, me: (i, 0)),
        ),
        out_shape=pltpu.HBM((n, 256), BF16),
        compiler_params=params(),
        cost_estimate=cost(n * 2**20 // 2, n * 1024),
        name="prepare_rows",
    )(me, feat)


def send_kernel(dir_ref, out_ref):
    out_ref[...] = jnp.broadcast_to(dir_ref[...].astype(BF16)[None], out_ref.shape)


def copies_of(direction, count):
    return pl.pallas_call(
        send_kernel,
        out_shape=jax.ShapeDtypeStruct((count, *direction.shape), BF16),
        compiler_params=params(),
        name="direction_copies",
    )(direction)


VMEM = pl.BlockSpec(memory_space=pltpu.VMEM)
SMEM = pl.BlockSpec(memory_space=pltpu.SMEM)
HBM = pl.BlockSpec(memory_space=pltpu.HBM)


def tile_kernel(*refs, first):
    if first:
        rows_ref, got_ref, tile_ref, fit_ref, cen_ref, coef_ref, rows_here, tile_here, rows_sems, sems = refs
    else:
        rows_ref, cen_ref, coef_ref, tile_ref, fit_ref, rows_here, tile_here, rows_sems, sems = refs
    blocks = sems.shape[0]
    block = fit_ref.shape[0] // blocks
    offset = 0 if first else fit_ref.shape[0]
    loads = [
        pltpu.make_async_copy(
            rows_ref.at[pl.ds(offset + j * block, block)], rows_here.at[pl.ds(j * block, block)], rows_sems.at[j]
        )
        for j in range(blocks)
    ]
    for load in loads:
        load.start()
    if first:
        parts, depth, width = got_ref.shape
        share = depth - 2 * FEAT
        for j in range(parts):
            both = got_ref[j, share:]
            cen_ref[:, j * width : (j + 1) * width] = operand(both[:FEAT], both[FEAT:], False)
            coef_ref[j * share : (j + 1) * share] = got_ref[j, :share]
    stores = []
    for j in range(blocks):
        loads[j].wait()
        here = slice(j * block, (j + 1) * block)
        power = jnp.dot(rows_here[here], cen_ref[...], preferred_element_type=F32)
        tile = jnp.exp2(power).astype(BF16)
        tile_here[here] = tile
        place = pl.ds(j * block, block)
        stores.append(pltpu.make_async_copy(tile_here.at[place], tile_ref.at[place], sems.at[j]))
        stores[-1].start()
        fit_ref[here] = jnp.dot(tile, coef_ref[...], preferred_element_type=F32).astype(fit_ref.dtype)
    for store in stores:
        store.wait()


def tile_forward(rows_op, operands, fit_type, block=256):
    n = rows_op.shape[0] // 2
    first = len(operands) == 1
    if first:
        parts, depth, width = operands[0].shape
        m = parts * width
        more = [
            jax.ShapeDtypeStruct((256, m), BF16),
            jax.ShapeDtypeStruct((parts * (depth - 2 * FEAT), OUTS), BF16),
        ]
    else:
        m = operands[0].shape[1]
        more = []
    return pl.pallas_call(
        functools.partial(tile_kernel, first=first),
        in_specs=[HBM] + [VMEM] * len(operands),
        out_specs=[HBM] + [VMEM] * (1 + len(more)),
        out_shape=[pltpu.HBM((n, m), BF16), jax.ShapeDtypeStruct((n, OUTS), fit_type), *more],
        scratch_shapes=[
            pltpu.VMEM((n, 256), BF16),
            pltpu.VMEM((n, m), BF16),
            pltpu.SemaphoreType.DMA((n // block,)),
            pltpu.SemaphoreType.DMA((n // block,)),
        ],
        compiler_params=params(),
        cost_estimate=cost(2 * n * m * 384, 2 * n * m, n * m),
        name="tile_forward",
    )(in_hbm(rows_op), *operands)


def back_kernel(*refs, last):
    tile_ref, fit_ref, *before, out_ref, tile_here, turned, total_ref, sems = refs
    blocks = sems.shape[0]
    block = tile_ref.shape[0] // blocks
    copies = [
        pltpu.make_async_copy(tile_ref.at[pl.ds(j * block, block)], tile_here.at[pl.ds(j * block, block)], sems.at[j])
        for j in range(blocks)
    ]
    for copy in copies:
        copy.start()
    parts, share, _ = fit_ref.shape
    for j in range(parts):
        turned[:, j * share : (j + 1) * share] = fit_ref[j].T
    for j in range(blocks):
        copies[j].wait()
        here = slice(j * block, (j + 1) * block)
        part = jnp.dot(turned[:, here], tile_here[here], preferred_element_type=F32)
        if j or before:
            part += total_ref[...] if j else before[0][...]
        if j < blocks - 1:
            total_ref[...] = part
        elif last:
            out_ref[...] = part.T.astype(BF16)
        else:
            out_ref[...] = part


def backward(tile, fitted, before=None, blocks=4):
    n, m = tile.shape
    last = before is not None
    return pl.pallas_call(
        functools.partial(back_kernel, last=last),
        in_specs=[HBM, VMEM] + [VMEM] * last,
        out_specs=VMEM,
        out_shape=jax.ShapeDtypeStruct((m, OUTS), BF16) if last else jax.ShapeDtypeStruct((OUTS, m), F32),
        scratch_shapes=[
            pltpu.VMEM((n, m), BF16),
            pltpu.VMEM((OUTS, n), BF16),
            pltpu.VMEM((OUTS, m), F32),
            pltpu.SemaphoreType.DMA((blocks,)),
        ],
        compiler_params=params(),
        cost_estimate=cost(2 * n * m * OUTS, 2 * n * m),
        name="tile_backward",
    )(in_hbm(tile), fitted, *([before] if last else []))


def field_kernel(me_ref, pre_ref, mine_ref, came_ref, feat_ref, out_ref, pre_here, dir_here, sems):
    parts = out_ref.shape[0]
    width = out_ref.shape[1] - 2 * FEAT
    blocks = sems.shape[0]
    block = pre_ref.shape[0] // blocks
    copies = [
        pltpu.make_async_copy(pre_ref.at[pl.ds(j * block, block)], pre_here.at[pl.ds(j * block, block)], sems.at[j])
        for j in range(blocks)
    ]
    for copy in copies:
        copy.start()
    me = me_ref[0]
    chips, share, _ = mine_ref.shape
    for j in range(chips):
        dir_here[pl.ds(pl.multiple_of((2 * j + me) * share, share), share)] = mine_ref[j]
        dir_here[pl.ds(pl.multiple_of((2 * j + 1 - me) * share, share), share)] = came_ref[j]
    for j in range(parts):
        out_ref[j, width:] = feat_ref[j]
    for j in range(blocks):
        copies[j].wait()
        part = jnp.dot(pre_here[j * block : (j + 1) * block], dir_here[...], preferred_element_type=F32).astype(BF16)
        for k in range(block // width):
            out_ref[j * (block // width) + k, :width] = part[k * width : (k + 1) * width]


def field(me, precond, mine, came, feat_parts, blocks=4):
    n, m = precond.shape
    parts = feat_parts.shape[0]
    return pl.pallas_call(
        field_kernel,
        in_specs=[SMEM, HBM, VMEM, VMEM, VMEM],
        out_specs=VMEM,
        out_shape=jax.ShapeDtypeStruct((parts, n // parts + 2 * FEAT, OUTS), BF16),
        scratch_shapes=[pltpu.VMEM((n, m), BF16), pltpu.VMEM((m, OUTS), BF16), pltpu.SemaphoreType.DMA((blocks,))],
        compiler_params=params(),
        cost_estimate=cost(2 * n * m * OUTS, 2 * n * m),
        name="precond_forward",
    )(me, in_hbm(precond), mine, came, feat_parts)


def image_kernel(core_ref, pre_ref, grad_ref, out_ref):
    core = core_ref[0]
    chips, width, _ = out_ref.shape
    grad = grad_ref[...].T
    for j in range(0, chips, 2):
        pair = [pre_ref[:, pl.ds(pl.multiple_of((2 * k + core) * width, width), width)] for k in (j, j + 1)]
        part = jnp.dot(grad, jnp.concatenate(pair, axis=1), preferred_element_type=F32).T
        out_ref[j] = part[:width]
        out_ref[j + 1] = part[width:]


def image_part(core, precond, grad, share):
    n, m = precond.shape
    return pl.pallas_call(
        image_kernel,
        in_specs=[SMEM, VMEM, VMEM],
        out_specs=VMEM,
        out_shape=jax.ShapeDtypeStruct((m // share // 2, share, OUTS), F32),
        compiler_params=params(),
        cost_estimate=cost(n * m * OUTS, n * m),
        name="precond_backward",
    )(core, precond, grad)


def numbers_kernel(part_ref, dir_ref, res_ref, image_ref, out_ref):
    direction, residual = dir_ref[...], res_ref[...]
    image = jnp.sum(part_ref[...].astype(F32), axis=0) + ridge_weight * direction
    image_ref[...] = image
    top = jnp.max(jnp.max(jnp.abs(image), axis=0, keepdims=True), axis=1, keepdims=True)
    top = jnp.where(top > 0, top, 1.0)
    scaled = image / top

    def total(value):
        return jnp.sum(jnp.sum(value, axis=0, keepdims=True), axis=1, keepdims=True)

    numbers = [total(residual * residual), total(direction * image), total(residual * scaled), total(scaled * scaled), top]
    lane = lax.broadcasted_iota(jnp.int32, (1, 128), 1)
    packed = jnp.zeros((1, 128), F32)
    for place, number in enumerate(numbers):
        packed = jnp.where(lane == place, number, packed)
    out_ref[...] = jnp.broadcast_to(packed, out_ref.shape)


def numbers(parts, direction, residual, devices):
    shape = jax.ShapeDtypeStruct(direction.shape, F32)
    return pl.pallas_call(
        numbers_kernel,
        out_shape=[shape, jax.ShapeDtypeStruct((devices, 128), F32)],
        compiler_params=params(),
        name="image_numbers",
    )(parts, direction, residual)


def finish_kernel(all_ref, image_ref, coef_ref, res_ref, dir_ref, coef_out, res_out, dir_out):
    every = all_ref[...]
    lane = lax.broadcasted_iota(jnp.int32, every.shape, 1)

    def column(place):
        return jnp.sum(jnp.where(lane == place, every, 0.0), axis=1, keepdims=True)

    tops = column(4)
    most = jnp.max(tops, axis=0, keepdims=True)
    ratio = tops / most
    norm_old = jnp.sum(column(0), axis=0, keepdims=True)
    curvature = jnp.sum(column(1), axis=0, keepdims=True)
    cross = jnp.sum(column(2) * ratio, axis=0, keepdims=True)
    square = jnp.sum(column(3) * ratio * ratio, axis=0, keepdims=True)
    step_size = norm_old / curvature
    reach = step_size * most
    norm_new = norm_old - 2.0 * reach * cross + reach * reach * square
    direction = dir_ref[...]
    coef_out[...] = coef_ref[...] + step_size * direction
    residual_next = res_ref[...] - step_size * image_ref[...]
    res_out[...] = residual_next
    dir_out[...] = residual_next + norm_new / norm_old * direction


def finish(every, image, coefficients, residual, direction):
    shape = jax.ShapeDtypeStruct(direction.shape, F32)
    return pl.pallas_call(
        finish_kernel,
        out_shape=[shape, shape, shape],
        compiler_params=params(),
        name="finish",
    )(every, image, coefficients, residual, direction)


def spread(part, axes):
    return lax.all_to_all(part, axes, 0, 0, tiled=True)


def gathered(part, axes):
    count = math.prod(lax.axis_size(axis) for axis in axes)
    return spread(jnp.broadcast_to(part[None], (count, *part.shape)), axes)


def summed(parts):
    return jnp.sum(parts.astype(F32), axis=0)


def swapped(part):
    return lax.ppermute(part, "core", SWAP)


def on_device(train_rows, centre_index, precond, coefficients, residual, direction):
    rows_here = train_rows.shape[0]
    cen_here = centre_index.shape[0]
    row_devices = lax.axis_size("yh") * lax.axis_size("z")
    cen_devices = lax.axis_size("yl") * lax.axis_size("x") * lax.axis_size("core")
    me = lax.axis_index("core").astype(jnp.int32)[None]
    start_row = (lax.axis_index(ROWS) * rows_here).astype(jnp.int32)
    share = cen_here // row_devices

    other = 1 - me
    dir_mine = spread(copies_of(direction, cen_devices // 2), CHIPS)

    feat = train_rows.T
    picked = pick(start_row[None], centre_index[None], feat, row_devices)
    dir_mine, picked, other = lax.optimization_barrier((dir_mine, picked, other))
    rows_op = prepare_rows(me, feat)
    parts = spread(field(me, precond, dir_mine, swapped(dir_mine), picked), ROWS)
    got = gathered(summed(parts).astype(BF16), ROWS)

    chips_shape = (cen_devices // 2, rows_here // cen_devices, OUTS)
    tile_other, fit_other, cen_op, coef = tile_forward(rows_op, [got], BF16)
    fit_came = swapped(fit_other)
    tile_mine, fit_mine = tile_forward(rows_op, [cen_op, coef], F32)
    fit_mine, fit_came = lax.optimization_barrier((fit_mine, fit_came))
    half = (fit_mine + fit_came.astype(F32)).astype(BF16).reshape(chips_shape)
    fitted = gathered(summed(spread(half, CHIPS)).astype(BF16), CHIPS)
    fitted_came = swapped(fitted)
    grad_mine = backward(tile_mine, fitted)
    grad_mine, fitted_came = lax.optimization_barrier((grad_mine, fitted_came))
    grad_part = backward(tile_other, fitted_came, grad_mine).reshape(row_devices, share, OUTS)

    grad_sum = summed(spread(grad_part, ROWS)) * float(rows_here * row_devices) ** (-0.5)
    grad_low = gathered(grad_sum.astype(BF16), ROWS).reshape(cen_here, OUTS)

    image_came = swapped(image_part(other, precond, grad_low, direction.shape[0]))
    image_mine = image_part(me, precond, grad_low, direction.shape[0])
    image_mine, image_came = lax.optimization_barrier((image_mine, image_came))
    half = (image_mine + image_came).astype(BF16)
    image, row = numbers(spread(half, CHIPS), direction, residual, row_devices * cen_devices)
    every = spread(row, (*ROWS, *CENT))
    return tuple(finish(every, image, coefficients, residual, direction))


def solution(mesh):
    fine = Mesh(np.asarray(mesh.devices).reshape([size for _, size in FINE]), [name for name, _ in FINE])
    every = P((*ROWS, *CENT), None)
    return jax.shard_map(
        on_device,
        mesh=fine,
        in_specs=(P(ROWS, None), P(CENT), P(CENT, ROWS), every, every, every),
        out_specs=(every, every, every),
        check_vma=False,
    )
```

```python
import functools
import math

import jax
import jax.numpy as jnp
import numpy as np
from jax import lax
from jax.experimental import pallas as pl
from jax.experimental.pallas import tpu as pltpu
from jax.sharding import Mesh
from jax.sharding import PartitionSpec as P

FEAT = 64
OUTS = 128
ridge_weight = 0.1
F32, BF16 = jnp.float32, jnp.bfloat16

FINE = (("yh", 2), ("z", 4), ("yl", 2), ("x", 4), ("core", 2))
ROWS = ("yh", "z")
CHIPS = ("yl", "x")
CENT = ("yl", "x", "core")
FEATURE_SCALE = math.sqrt(2.0 * (2.0 / FEAT) * math.log2(math.e))
SWAP = [(0, 1), (1, 0)]


def params(limit=16):
    return pltpu.CompilerParams(vmem_limit_bytes=limit * 1024 * 1024)


def cost(flops, nbytes, exps=0):
    return pl.CostEstimate(flops=flops, bytes_accessed=nbytes, transcendentals=exps)


def in_hbm(value):
    return pltpu.with_memory_space_constraint(value, pltpu.HBM)


def split_pieces(value, count):
    out = []
    for _ in range(count):
        top = value.astype(BF16)
        out.append(top)
        value = value - top.astype(F32)
    return out


def operand(high, mid, row_side):
    n = high.shape[1]
    value = high.astype(F32) + mid.astype(F32)
    norm = -0.5 * jnp.sum(value * value, axis=0, keepdims=True)
    line = lax.broadcasted_iota(jnp.int32, (FEAT, n), 0)
    tail = jnp.zeros((FEAT, n), F32)
    first_norm, first_one = (0, 3) if row_side else (3, 0)
    for place, piece in enumerate(split_pieces(norm, 3)):
        tail = jnp.where(line == first_norm + place, piece.astype(F32), tail)
    tail = jnp.where((line >= first_one) & (line < first_one + 3), 1.0, tail).astype(BF16)
    middle = (high, mid) if row_side else (mid, high)
    return jnp.concatenate([high, *middle, tail], axis=0)


def pick_kernel(start_ref, index_ref, feat_ref, out_ref, total_ref):
    step = pl.program_id(0)
    block = feat_ref.shape[1]

    @pl.when(step == 0)
    def _():
        total_ref[...] = jnp.zeros_like(total_ref)

    table = jnp.concatenate(split_pieces(feat_ref[...] * FEATURE_SCALE, 2), axis=0)
    wanted = index_ref[...] - (start_ref[0] + step * block)
    place = lax.broadcasted_iota(jnp.int32, (block, wanted.shape[1]), 0)
    choice = jnp.where(place == wanted, 1.0, 0.0).astype(BF16)
    total_ref[...] += jnp.dot(table, choice, preferred_element_type=F32)

    @pl.when(step == pl.num_programs(0) - 1)
    def _():
        for j in range(out_ref.shape[0]):
            width = out_ref.shape[2]
            out_ref[j] = total_ref[:, j * width : (j + 1) * width].astype(BF16)


def pick(start, index, feat, parts, block=512):
    depth, n = feat.shape
    m = index.shape[1]
    return pl.pallas_call(
        pick_kernel,
        grid=(n // block,),
        in_specs=[
            pl.BlockSpec(memory_space=pltpu.SMEM),
            pl.BlockSpec((1, m), lambda i: (0, 0)),
            pl.BlockSpec((depth, block), lambda i: (0, i)),
        ],
        out_specs=pl.BlockSpec((parts, 2 * depth, m // parts), lambda i: (0, 0, 0)),
        out_shape=jax.ShapeDtypeStruct((parts, 2 * depth, m // parts), BF16),
        scratch_shapes=[pltpu.VMEM((2 * depth, m), F32)],
        compiler_params=params(),
        cost_estimate=cost(2 * n * m * 128 * 4, n * depth * 4),
        name="pick_centres",
    )(start, index, feat)


def send_kernel(dir_ref, out_ref):
    out_ref[...] = jnp.broadcast_to(dir_ref[...].astype(BF16)[None], out_ref.shape)


def copies_of(direction, count):
    return pl.pallas_call(
        send_kernel,
        out_shape=jax.ShapeDtypeStruct((count, *direction.shape), BF16),
        compiler_params=params(),
        name="direction_copies",
    )(direction)


VMEM = pl.BlockSpec(memory_space=pltpu.VMEM)
SMEM = pl.BlockSpec(memory_space=pltpu.SMEM)
HBM = pl.BlockSpec(memory_space=pltpu.HBM)


def tile_kernel(*refs, first):
    if first:
        half_ref, feat_ref, got_ref, tile_ref, fit_ref, cen_ref, coef_ref, tile_here, sems = refs
        parts, depth, width = got_ref.shape
        share = depth - 2 * FEAT
        for j in range(parts):
            both = got_ref[j, share:]
            cen_ref[:, j * width : (j + 1) * width] = operand(both[:FEAT], both[FEAT:], False)
            coef_ref[j * share : (j + 1) * share] = got_ref[j, :share]
    else:
        half_ref, feat_ref, cen_ref, coef_ref, tile_ref, fit_ref, tile_here, sems = refs
    blocks = sems.shape[0]
    n = fit_ref.shape[0]
    block = n // blocks
    stores = []
    for j in range(blocks):
        here = slice(j * block, (j + 1) * block)
        place = pl.ds(pl.multiple_of(half_ref[0] * n + j * block, block), block)
        high, mid = split_pieces(feat_ref[:, place] * FEATURE_SCALE, 2)
        power = jnp.dot(operand(high, mid, True).T, cen_ref[...], preferred_element_type=F32)
        tile = jnp.exp2(power).astype(BF16)
        tile_here[here] = tile
        place = pl.ds(j * block, block)
        stores.append(pltpu.make_async_copy(tile_here.at[place], tile_ref.at[place], sems.at[j]))
        stores[-1].start()
        fit_ref[here] = jnp.dot(tile, coef_ref[...], preferred_element_type=F32).astype(fit_ref.dtype)
    for store in stores:
        store.wait()


def tile_forward(half, feat, operands, fit_type, block=256):
    n = feat.shape[1] // 2
    first = len(operands) == 1
    if first:
        parts, depth, width = operands[0].shape
        m = parts * width
        more = [
            jax.ShapeDtypeStruct((256, m), BF16),
            jax.ShapeDtypeStruct((parts * (depth - 2 * FEAT), OUTS), BF16),
        ]
    else:
        m = operands[0].shape[1]
        more = []
    return pl.pallas_call(
        functools.partial(tile_kernel, first=first),
        in_specs=[SMEM, VMEM] + [VMEM] * len(operands),
        out_specs=[HBM] + [VMEM] * (1 + len(more)),
        out_shape=[pltpu.HBM((n, m), BF16), jax.ShapeDtypeStruct((n, OUTS), fit_type), *more],
        scratch_shapes=[pltpu.VMEM((n, m), BF16), pltpu.SemaphoreType.DMA((n // block,))],
        compiler_params=params(),
        cost_estimate=cost(2 * n * m * 384, 2 * n * m, n * m),
        name="tile_forward",
    )(half, feat, *operands)


def back_kernel(*refs, last):
    tile_ref, fit_ref, *before, out_ref, tile_here, turned, total_ref, sems = refs
    blocks = sems.shape[0]
    block = tile_ref.shape[0] // blocks
    copies = [
        pltpu.make_async_copy(tile_ref.at[pl.ds(j * block, block)], tile_here.at[pl.ds(j * block, block)], sems.at[j])
        for j in range(blocks)
    ]
    for copy in copies:
        copy.start()
    parts, share, _ = fit_ref.shape
    for j in range(parts):
        turned[:, j * share : (j + 1) * share] = fit_ref[j].T
    for j in range(blocks):
        copies[j].wait()
        here = slice(j * block, (j + 1) * block)
        part = jnp.dot(turned[:, here], tile_here[here], preferred_element_type=F32)
        if j or before:
            part += total_ref[...] if j else before[0][...]
        if j < blocks - 1:
            total_ref[...] = part
        elif last:
            out_ref[...] = part.T.astype(BF16)
        else:
            out_ref[...] = part


def backward(tile, fitted, before=None, blocks=4):
    n, m = tile.shape
    last = before is not None
    return pl.pallas_call(
        functools.partial(back_kernel, last=last),
        in_specs=[HBM, VMEM] + [VMEM] * last,
        out_specs=VMEM,
        out_shape=jax.ShapeDtypeStruct((m, OUTS), BF16) if last else jax.ShapeDtypeStruct((OUTS, m), F32),
        scratch_shapes=[
            pltpu.VMEM((n, m), BF16),
            pltpu.VMEM((OUTS, n), BF16),
            pltpu.VMEM((OUTS, m), F32),
            pltpu.SemaphoreType.DMA((blocks,)),
        ],
        compiler_params=params(),
        cost_estimate=cost(2 * n * m * OUTS, 2 * n * m),
        name="tile_backward",
    )(in_hbm(tile), fitted, *([before] if last else []))


def field_kernel(me_ref, pre_ref, mine_ref, came_ref, feat_ref, out_ref, pre_here, dir_here, sems):
    parts = out_ref.shape[0]
    width = out_ref.shape[1] - 2 * FEAT
    blocks = sems.shape[0]
    block = pre_ref.shape[0] // blocks
    copies = [
        pltpu.make_async_copy(pre_ref.at[pl.ds(j * block, block)], pre_here.at[pl.ds(j * block, block)], sems.at[j])
        for j in range(blocks)
    ]
    for copy in copies:
        copy.start()
    me = me_ref[0]
    chips, share, _ = mine_ref.shape
    for j in range(chips):
        dir_here[pl.ds(pl.multiple_of((2 * j + me) * share, share), share)] = mine_ref[j]
        dir_here[pl.ds(pl.multiple_of((2 * j + 1 - me) * share, share), share)] = came_ref[j]
    for j in range(parts):
        out_ref[j, width:] = feat_ref[j]
    for j in range(blocks):
        copies[j].wait()
        part = jnp.dot(pre_here[j * block : (j + 1) * block], dir_here[...], preferred_element_type=F32).astype(BF16)
        for k in range(block // width):
            out_ref[j * (block // width) + k, :width] = part[k * width : (k + 1) * width]


def field(me, precond, mine, came, feat_parts, blocks=4):
    n, m = precond.shape
    parts = feat_parts.shape[0]
    return pl.pallas_call(
        field_kernel,
        in_specs=[SMEM, HBM, VMEM, VMEM, VMEM],
        out_specs=VMEM,
        out_shape=jax.ShapeDtypeStruct((parts, n // parts + 2 * FEAT, OUTS), BF16),
        scratch_shapes=[pltpu.VMEM((n, m), BF16), pltpu.VMEM((m, OUTS), BF16), pltpu.SemaphoreType.DMA((blocks,))],
        compiler_params=params(),
        cost_estimate=cost(2 * n * m * OUTS, 2 * n * m),
        name="precond_forward",
    )(me, in_hbm(precond), mine, came, feat_parts)


def image_kernel(core_ref, pre_ref, grad_ref, out_ref):
    core = core_ref[0]
    chips, width, _ = out_ref.shape
    grad = grad_ref[...].T
    for j in range(0, chips, 2):
        pair = [pre_ref[:, pl.ds(pl.multiple_of((2 * k + core) * width, width), width)] for k in (j, j + 1)]
        part = jnp.dot(grad, jnp.concatenate(pair, axis=1), preferred_element_type=F32).T
        out_ref[j] = part[:width]
        out_ref[j + 1] = part[width:]


def image_part(core, precond, grad, share):
    n, m = precond.shape
    return pl.pallas_call(
        image_kernel,
        in_specs=[SMEM, VMEM, VMEM],
        out_specs=VMEM,
        out_shape=jax.ShapeDtypeStruct((m // share // 2, share, OUTS), F32),
        compiler_params=params(),
        cost_estimate=cost(n * m * OUTS, n * m),
        name="precond_backward",
    )(core, precond, grad)


def numbers_kernel(part_ref, dir_ref, res_ref, image_ref, out_ref):
    direction, residual = dir_ref[...], res_ref[...]
    image = jnp.sum(part_ref[...].astype(F32), axis=0) + ridge_weight * direction
    image_ref[...] = image
    top = jnp.max(jnp.max(jnp.abs(image), axis=0, keepdims=True), axis=1, keepdims=True)
    top = jnp.where(top > 0, top, 1.0)
    scaled = image / top

    def total(value):
        return jnp.sum(jnp.sum(value, axis=0, keepdims=True), axis=1, keepdims=True)

    numbers = [total(residual * residual), total(direction * image), total(residual * scaled), total(scaled * scaled), top]
    lane = lax.broadcasted_iota(jnp.int32, (1, 128), 1)
    packed = jnp.zeros((1, 128), F32)
    for place, number in enumerate(numbers):
        packed = jnp.where(lane == place, number, packed)
    out_ref[...] = jnp.broadcast_to(packed, out_ref.shape)


def numbers(parts, direction, residual, devices):
    shape = jax.ShapeDtypeStruct(direction.shape, F32)
    return pl.pallas_call(
        numbers_kernel,
        out_shape=[shape, jax.ShapeDtypeStruct((devices, 128), F32)],
        compiler_params=params(),
        name="image_numbers",
    )(parts, direction, residual)


def finish_kernel(all_ref, image_ref, coef_ref, res_ref, dir_ref, coef_out, res_out, dir_out):
    every = all_ref[...]
    lane = lax.broadcasted_iota(jnp.int32, every.shape, 1)

    def column(place):
        return jnp.sum(jnp.where(lane == place, every, 0.0), axis=1, keepdims=True)

    tops = column(4)
    most = jnp.max(tops, axis=0, keepdims=True)
    ratio = tops / most
    norm_old = jnp.sum(column(0), axis=0, keepdims=True)
    curvature = jnp.sum(column(1), axis=0, keepdims=True)
    cross = jnp.sum(column(2) * ratio, axis=0, keepdims=True)
    square = jnp.sum(column(3) * ratio * ratio, axis=0, keepdims=True)
    step_size = norm_old / curvature
    reach = step_size * most
    norm_new = norm_old - 2.0 * reach * cross + reach * reach * square
    direction = dir_ref[...]
    coef_out[...] = coef_ref[...] + step_size * direction
    residual_next = res_ref[...] - step_size * image_ref[...]
    res_out[...] = residual_next
    dir_out[...] = residual_next + norm_new / norm_old * direction


def finish(every, image, coefficients, residual, direction):
    shape = jax.ShapeDtypeStruct(direction.shape, F32)
    return pl.pallas_call(
        finish_kernel,
        out_shape=[shape, shape, shape],
        compiler_params=params(),
        name="finish",
    )(every, image, coefficients, residual, direction)


def spread(part, axes):
    return lax.all_to_all(part, axes, 0, 0, tiled=True)


def gathered(part, axes):
    count = math.prod(lax.axis_size(axis) for axis in axes)
    return spread(jnp.broadcast_to(part[None], (count, *part.shape)), axes)


def summed(parts):
    return jnp.sum(parts.astype(F32), axis=0)


def swapped(part):
    return lax.ppermute(part, "core", SWAP)


def on_device(train_rows, centre_index, precond, coefficients, residual, direction):
    rows_here = train_rows.shape[0]
    cen_here = centre_index.shape[0]
    row_devices = lax.axis_size("yh") * lax.axis_size("z")
    cen_devices = lax.axis_size("yl") * lax.axis_size("x") * lax.axis_size("core")
    me = lax.axis_index("core").astype(jnp.int32)[None]
    start_row = (lax.axis_index(ROWS) * rows_here).astype(jnp.int32)
    share = cen_here // row_devices

    other = 1 - me
    dir_mine = spread(copies_of(direction, cen_devices // 2), CHIPS)

    feat = train_rows.T
    picked = pick(start_row[None], centre_index[None], feat, row_devices)
    dir_mine, picked, other = lax.optimization_barrier((dir_mine, picked, other))
    parts = spread(field(me, precond, dir_mine, swapped(dir_mine), picked), ROWS)
    got = gathered(summed(parts).astype(BF16), ROWS)

    chips_shape = (cen_devices // 2, rows_here // cen_devices, OUTS)
    tile_other, fit_other, cen_op, coef = tile_forward(other, feat, [got], BF16)
    fit_came = swapped(fit_other)
    tile_mine, fit_mine = tile_forward(me, feat, [cen_op, coef], F32)
    fit_mine, fit_came = lax.optimization_barrier((fit_mine, fit_came))
    half = (fit_mine + fit_came.astype(F32)).astype(BF16).reshape(chips_shape)
    fitted = gathered(summed(spread(half, CHIPS)).astype(BF16), CHIPS)
    fitted_came = swapped(fitted)
    grad_mine = backward(tile_mine, fitted)
    grad_mine, fitted_came = lax.optimization_barrier((grad_mine, fitted_came))
    grad_part = backward(tile_other, fitted_came, grad_mine).reshape(row_devices, share, OUTS)

    grad_sum = summed(spread(grad_part, ROWS)) * float(rows_here * row_devices) ** (-0.5)
    grad_low = gathered(grad_sum.astype(BF16), ROWS).reshape(cen_here, OUTS)

    image_came = swapped(image_part(other, precond, grad_low, direction.shape[0]))
    image_mine = image_part(me, precond, grad_low, direction.shape[0])
    image_mine, image_came = lax.optimization_barrier((image_mine, image_came))
    half = (image_mine + image_came).astype(BF16)
    image, row = numbers(spread(half, CHIPS), direction, residual, row_devices * cen_devices)
    every = spread(row, (*ROWS, *CENT))
    return tuple(finish(every, image, coefficients, residual, direction))


def solution(mesh):
    fine = Mesh(np.asarray(mesh.devices).reshape([size for _, size in FINE]), [name for name, _ in FINE])
    every = P((*ROWS, *CENT), None)
    return jax.shard_map(
        on_device,
        mesh=fine,
        in_specs=(P(ROWS, None), P(CENT), P(CENT, ROWS), every, every, every),
        out_specs=(every, every, every),
        check_vma=False,
    )
```

```python
import functools
import math

import jax
import jax.numpy as jnp
import numpy as np
from jax import lax
from jax.experimental import pallas as pl
from jax.experimental.pallas import tpu as pltpu
from jax.sharding import Mesh
from jax.sharding import PartitionSpec as P

FEAT = 64
OUTS = 128
ridge_weight = 0.1
F32, BF16 = jnp.float32, jnp.bfloat16

FINE = (("yh", 2), ("z", 4), ("yl", 2), ("x", 4), ("core", 2))
ROWS = ("yh", "z")
CHIPS = ("yl", "x")
CENT = ("yl", "x", "core")
FEATURE_SCALE = math.sqrt(2.0 * (2.0 / FEAT) * math.log2(math.e))
SWAP = [(0, 1), (1, 0)]


def params(limit=16):
    return pltpu.CompilerParams(vmem_limit_bytes=limit * 1024 * 1024)


def cost(flops, nbytes, exps=0):
    return pl.CostEstimate(flops=flops, bytes_accessed=nbytes, transcendentals=exps)


def in_hbm(value):
    return pltpu.with_memory_space_constraint(value, pltpu.HBM)


def split_pieces(value, count):
    out = []
    for _ in range(count):
        top = value.astype(BF16)
        out.append(top)
        value = value - top.astype(F32)
    return out


def operand(high, mid, row_side):
    n = high.shape[1]
    value = high.astype(F32) + mid.astype(F32)
    norm = -0.5 * jnp.sum(value * value, axis=0, keepdims=True)
    line = lax.broadcasted_iota(jnp.int32, (FEAT, n), 0)
    tail = jnp.zeros((FEAT, n), F32)
    first_norm, first_one = (0, 3) if row_side else (3, 0)
    for place, piece in enumerate(split_pieces(norm, 3)):
        tail = jnp.where(line == first_norm + place, piece.astype(F32), tail)
    tail = jnp.where((line >= first_one) & (line < first_one + 3), 1.0, tail).astype(BF16)
    middle = (high, mid) if row_side else (mid, high)
    return jnp.concatenate([high, *middle, tail], axis=0)


def pick_kernel(start_ref, index_ref, feat_ref, out_ref, total_ref):
    step = pl.program_id(0)
    block = feat_ref.shape[1]

    @pl.when(step == 0)
    def _():
        total_ref[...] = jnp.zeros_like(total_ref)

    table = jnp.concatenate(split_pieces(feat_ref[...] * FEATURE_SCALE, 2), axis=0)
    wanted = index_ref[...] - (start_ref[0] + step * block)
    place = lax.broadcasted_iota(jnp.int32, (block, wanted.shape[1]), 0)
    choice = jnp.where(place == wanted, 1.0, 0.0).astype(BF16)
    total_ref[...] += jnp.dot(table, choice, preferred_element_type=F32)

    @pl.when(step == pl.num_programs(0) - 1)
    def _():
        for j in range(out_ref.shape[0]):
            width = out_ref.shape[2]
            out_ref[j] = total_ref[:, j * width : (j + 1) * width].astype(BF16)


def pick(start, index, feat, parts, block=512):
    depth, n = feat.shape
    m = index.shape[1]
    return pl.pallas_call(
        pick_kernel,
        grid=(n // block,),
        in_specs=[
            pl.BlockSpec(memory_space=pltpu.SMEM),
            pl.BlockSpec((1, m), lambda i: (0, 0)),
            pl.BlockSpec((depth, block), lambda i: (0, i)),
        ],
        out_specs=pl.BlockSpec((parts, 2 * depth, m // parts), lambda i: (0, 0, 0)),
        out_shape=jax.ShapeDtypeStruct((parts, 2 * depth, m // parts), BF16),
        scratch_shapes=[pltpu.VMEM((2 * depth, m), F32)],
        compiler_params=params(),
        cost_estimate=cost(2 * n * m * 128 * 4, n * depth * 4),
        name="pick_centres",
    )(start, index, feat)


def send_kernel(dir_ref, out_ref):
    out_ref[...] = jnp.broadcast_to(dir_ref[...].astype(BF16)[None], out_ref.shape)


def copies_of(direction, count):
    return pl.pallas_call(
        send_kernel,
        out_shape=jax.ShapeDtypeStruct((count, *direction.shape), BF16),
        compiler_params=params(),
        name="direction_copies",
    )(direction)


VMEM = pl.BlockSpec(memory_space=pltpu.VMEM)
SMEM = pl.BlockSpec(memory_space=pltpu.SMEM)
HBM = pl.BlockSpec(memory_space=pltpu.HBM)


def tile_kernel(*refs, first):
    if first:
        half_ref, feat_ref, got_ref, tile_ref, fit_ref, cen_ref, coef_ref, tile_here, sems = refs
        parts, depth, width = got_ref.shape
        share = depth - 2 * FEAT
        for j in range(parts):
            both = got_ref[j, share:]
            cen_ref[:, j * width : (j + 1) * width] = operand(both[:FEAT], both[FEAT:], False)
            coef_ref[j * share : (j + 1) * share] = got_ref[j, :share]
    else:
        half_ref, feat_ref, cen_ref, coef_ref, tile_ref, fit_ref, tile_here, sems = refs
    blocks = sems.shape[0]
    n = fit_ref.shape[0]
    block = n // blocks
    stores = []
    for j in range(blocks):
        here = slice(j * block, (j + 1) * block)
        place = pl.ds(pl.multiple_of(half_ref[0] * n + j * block, block), block)
        high, mid = split_pieces(feat_ref[:, place] * FEATURE_SCALE, 2)
        power = jnp.dot(operand(high, mid, True).T, cen_ref[...], preferred_element_type=F32)
        tile = jnp.exp2(power).astype(BF16)
        tile_here[here] = tile
        place = pl.ds(j * block, block)
        stores.append(pltpu.make_async_copy(tile_here.at[place], tile_ref.at[place], sems.at[j]))
        stores[-1].start()
        fit_ref[here] = jnp.dot(tile, coef_ref[...], preferred_element_type=F32).astype(fit_ref.dtype)
    for store in stores:
        store.wait()


def tile_forward(half, feat, operands, fit_type, block=256):
    n = feat.shape[1] // 2
    first = len(operands) == 1
    if first:
        parts, depth, width = operands[0].shape
        m = parts * width
        more = [
            jax.ShapeDtypeStruct((256, m), BF16),
            jax.ShapeDtypeStruct((parts * (depth - 2 * FEAT), OUTS), BF16),
        ]
    else:
        m = operands[0].shape[1]
        more = []
    return pl.pallas_call(
        functools.partial(tile_kernel, first=first),
        in_specs=[SMEM, VMEM] + [VMEM] * len(operands),
        out_specs=[HBM] + [VMEM] * (1 + len(more)),
        out_shape=[pltpu.HBM((n, m), BF16), jax.ShapeDtypeStruct((n, OUTS), fit_type), *more],
        scratch_shapes=[pltpu.VMEM((n, m), BF16), pltpu.SemaphoreType.DMA((n // block,))],
        compiler_params=params(),
        cost_estimate=cost(2 * n * m * 384, 2 * n * m, n * m),
        name="tile_forward",
    )(half, feat, *operands)


def back_kernel(*refs, last):
    tile_ref, fit_ref, *before, out_ref, turned = refs
    parts, share, _ = fit_ref.shape
    for j in range(parts):
        turned[:, j * share : (j + 1) * share] = fit_ref[j].T
    part = jnp.dot(turned[...], tile_ref[...], preferred_element_type=F32)
    if last:
        out_ref[...] = (part + before[0][...]).T.astype(BF16)
    else:
        out_ref[...] = part


def backward(tile, fitted, before=None):
    n, m = tile.shape
    last = before is not None
    return pl.pallas_call(
        functools.partial(back_kernel, last=last),
        in_specs=[VMEM, VMEM] + [VMEM] * last,
        out_specs=VMEM,
        out_shape=jax.ShapeDtypeStruct((m, OUTS), BF16) if last else jax.ShapeDtypeStruct((OUTS, m), F32),
        scratch_shapes=[pltpu.VMEM((OUTS, n), BF16)],
        compiler_params=params(),
        cost_estimate=cost(2 * n * m * OUTS, 2 * n * m),
        name="tile_backward",
    )(tile, fitted, *([before] if last else []))


def field_kernel(me_ref, pre_ref, mine_ref, came_ref, feat_ref, out_ref, pre_here, dir_here, sems):
    parts = out_ref.shape[0]
    width = out_ref.shape[1] - 2 * FEAT
    blocks = sems.shape[0]
    block = pre_ref.shape[0] // blocks
    copies = [
        pltpu.make_async_copy(pre_ref.at[pl.ds(j * block, block)], pre_here.at[pl.ds(j * block, block)], sems.at[j])
        for j in range(blocks)
    ]
    for copy in copies:
        copy.start()
    me = me_ref[0]
    chips, share, _ = mine_ref.shape
    for j in range(chips):
        dir_here[pl.ds(pl.multiple_of((2 * j + me) * share, share), share)] = mine_ref[j]
        dir_here[pl.ds(pl.multiple_of((2 * j + 1 - me) * share, share), share)] = came_ref[j]
    for j in range(parts):
        out_ref[j, width:] = feat_ref[j]
    for j in range(blocks):
        copies[j].wait()
        part = jnp.dot(pre_here[j * block : (j + 1) * block], dir_here[...], preferred_element_type=F32).astype(BF16)
        for k in range(block // width):
            out_ref[j * (block // width) + k, :width] = part[k * width : (k + 1) * width]


def field(me, precond, mine, came, feat_parts, blocks=4):
    n, m = precond.shape
    parts = feat_parts.shape[0]
    return pl.pallas_call(
        field_kernel,
        in_specs=[SMEM, HBM, VMEM, VMEM, VMEM],
        out_specs=VMEM,
        out_shape=jax.ShapeDtypeStruct((parts, n // parts + 2 * FEAT, OUTS), BF16),
        scratch_shapes=[pltpu.VMEM((n, m), BF16), pltpu.VMEM((m, OUTS), BF16), pltpu.SemaphoreType.DMA((blocks,))],
        compiler_params=params(),
        cost_estimate=cost(2 * n * m * OUTS, 2 * n * m),
        name="precond_forward",
    )(me, in_hbm(precond), mine, came, feat_parts)


def image_kernel(core_ref, pre_ref, grad_ref, out_ref):
    core = core_ref[0]
    chips, width, _ = out_ref.shape
    grad = grad_ref[...].T
    for j in range(0, chips, 2):
        pair = [pre_ref[:, pl.ds(pl.multiple_of((2 * k + core) * width, width), width)] for k in (j, j + 1)]
        part = jnp.dot(grad, jnp.concatenate(pair, axis=1), preferred_element_type=F32).T
        out_ref[j] = part[:width]
        out_ref[j + 1] = part[width:]


def image_part(core, precond, grad, share):
    n, m = precond.shape
    return pl.pallas_call(
        image_kernel,
        in_specs=[SMEM, VMEM, VMEM],
        out_specs=VMEM,
        out_shape=jax.ShapeDtypeStruct((m // share // 2, share, OUTS), F32),
        compiler_params=params(),
        cost_estimate=cost(n * m * OUTS, n * m),
        name="precond_backward",
    )(core, precond, grad)


def numbers_kernel(part_ref, dir_ref, res_ref, image_ref, out_ref):
    direction, residual = dir_ref[...], res_ref[...]
    image = jnp.sum(part_ref[...].astype(F32), axis=0) + ridge_weight * direction
    image_ref[...] = image
    top = jnp.max(jnp.max(jnp.abs(image), axis=0, keepdims=True), axis=1, keepdims=True)
    top = jnp.where(top > 0, top, 1.0)
    scaled = image / top

    def total(value):
        return jnp.sum(jnp.sum(value, axis=0, keepdims=True), axis=1, keepdims=True)

    numbers = [total(residual * residual), total(direction * image), total(residual * scaled), total(scaled * scaled), top]
    lane = lax.broadcasted_iota(jnp.int32, (1, 128), 1)
    packed = jnp.zeros((1, 128), F32)
    for place, number in enumerate(numbers):
        packed = jnp.where(lane == place, number, packed)
    out_ref[...] = jnp.broadcast_to(packed, out_ref.shape)


def numbers(parts, direction, residual, devices):
    shape = jax.ShapeDtypeStruct(direction.shape, F32)
    return pl.pallas_call(
        numbers_kernel,
        out_shape=[shape, jax.ShapeDtypeStruct((devices, 128), F32)],
        compiler_params=params(),
        name="image_numbers",
    )(parts, direction, residual)


def finish_kernel(all_ref, image_ref, coef_ref, res_ref, dir_ref, coef_out, res_out, dir_out):
    every = all_ref[...]
    lane = lax.broadcasted_iota(jnp.int32, every.shape, 1)

    def column(place):
        return jnp.sum(jnp.where(lane == place, every, 0.0), axis=1, keepdims=True)

    tops = column(4)
    most = jnp.max(tops, axis=0, keepdims=True)
    ratio = tops / most
    norm_old = jnp.sum(column(0), axis=0, keepdims=True)
    curvature = jnp.sum(column(1), axis=0, keepdims=True)
    cross = jnp.sum(column(2) * ratio, axis=0, keepdims=True)
    square = jnp.sum(column(3) * ratio * ratio, axis=0, keepdims=True)
    step_size = norm_old / curvature
    reach = step_size * most
    norm_new = norm_old - 2.0 * reach * cross + reach * reach * square
    direction = dir_ref[...]
    coef_out[...] = coef_ref[...] + step_size * direction
    residual_next = res_ref[...] - step_size * image_ref[...]
    res_out[...] = residual_next
    dir_out[...] = residual_next + norm_new / norm_old * direction


def finish(every, image, coefficients, residual, direction):
    shape = jax.ShapeDtypeStruct(direction.shape, F32)
    return pl.pallas_call(
        finish_kernel,
        out_shape=[shape, shape, shape],
        compiler_params=params(),
        name="finish",
    )(every, image, coefficients, residual, direction)


def spread(part, axes):
    return lax.all_to_all(part, axes, 0, 0, tiled=True)


def gathered(part, axes):
    count = math.prod(lax.axis_size(axis) for axis in axes)
    return spread(jnp.broadcast_to(part[None], (count, *part.shape)), axes)


def summed(parts):
    return jnp.sum(parts.astype(F32), axis=0)


def swapped(part):
    return lax.ppermute(part, "core", SWAP)


def on_device(train_rows, centre_index, precond, coefficients, residual, direction):
    rows_here = train_rows.shape[0]
    cen_here = centre_index.shape[0]
    row_devices = lax.axis_size("yh") * lax.axis_size("z")
    cen_devices = lax.axis_size("yl") * lax.axis_size("x") * lax.axis_size("core")
    me = lax.axis_index("core").astype(jnp.int32)[None]
    start_row = (lax.axis_index(ROWS) * rows_here).astype(jnp.int32)
    share = cen_here // row_devices

    other = 1 - me
    dir_mine = spread(copies_of(direction, cen_devices // 2), CHIPS)

    feat = train_rows.T
    picked = pick(start_row[None], centre_index[None], feat, row_devices)
    dir_mine, picked, other = lax.optimization_barrier((dir_mine, picked, other))
    parts = spread(field(me, precond, dir_mine, swapped(dir_mine), picked), ROWS)
    got = gathered(summed(parts).astype(BF16), ROWS)

    chips_shape = (cen_devices // 2, rows_here // cen_devices, OUTS)
    tile_other, fit_other, cen_op, coef = tile_forward(other, feat, [got], BF16)
    fit_came = swapped(fit_other)
    tile_mine, fit_mine = tile_forward(me, feat, [cen_op, coef], F32)
    fit_mine, fit_came = lax.optimization_barrier((fit_mine, fit_came))
    half = (fit_mine + fit_came.astype(F32)).astype(BF16).reshape(chips_shape)
    fitted = gathered(summed(spread(half, CHIPS)).astype(BF16), CHIPS)
    fitted_came = swapped(fitted)
    grad_mine = backward(tile_mine, fitted)
    grad_mine, fitted_came = lax.optimization_barrier((grad_mine, fitted_came))
    grad_part = backward(tile_other, fitted_came, grad_mine).reshape(row_devices, share, OUTS)

    grad_sum = summed(spread(grad_part, ROWS)) * float(rows_here * row_devices) ** (-0.5)
    grad_low = gathered(grad_sum.astype(BF16), ROWS).reshape(cen_here, OUTS)

    image_came = swapped(image_part(other, precond, grad_low, direction.shape[0]))
    image_mine = image_part(me, precond, grad_low, direction.shape[0])
    image_mine, image_came = lax.optimization_barrier((image_mine, image_came))
    half = (image_mine + image_came).astype(BF16)
    image, row = numbers(spread(half, CHIPS), direction, residual, row_devices * cen_devices)
    every = spread(row, (*ROWS, *CENT))
    return tuple(finish(every, image, coefficients, residual, direction))


def solution(mesh):
    fine = Mesh(np.asarray(mesh.devices).reshape([size for _, size in FINE]), [name for name, _ in FINE])
    every = P((*ROWS, *CENT), None)
    return jax.shard_map(
        on_device,
        mesh=fine,
        in_specs=(P(ROWS, None), P(CENT), P(CENT, ROWS), every, every, every),
        out_specs=(every, every, every),
        check_vma=False,
    )
```

```python
import functools
import math

import jax
import jax.numpy as jnp
import numpy as np
from jax import lax
from jax.experimental import pallas as pl
from jax.experimental.pallas import tpu as pltpu
from jax.sharding import Mesh
from jax.sharding import PartitionSpec as P

FEAT = 64
OUTS = 128
ridge_weight = 0.1
F32, BF16 = jnp.float32, jnp.bfloat16

FINE = (("yh", 2), ("z", 4), ("yl", 2), ("x", 4), ("core", 2))
ROWS = ("yh", "z")
CHIPS = ("yl", "x")
CENT = ("yl", "x", "core")
FEATURE_SCALE = math.sqrt(2.0 * (2.0 / FEAT) * math.log2(math.e))
SWAP = [(0, 1), (1, 0)]


def params(limit=16):
    return pltpu.CompilerParams(vmem_limit_bytes=limit * 1024 * 1024)


def cost(flops, nbytes, exps=0):
    return pl.CostEstimate(flops=flops, bytes_accessed=nbytes, transcendentals=exps)


def in_hbm(value):
    return pltpu.with_memory_space_constraint(value, pltpu.HBM)


def split_pieces(value, count):
    out = []
    for _ in range(count):
        top = value.astype(BF16)
        out.append(top)
        value = value - top.astype(F32)
    return out


def operand(high, mid, row_side):
    n = high.shape[1]
    value = high.astype(F32) + mid.astype(F32)
    norm = -0.5 * jnp.sum(value * value, axis=0, keepdims=True)
    line = lax.broadcasted_iota(jnp.int32, (FEAT, n), 0)
    tail = jnp.zeros((FEAT, n), F32)
    first_norm, first_one = (0, 3) if row_side else (3, 0)
    for place, piece in enumerate(split_pieces(norm, 3)):
        tail = jnp.where(line == first_norm + place, piece.astype(F32), tail)
    tail = jnp.where((line >= first_one) & (line < first_one + 3), 1.0, tail).astype(BF16)
    middle = (high, mid) if row_side else (mid, high)
    return jnp.concatenate([high, *middle, tail], axis=0)


def pick_kernel(start_ref, index_ref, feat_ref, out_ref, total_ref):
    step = pl.program_id(0)
    block = feat_ref.shape[1]

    @pl.when(step == 0)
    def _():
        total_ref[...] = jnp.zeros_like(total_ref)

    table = jnp.concatenate(split_pieces(feat_ref[...] * FEATURE_SCALE, 2), axis=0)
    wanted = index_ref[...] - (start_ref[0] + step * block)
    place = lax.broadcasted_iota(jnp.int32, (block, wanted.shape[1]), 0)
    choice = jnp.where(place == wanted, 1.0, 0.0).astype(BF16)
    total_ref[...] += jnp.dot(table, choice, preferred_element_type=F32)

    @pl.when(step == pl.num_programs(0) - 1)
    def _():
        for j in range(out_ref.shape[0]):
            width = out_ref.shape[2]
            out_ref[j] = total_ref[:, j * width : (j + 1) * width].astype(BF16)


def pick(start, index, feat, parts, block=512):
    depth, n = feat.shape
    m = index.shape[1]
    return pl.pallas_call(
        pick_kernel,
        grid=(n // block,),
        in_specs=[
            pl.BlockSpec(memory_space=pltpu.SMEM),
            pl.BlockSpec((1, m), lambda i: (0, 0)),
            pl.BlockSpec((depth, block), lambda i: (0, i)),
        ],
        out_specs=pl.BlockSpec((parts, 2 * depth, m // parts), lambda i: (0, 0, 0)),
        out_shape=jax.ShapeDtypeStruct((parts, 2 * depth, m // parts), BF16),
        scratch_shapes=[pltpu.VMEM((2 * depth, m), F32)],
        compiler_params=params(),
        cost_estimate=cost(2 * n * m * 128 * 4, n * depth * 4),
        name="pick_centres",
    )(start, index, feat)


def send_kernel(dir_ref, out_ref):
    out_ref[...] = jnp.broadcast_to(dir_ref[...].astype(BF16)[None], out_ref.shape)


def copies_of(direction, count):
    return pl.pallas_call(
        send_kernel,
        out_shape=jax.ShapeDtypeStruct((count, *direction.shape), BF16),
        compiler_params=params(),
        name="direction_copies",
    )(direction)


VMEM = pl.BlockSpec(memory_space=pltpu.VMEM)
SMEM = pl.BlockSpec(memory_space=pltpu.SMEM)
HBM = pl.BlockSpec(memory_space=pltpu.HBM)


def tile_kernel(*refs, first):
    if first:
        half_ref, feat_ref, got_ref, tile_ref, fit_ref, cen_ref, coef_ref = refs
        parts, depth, width = got_ref.shape
        share = depth - 2 * FEAT
        for j in range(parts):
            both = got_ref[j, share:]
            cen_ref[:, j * width : (j + 1) * width] = operand(both[:FEAT], both[FEAT:], False)
            coef_ref[j * share : (j + 1) * share] = got_ref[j, :share]
    else:
        half_ref, feat_ref, cen_ref, coef_ref, tile_ref, fit_ref = refs
    n = fit_ref.shape[0]
    block = 256
    blocks = n // block
    for j in range(blocks):
        here = slice(j * block, (j + 1) * block)
        place = pl.ds(pl.multiple_of(half_ref[0] * n + j * block, block), block)
        high, mid = split_pieces(feat_ref[:, place] * FEATURE_SCALE, 2)
        power = jnp.dot(operand(high, mid, True).T, cen_ref[...], preferred_element_type=F32)
        tile = jnp.exp2(power).astype(BF16)
        tile_ref[here] = tile
        fit_ref[here] = jnp.dot(tile, coef_ref[...], preferred_element_type=F32).astype(fit_ref.dtype)


def tile_forward(half, feat, operands, fit_type):
    n = feat.shape[1] // 2
    first = len(operands) == 1
    if first:
        parts, depth, width = operands[0].shape
        m = parts * width
        more = [
            jax.ShapeDtypeStruct((256, m), BF16),
            jax.ShapeDtypeStruct((parts * (depth - 2 * FEAT), OUTS), BF16),
        ]
    else:
        m = operands[0].shape[1]
        more = []
    return pl.pallas_call(
        functools.partial(tile_kernel, first=first),
        in_specs=[SMEM, VMEM] + [VMEM] * len(operands),
        out_specs=[VMEM] * (2 + len(more)),
        out_shape=[jax.ShapeDtypeStruct((n, m), BF16), jax.ShapeDtypeStruct((n, OUTS), fit_type), *more],
        compiler_params=params(),
        cost_estimate=cost(2 * n * m * 384, 2 * n * m, n * m),
        name="tile_forward",
    )(half, feat, *operands)


def back_kernel(*refs, last):
    tile_ref, fit_ref, *before, out_ref, turned = refs
    parts, share, _ = fit_ref.shape
    for j in range(parts):
        turned[:, j * share : (j + 1) * share] = fit_ref[j].T
    part = jnp.dot(turned[...], tile_ref[...], preferred_element_type=F32)
    if last:
        out_ref[...] = (part + before[0][...]).T.astype(BF16)
    else:
        out_ref[...] = part


def backward(tile, fitted, before=None):
    n, m = tile.shape
    last = before is not None
    return pl.pallas_call(
        functools.partial(back_kernel, last=last),
        in_specs=[VMEM, VMEM] + [VMEM] * last,
        out_specs=VMEM,
        out_shape=jax.ShapeDtypeStruct((m, OUTS), BF16) if last else jax.ShapeDtypeStruct((OUTS, m), F32),
        scratch_shapes=[pltpu.VMEM((OUTS, n), BF16)],
        compiler_params=params(),
        cost_estimate=cost(2 * n * m * OUTS, 2 * n * m),
        name="tile_backward",
    )(tile, fitted, *([before] if last else []))


def field_kernel(me_ref, pre_ref, mine_ref, came_ref, feat_ref, out_ref, pre_here, dir_here, sems):
    parts = out_ref.shape[0]
    width = out_ref.shape[1] - 2 * FEAT
    blocks = sems.shape[0]
    block = pre_ref.shape[0] // blocks
    copies = [
        pltpu.make_async_copy(pre_ref.at[pl.ds(j * block, block)], pre_here.at[pl.ds(j * block, block)], sems.at[j])
        for j in range(blocks)
    ]
    for copy in copies:
        copy.start()
    me = me_ref[0]
    chips, share, _ = mine_ref.shape
    for j in range(chips):
        dir_here[pl.ds(pl.multiple_of((2 * j + me) * share, share), share)] = mine_ref[j]
        dir_here[pl.ds(pl.multiple_of((2 * j + 1 - me) * share, share), share)] = came_ref[j]
    for j in range(parts):
        out_ref[j, width:] = feat_ref[j]
    for j in range(blocks):
        copies[j].wait()
        part = jnp.dot(pre_here[j * block : (j + 1) * block], dir_here[...], preferred_element_type=F32).astype(BF16)
        for k in range(block // width):
            out_ref[j * (block // width) + k, :width] = part[k * width : (k + 1) * width]


def field(me, precond, mine, came, feat_parts, blocks=4):
    n, m = precond.shape
    parts = feat_parts.shape[0]
    return pl.pallas_call(
        field_kernel,
        in_specs=[SMEM, HBM, VMEM, VMEM, VMEM],
        out_specs=VMEM,
        out_shape=jax.ShapeDtypeStruct((parts, n // parts + 2 * FEAT, OUTS), BF16),
        scratch_shapes=[pltpu.VMEM((n, m), BF16), pltpu.VMEM((m, OUTS), BF16), pltpu.SemaphoreType.DMA((blocks,))],
        compiler_params=params(),
        cost_estimate=cost(2 * n * m * OUTS, 2 * n * m),
        name="precond_forward",
    )(me, in_hbm(precond), mine, came, feat_parts)


def image_kernel(core_ref, pre_ref, grad_ref, out_ref):
    core = core_ref[0]
    chips, width, _ = out_ref.shape
    grad = grad_ref[...].T
    for j in range(0, chips, 2):
        pair = [pre_ref[:, pl.ds(pl.multiple_of((2 * k + core) * width, width), width)] for k in (j, j + 1)]
        part = jnp.dot(grad, jnp.concatenate(pair, axis=1), preferred_element_type=F32).T
        out_ref[j] = part[:width]
        out_ref[j + 1] = part[width:]


def image_part(core, precond, grad, share):
    n, m = precond.shape
    return pl.pallas_call(
        image_kernel,
        in_specs=[SMEM, VMEM, VMEM],
        out_specs=VMEM,
        out_shape=jax.ShapeDtypeStruct((m // share // 2, share, OUTS), F32),
        compiler_params=params(),
        cost_estimate=cost(n * m * OUTS, n * m),
        name="precond_backward",
    )(core, precond, grad)


def numbers_kernel(part_ref, dir_ref, res_ref, image_ref, out_ref):
    direction, residual = dir_ref[...], res_ref[...]
    image = jnp.sum(part_ref[...].astype(F32), axis=0) + ridge_weight * direction
    image_ref[...] = image
    top = jnp.max(jnp.max(jnp.abs(image), axis=0, keepdims=True), axis=1, keepdims=True)
    top = jnp.where(top > 0, top, 1.0)
    scaled = image / top

    def total(value):
        return jnp.sum(jnp.sum(value, axis=0, keepdims=True), axis=1, keepdims=True)

    numbers = [total(residual * residual), total(direction * image), total(residual * scaled), total(scaled * scaled), top]
    lane = lax.broadcasted_iota(jnp.int32, (1, 128), 1)
    packed = jnp.zeros((1, 128), F32)
    for place, number in enumerate(numbers):
        packed = jnp.where(lane == place, number, packed)
    out_ref[...] = jnp.broadcast_to(packed, out_ref.shape)


def numbers(parts, direction, residual, devices):
    shape = jax.ShapeDtypeStruct(direction.shape, F32)
    return pl.pallas_call(
        numbers_kernel,
        out_shape=[shape, jax.ShapeDtypeStruct((devices, 128), F32)],
        compiler_params=params(),
        name="image_numbers",
    )(parts, direction, residual)


def finish_kernel(all_ref, image_ref, coef_ref, res_ref, dir_ref, coef_out, res_out, dir_out):
    every = all_ref[...]
    lane = lax.broadcasted_iota(jnp.int32, every.shape, 1)

    def column(place):
        return jnp.sum(jnp.where(lane == place, every, 0.0), axis=1, keepdims=True)

    tops = column(4)
    most = jnp.max(tops, axis=0, keepdims=True)
    ratio = tops / most
    norm_old = jnp.sum(column(0), axis=0, keepdims=True)
    curvature = jnp.sum(column(1), axis=0, keepdims=True)
    cross = jnp.sum(column(2) * ratio, axis=0, keepdims=True)
    square = jnp.sum(column(3) * ratio * ratio, axis=0, keepdims=True)
    step_size = norm_old / curvature
    reach = step_size * most
    norm_new = norm_old - 2.0 * reach * cross + reach * reach * square
    direction = dir_ref[...]
    coef_out[...] = coef_ref[...] + step_size * direction
    residual_next = res_ref[...] - step_size * image_ref[...]
    res_out[...] = residual_next
    dir_out[...] = residual_next + norm_new / norm_old * direction


def finish(every, image, coefficients, residual, direction):
    shape = jax.ShapeDtypeStruct(direction.shape, F32)
    return pl.pallas_call(
        finish_kernel,
        out_shape=[shape, shape, shape],
        compiler_params=params(),
        name="finish",
    )(every, image, coefficients, residual, direction)


def spread(part, axes):
    return lax.all_to_all(part, axes, 0, 0, tiled=True)


def sum_kernel(parts_ref, out_ref, *, scale):
    total = jnp.sum(parts_ref[...].astype(F32), axis=0)
    if scale is not None:
        total = total * scale
    out_ref[...] = jnp.broadcast_to(total.astype(BF16)[None], out_ref.shape)


def all_summed(parts, axes, scale=None):
    own = spread(parts, axes)
    copies = pl.pallas_call(
        functools.partial(sum_kernel, scale=scale),
        out_shape=jax.ShapeDtypeStruct(parts.shape, BF16),
        compiler_params=params(8),
        name="sum_copies",
    )(own)
    return spread(copies, axes)


def swapped(part):
    return lax.ppermute(part, "core", SWAP)


def on_device(train_rows, centre_index, precond, coefficients, residual, direction):
    rows_here = train_rows.shape[0]
    cen_here = centre_index.shape[0]
    row_devices = lax.axis_size("yh") * lax.axis_size("z")
    cen_devices = lax.axis_size("yl") * lax.axis_size("x") * lax.axis_size("core")
    me = lax.axis_index("core").astype(jnp.int32)[None]
    start_row = (lax.axis_index(ROWS) * rows_here).astype(jnp.int32)
    share = cen_here // row_devices

    other = 1 - me
    dir_mine = spread(copies_of(direction, cen_devices // 2), CHIPS)

    feat = train_rows.T
    picked = pick(start_row[None], centre_index[None], feat, row_devices)
    dir_mine, picked, other = lax.optimization_barrier((dir_mine, picked, other))
    got = all_summed(field(me, precond, dir_mine, swapped(dir_mine), picked), ROWS)

    chips_shape = (cen_devices // 2, rows_here // cen_devices, OUTS)
    tile_other, fit_other, cen_op, coef = tile_forward(other, feat, [got], BF16)
    fit_came = swapped(fit_other)
    tile_mine, fit_mine = tile_forward(me, feat, [cen_op, coef], F32)
    fit_mine, fit_came = lax.optimization_barrier((fit_mine, fit_came))
    half = (fit_mine + fit_came.astype(F32)).astype(BF16).reshape(chips_shape)
    fitted = all_summed(half, CHIPS)
    fitted_came = swapped(fitted)
    grad_mine = backward(tile_mine, fitted)
    grad_mine, fitted_came = lax.optimization_barrier((grad_mine, fitted_came))
    grad_part = backward(tile_other, fitted_came, grad_mine).reshape(row_devices, share, OUTS)

    grad_low = all_summed(grad_part, ROWS, float(rows_here * row_devices) ** (-0.5)).reshape(cen_here, OUTS)

    image_came = swapped(image_part(other, precond, grad_low, direction.shape[0]))
    image_mine = image_part(me, precond, grad_low, direction.shape[0])
    image_mine, image_came = lax.optimization_barrier((image_mine, image_came))
    half = (image_mine + image_came).astype(BF16)
    image, row = numbers(spread(half, CHIPS), direction, residual, row_devices * cen_devices)
    every = spread(row, (*ROWS, *CENT))
    return tuple(finish(every, image, coefficients, residual, direction))


def solution(mesh):
    fine = Mesh(np.asarray(mesh.devices).reshape([size for _, size in FINE]), [name for name, _ in FINE])
    every = P((*ROWS, *CENT), None)
    return jax.shard_map(
        on_device,
        mesh=fine,
        in_specs=(P(ROWS, None), P(CENT), P(CENT, ROWS), every, every, every),
        out_specs=(every, every, every),
        check_vma=False,
    )
```

```python
import functools
import math

import jax
import jax.numpy as jnp
import numpy as np
from jax import lax
from jax.experimental import pallas as pl
from jax.experimental.pallas import tpu as pltpu
from jax.sharding import Mesh
from jax.sharding import PartitionSpec as P

FEAT = 64
OUTS = 128
ridge_weight = 0.1
F32, BF16 = jnp.float32, jnp.bfloat16

FINE = (("yh", 2), ("z", 4), ("yl", 2), ("x", 4), ("core", 2))
ROWS = ("yh", "z")
CHIPS = ("yl", "x")
CENT = ("yl", "x", "core")
FEATURE_SCALE = math.sqrt(2.0 * (2.0 / FEAT) * math.log2(math.e))
SWAP = [(0, 1), (1, 0)]


VMEM = pl.BlockSpec(memory_space=pltpu.VMEM)
SMEM = pl.BlockSpec(memory_space=pltpu.SMEM)
HBM = pl.BlockSpec(memory_space=pltpu.HBM)


def params(limit=16):
    return pltpu.CompilerParams(vmem_limit_bytes=limit * 1024 * 1024)


def cost(flops, nbytes, exps=0):
    return pl.CostEstimate(flops=flops, bytes_accessed=nbytes, transcendentals=exps)


def in_hbm(value):
    return pltpu.with_memory_space_constraint(value, pltpu.HBM)


def split_pieces(value, count):
    out = []
    for _ in range(count):
        top = value.astype(BF16)
        out.append(top)
        value = value - top.astype(F32)
    return out


def operand(high, mid, row_side):
    n = high.shape[1]
    value = high.astype(F32) + mid.astype(F32)
    norm = -0.5 * jnp.sum(value * value, axis=0, keepdims=True)
    line = lax.broadcasted_iota(jnp.int32, (FEAT, n), 0)
    tail = jnp.zeros((FEAT, n), F32)
    first_norm, first_one = (0, 3) if row_side else (3, 0)
    for place, piece in enumerate(split_pieces(norm, 3)):
        tail = jnp.where(line == first_norm + place, piece.astype(F32), tail)
    tail = jnp.where((line >= first_one) & (line < first_one + 3), 1.0, tail).astype(BF16)
    middle = (high, mid) if row_side else (mid, high)
    return jnp.concatenate([high, *middle, tail], axis=0)


def pick_kernel(place_ref, index_hbm, feat_hbm, *refs, ring):
    parts = refs[:ring]
    feat_ref, index_ref, total_ref, sems = refs[ring:]
    n = feat_ref.shape[1]
    m = index_ref.shape[1]
    pieces = sems.shape[0] - 1
    wide = n // pieces
    copies = [pltpu.make_async_copy(index_hbm, index_ref, sems.at[0])]
    for j in range(pieces):
        here = pl.ds(j * wide, wide)
        copies.append(pltpu.make_async_copy(feat_hbm.at[:, here], feat_ref.at[:, here], sems.at[1 + j]))
    for copy in copies:
        copy.start()
    copies[0].wait()
    block = 512
    for j in range(n // block):
        if j * block % wide == 0:
            copies[1 + j * block // wide].wait()
        here = slice(j * block, (j + 1) * block)
        table = jnp.concatenate(split_pieces(feat_ref[:, here] * FEATURE_SCALE, 2), axis=0)
        wanted = index_ref[...] - (place_ref[0] + j * block)
        row = lax.broadcasted_iota(jnp.int32, (block, m), 0)
        choice = jnp.where(row == wanted, 1.0, 0.0).astype(BF16)
        part = jnp.dot(table, choice, preferred_element_type=F32)
        if j == 0:
            total_ref[...] = part
        else:
            total_ref[...] += part
    width = m // ring
    for k in range(ring):
        first = pl.multiple_of(lax.rem(place_ref[1] + k, ring) * width, width)
        parts[k][...] = total_ref[:, pl.ds(first, width)].astype(BF16)


def pick(place, index, feat, ring, pieces=4):
    depth, n = feat.shape
    m = index.shape[1]
    return pl.pallas_call(
        functools.partial(pick_kernel, ring=ring),
        in_specs=[SMEM, HBM, HBM],
        out_specs=[VMEM] * ring,
        out_shape=[jax.ShapeDtypeStruct((2 * depth, m // ring), BF16)] * ring,
        scratch_shapes=[
            pltpu.VMEM(feat.shape, F32),
            pltpu.VMEM((1, m), jnp.int32),
            pltpu.VMEM((2 * depth, m), F32),
            pltpu.SemaphoreType.DMA((1 + pieces,)),
        ],
        compiler_params=params(),
        cost_estimate=cost(2 * n * m * 128 * 4, n * depth * 4),
        name="pick_centres",
    )(place, in_hbm(index), in_hbm(feat))


def load_kernel(source, out_ref, sems):
    pieces = sems.shape[0]
    tall = source.shape[0] // pieces
    copies = [
        pltpu.make_async_copy(source.at[pl.ds(j * tall, tall)], out_ref.at[pl.ds(j * tall, tall)], sems.at[j])
        for j in range(pieces)
    ]
    for copy in copies:
        copy.start()
    for copy in copies:
        copy.wait()


def loaded(source, pieces=2):
    return pl.pallas_call(
        load_kernel,
        in_specs=[HBM],
        out_specs=VMEM,
        out_shape=jax.ShapeDtypeStruct(source.shape, source.dtype),
        scratch_shapes=[pltpu.SemaphoreType.DMA((pieces,))],
        compiler_params=params(8),
        cost_estimate=cost(0, 2 * source.size),
        name="precond_load",
    )(in_hbm(source))


def add_kernel(*refs):
    *parts, out_ref = refs
    out_ref[...] = sum(part[...].astype(F32) for part in parts).astype(BF16)


def added(*parts):
    return pl.pallas_call(
        add_kernel,
        out_shape=jax.ShapeDtypeStruct(parts[0].shape, BF16),
        compiler_params=params(8),
        name="features_sum",
    )(*parts)


def send_kernel(dir_ref, out_ref):
    out_ref[...] = jnp.broadcast_to(dir_ref[...].astype(BF16)[None], out_ref.shape)


def copies_of(direction, count):
    return pl.pallas_call(
        send_kernel,
        out_shape=jax.ShapeDtypeStruct((count, *direction.shape), BF16),
        compiler_params=params(),
        name="direction_copies",
    )(direction)


def tile_kernel(place_ref, half_ref, feat_ref, coef_ref, *refs, first):
    tile_ref, fit_ref, cen_ref = refs[-3:] if first else (*refs[1:], refs[0])
    if first:
        parts = refs[:-3]
        ring = len(parts)
        width = parts[0].shape[1]
        for k in range(ring):
            start = pl.multiple_of(lax.rem(place_ref[1] + ring - k, ring) * width, width)
            cen_ref[:, pl.ds(start, width)] = operand(parts[k][:FEAT], parts[k][FEAT:], False)
    n = fit_ref.shape[0]
    block = 256
    for j in range(n // block):
        here = slice(j * block, (j + 1) * block)
        place = pl.ds(pl.multiple_of(half_ref[0] * n + j * block, block), block)
        high, mid = split_pieces(feat_ref[:, place] * FEATURE_SCALE, 2)
        power = jnp.dot(operand(high, mid, True).T, cen_ref[...], preferred_element_type=F32)
        tile = jnp.exp2(power).astype(BF16)
        tile_ref[here] = tile
        fit_ref[here] = jnp.dot(tile, coef_ref[...], preferred_element_type=F32).astype(fit_ref.dtype)


def tile_forward(place, half, feat, coef, centres, fit_type):
    n, m = feat.shape[1] // 2, coef.shape[0]
    first = len(centres) > 1
    more = [jax.ShapeDtypeStruct((256, m), BF16)] * first
    return pl.pallas_call(
        functools.partial(tile_kernel, first=first),
        in_specs=[SMEM, SMEM] + [VMEM] * (2 + len(centres)),
        out_specs=[VMEM] * (2 + len(more)),
        out_shape=[jax.ShapeDtypeStruct((n, m), BF16), jax.ShapeDtypeStruct((n, OUTS), fit_type), *more],
        compiler_params=params(),
        cost_estimate=cost(2 * n * m * 384, 2 * n * m, n * m),
        name="tile_forward",
    )(place, half, feat, coef, *centres)


def back_kernel(*refs, last):
    tile_ref, fit_ref, *before, out_ref, turned = refs
    parts, share, _ = fit_ref.shape
    for j in range(parts):
        turned[:, j * share : (j + 1) * share] = fit_ref[j].T
    part = jnp.dot(turned[...], tile_ref[...], preferred_element_type=F32)
    if last:
        out_ref[...] = (part + before[0][...]).T.astype(BF16)
    else:
        out_ref[...] = part


def backward(tile, fitted, before=None):
    n, m = tile.shape
    last = before is not None
    return pl.pallas_call(
        functools.partial(back_kernel, last=last),
        in_specs=[VMEM, VMEM] + [VMEM] * last,
        out_specs=VMEM,
        out_shape=jax.ShapeDtypeStruct((m, OUTS), BF16) if last else jax.ShapeDtypeStruct((OUTS, m), F32),
        scratch_shapes=[pltpu.VMEM((OUTS, n), BF16)],
        compiler_params=params(),
        cost_estimate=cost(2 * n * m * OUTS, 2 * n * m),
        name="tile_backward",
    )(tile, fitted, *([before] if last else []))


def field_kernel(me_ref, pre_ref, mine_ref, came_ref, out_ref, dir_here):
    me = me_ref[0]
    chips, share, _ = mine_ref.shape
    for j in range(chips):
        dir_here[pl.ds(pl.multiple_of((2 * j + me) * share, share), share)] = mine_ref[j]
        dir_here[pl.ds(pl.multiple_of((2 * j + 1 - me) * share, share), share)] = came_ref[j]
    out_ref[...] = jnp.dot(pre_ref[...], dir_here[...], preferred_element_type=F32).astype(BF16)


def field(me, precond, mine, came):
    n, m = precond.shape
    return pl.pallas_call(
        field_kernel,
        in_specs=[SMEM, VMEM, VMEM, VMEM],
        out_specs=VMEM,
        out_shape=jax.ShapeDtypeStruct((n, OUTS), BF16),
        scratch_shapes=[pltpu.VMEM((m, OUTS), BF16)],
        compiler_params=params(),
        cost_estimate=cost(2 * n * m * OUTS, 2 * n * m),
        name="precond_forward",
    )(me, precond, mine, came)


def image_kernel(core_ref, pre_ref, grad_ref, out_ref):
    core = core_ref[0]
    chips, width, _ = out_ref.shape
    grad = grad_ref[...].T
    for j in range(0, chips, 2):
        pair = [pre_ref[:, pl.ds(pl.multiple_of((2 * k + core) * width, width), width)] for k in (j, j + 1)]
        part = jnp.dot(grad, jnp.concatenate(pair, axis=1), preferred_element_type=F32).T
        out_ref[j] = part[:width]
        out_ref[j + 1] = part[width:]


def image_part(core, precond, grad, share):
    n, m = precond.shape
    return pl.pallas_call(
        image_kernel,
        in_specs=[SMEM, VMEM, VMEM],
        out_specs=VMEM,
        out_shape=jax.ShapeDtypeStruct((m // share // 2, share, OUTS), F32),
        compiler_params=params(),
        cost_estimate=cost(n * m * OUTS, n * m),
        name="precond_backward",
    )(core, precond, grad)


def numbers_kernel(part_ref, dir_ref, res_ref, image_ref, out_ref):
    direction, residual = dir_ref[...], res_ref[...]
    image = jnp.sum(part_ref[...].astype(F32), axis=0) + ridge_weight * direction
    image_ref[...] = image
    top = jnp.max(jnp.max(jnp.abs(image), axis=0, keepdims=True), axis=1, keepdims=True)
    top = jnp.where(top > 0, top, 1.0)
    scaled = image / top

    def total(value):
        return jnp.sum(jnp.sum(value, axis=0, keepdims=True), axis=1, keepdims=True)

    numbers = [total(residual * residual), total(direction * image), total(residual * scaled), total(scaled * scaled), top]
    lane = lax.broadcasted_iota(jnp.int32, (1, 128), 1)
    packed = jnp.zeros((1, 128), F32)
    for place, number in enumerate(numbers):
        packed = jnp.where(lane == place, number, packed)
    out_ref[...] = jnp.broadcast_to(packed, out_ref.shape)


def numbers(parts, direction, residual, devices):
    shape = jax.ShapeDtypeStruct(direction.shape, F32)
    return pl.pallas_call(
        numbers_kernel,
        out_shape=[shape, jax.ShapeDtypeStruct((devices, 128), F32)],
        compiler_params=params(),
        name="image_numbers",
    )(parts, direction, residual)


def finish_kernel(all_ref, image_ref, coef_ref, res_ref, dir_ref, coef_out, res_out, dir_out):
    every = all_ref[...]
    lane = lax.broadcasted_iota(jnp.int32, every.shape, 1)

    def column(place):
        return jnp.sum(jnp.where(lane == place, every, 0.0), axis=1, keepdims=True)

    tops = column(4)
    most = jnp.max(tops, axis=0, keepdims=True)
    ratio = tops / most
    norm_old = jnp.sum(column(0), axis=0, keepdims=True)
    curvature = jnp.sum(column(1), axis=0, keepdims=True)
    cross = jnp.sum(column(2) * ratio, axis=0, keepdims=True)
    square = jnp.sum(column(3) * ratio * ratio, axis=0, keepdims=True)
    step_size = norm_old / curvature
    reach = step_size * most
    norm_new = norm_old - 2.0 * reach * cross + reach * reach * square
    direction = dir_ref[...]
    coef_out[...] = coef_ref[...] + step_size * direction
    residual_next = res_ref[...] - step_size * image_ref[...]
    res_out[...] = residual_next
    dir_out[...] = residual_next + norm_new / norm_old * direction


def finish(every, image, coefficients, residual, direction):
    shape = jax.ShapeDtypeStruct(direction.shape, F32)
    return pl.pallas_call(
        finish_kernel,
        out_shape=[shape, shape, shape],
        compiler_params=params(),
        name="finish",
    )(every, image, coefficients, residual, direction)


def spread(part, axes):
    return lax.all_to_all(part, axes, 0, 0, tiled=True)


def sum_kernel(parts_ref, out_ref, *, scale):
    total = jnp.sum(parts_ref[...].astype(F32), axis=0)
    if scale is not None:
        total = total * scale
    out_ref[...] = jnp.broadcast_to(total.astype(BF16)[None], out_ref.shape)


def sum_copies(parts, scale=None):
    return pl.pallas_call(
        functools.partial(sum_kernel, scale=scale),
        out_shape=jax.ShapeDtypeStruct(parts.shape, BF16),
        compiler_params=params(8),
        name="sum_copies",
    )(parts)


def all_summed(parts, axes, scale=None):
    return spread(sum_copies(spread(parts, axes), scale), axes)


def swapped(part):
    return lax.ppermute(part, "core", SWAP)


def on_device(train_rows, centre_index, precond, coefficients, residual, direction):
    rows_here = train_rows.shape[0]
    cen_here = centre_index.shape[0]
    row_devices = lax.axis_size("yh") * lax.axis_size("z")
    cen_devices = lax.axis_size("yl") * lax.axis_size("x") * lax.axis_size("core")
    me = lax.axis_index("core").astype(jnp.int32)[None]
    other = 1 - me
    ring = lax.axis_size("z")
    place = jnp.stack([lax.axis_index(ROWS) * rows_here, lax.axis_index("z")]).astype(jnp.int32)
    share = cen_here // row_devices

    def onward(part, by):
        return lax.ppermute(part, "z", [(i, (i + by) % ring) for i in range(ring)])

    dir_mine = spread(copies_of(direction, cen_devices // 2), CHIPS)

    feat = train_rows.T
    picked = pick(place, centre_index[None], feat, ring)
    dir_mine, *picked = lax.optimization_barrier((dir_mine, *picked))
    came = [picked[0]] + [onward(picked[k], k) for k in range(1, ring)]
    dir_mine, own_precond, other = lax.optimization_barrier((dir_mine, precond, other))
    field_part = field(me, loaded(own_precond), dir_mine, swapped(dir_mine))
    field_part, came[0] = lax.optimization_barrier((field_part, came[0]))
    own = added(*came)
    own = added(own, lax.ppermute(own, "yh", SWAP))
    features = [own] + [onward(own, k) for k in range(1, ring)]
    copies = sum_copies(spread(field_part.reshape(row_devices, share, OUTS), ROWS))
    copies, features = lax.optimization_barrier((copies, features))
    coef = spread(copies, ROWS).reshape(cen_here, OUTS)

    chips_shape = (cen_devices // 2, rows_here // cen_devices, OUTS)
    tile_other, fit_other, cen_op = tile_forward(place, other, feat, coef, features, BF16)
    fit_came = swapped(fit_other)
    tile_mine, fit_mine = tile_forward(place, me, feat, coef, [cen_op], F32)
    fit_mine, fit_came = lax.optimization_barrier((fit_mine, fit_came))
    half = (fit_mine + fit_came.astype(F32)).astype(BF16).reshape(chips_shape)
    fitted = all_summed(half, CHIPS)
    fitted_came = swapped(fitted)
    grad_mine = backward(tile_mine, fitted)
    grad_mine, fitted_came = lax.optimization_barrier((grad_mine, fitted_came))
    grad_part = backward(tile_other, fitted_came, grad_mine).reshape(row_devices, share, OUTS)

    grad_low = all_summed(grad_part, ROWS, float(rows_here * row_devices) ** (-0.5)).reshape(cen_here, OUTS)

    image_came = swapped(image_part(other, precond, grad_low, direction.shape[0]))
    image_mine = image_part(me, precond, grad_low, direction.shape[0])
    image_mine, image_came = lax.optimization_barrier((image_mine, image_came))
    half = (image_mine + image_came).astype(BF16)
    image, row = numbers(spread(half, CHIPS), direction, residual, row_devices * cen_devices)
    every = spread(row, (*ROWS, *CENT))
    return tuple(finish(every, image, coefficients, residual, direction))


def solution(mesh):
    fine = Mesh(np.asarray(mesh.devices).reshape([size for _, size in FINE]), [name for name, _ in FINE])
    every = P((*ROWS, *CENT), None)
    return jax.shard_map(
        on_device,
        mesh=fine,
        in_specs=(P(ROWS, None), P(CENT), P(CENT, ROWS), every, every, every),
        out_specs=(every, every, every),
        check_vma=False,
    )
```

```python
import functools
import math

import jax
import jax.numpy as jnp
import numpy as np
from jax import lax
from jax.experimental import pallas as pl
from jax.experimental.pallas import tpu as pltpu
from jax.sharding import Mesh
from jax.sharding import PartitionSpec as P

FEAT = 64
OUTS = 128
ridge_weight = 0.1
F32, BF16 = jnp.float32, jnp.bfloat16

FINE = (("yh", 2), ("z", 4), ("yl", 2), ("x", 4), ("core", 2))
ROWS = ("yh", "z")
CHIPS = ("yl", "x")
CENT = ("yl", "x", "core")
FEATURE_SCALE = math.sqrt(2.0 * (2.0 / FEAT) * math.log2(math.e))
SWAP = [(0, 1), (1, 0)]


VMEM = pl.BlockSpec(memory_space=pltpu.VMEM)
SMEM = pl.BlockSpec(memory_space=pltpu.SMEM)
HBM = pl.BlockSpec(memory_space=pltpu.HBM)


def params(limit=16):
    return pltpu.CompilerParams(vmem_limit_bytes=limit * 1024 * 1024)


def cost(flops, nbytes, exps=0):
    return pl.CostEstimate(flops=flops, bytes_accessed=nbytes, transcendentals=exps)


def in_hbm(value):
    return pltpu.with_memory_space_constraint(value, pltpu.HBM)


def split_pieces(value, count):
    out = []
    for _ in range(count):
        top = value.astype(BF16)
        out.append(top)
        value = value - top.astype(F32)
    return out


def operand(high, mid, row_side):
    n = high.shape[1]
    value = high.astype(F32) + mid.astype(F32)
    norm = -0.5 * jnp.sum(value * value, axis=0, keepdims=True)
    line = lax.broadcasted_iota(jnp.int32, (FEAT, n), 0)
    tail = jnp.zeros((FEAT, n), F32)
    first_norm, first_one = (0, 3) if row_side else (3, 0)
    for place, piece in enumerate(split_pieces(norm, 3)):
        tail = jnp.where(line == first_norm + place, piece.astype(F32), tail)
    tail = jnp.where((line >= first_one) & (line < first_one + 3), 1.0, tail).astype(BF16)
    middle = (high, mid) if row_side else (mid, high)
    return jnp.concatenate([high, *middle, tail], axis=0)


def pick_kernel(start_ref, index_ref, feat_ref, out_ref, total_ref):
    step = pl.program_id(0)
    block = feat_ref.shape[1]

    @pl.when(step == 0)
    def _():
        total_ref[...] = jnp.zeros_like(total_ref)

    table = jnp.concatenate(split_pieces(feat_ref[...] * FEATURE_SCALE, 2), axis=0)
    wanted = index_ref[...] - (start_ref[0] + step * block)
    place = lax.broadcasted_iota(jnp.int32, (block, wanted.shape[1]), 0)
    choice = jnp.where(place == wanted, 1.0, 0.0).astype(BF16)
    total_ref[...] += jnp.dot(table, choice, preferred_element_type=F32)

    @pl.when(step == pl.num_programs(0) - 1)
    def _():
        for j in range(out_ref.shape[0]):
            width = out_ref.shape[2]
            out_ref[j] = total_ref[:, j * width : (j + 1) * width].astype(BF16)


def pick(start, index, feat, parts, block=512):
    depth, n = feat.shape
    m = index.shape[1]
    return pl.pallas_call(
        pick_kernel,
        grid=(n // block,),
        in_specs=[
            pl.BlockSpec(memory_space=pltpu.SMEM),
            pl.BlockSpec((1, m), lambda i: (0, 0)),
            pl.BlockSpec((depth, block), lambda i: (0, i)),
        ],
        out_specs=pl.BlockSpec((parts, 2 * depth, m // parts), lambda i: (0, 0, 0)),
        out_shape=jax.ShapeDtypeStruct((parts, 2 * depth, m // parts), BF16),
        scratch_shapes=[pltpu.VMEM((2 * depth, m), F32)],
        compiler_params=params(),
        cost_estimate=cost(2 * n * m * 128 * 4, n * depth * 4),
        name="pick_centres",
    )(start, index, feat)


def send_kernel(dir_hbm, out_hbm, dir_ref, low_ref, sems):
    load = pltpu.make_async_copy(dir_hbm, dir_ref, sems.at[0])
    load.start()
    load.wait()
    low_ref[...] = dir_ref[...].astype(BF16)
    stores = [pltpu.make_async_copy(low_ref, out_hbm.at[j], sems.at[1 + j]) for j in range(out_hbm.shape[0])]
    for store in stores:
        store.start()
    for store in stores:
        store.wait()


def copies_of(direction, count):
    return pl.pallas_call(
        send_kernel,
        in_specs=[HBM],
        out_specs=HBM,
        out_shape=pltpu.HBM((count, *direction.shape), BF16),
        scratch_shapes=[
            pltpu.VMEM(direction.shape, F32),
            pltpu.VMEM(direction.shape, BF16),
            pltpu.SemaphoreType.DMA((1 + count,)),
        ],
        compiler_params=params(8),
        name="direction_copies",
    )(in_hbm(direction))


def tile_kernel(*refs, first):
    if first:
        half_ref, feat_ref, got_ref, tile_ref, fit_ref, cen_ref, coef_ref = refs
        parts, depth, width = got_ref.shape
        share = depth - 2 * FEAT
        for j in range(parts):
            both = got_ref[j, share:]
            cen_ref[:, j * width : (j + 1) * width] = operand(both[:FEAT], both[FEAT:], False)
            coef_ref[j * share : (j + 1) * share] = got_ref[j, :share]
    else:
        half_ref, feat_ref, cen_ref, coef_ref, tile_ref, fit_ref = refs
    n = fit_ref.shape[0]
    block = 256
    blocks = n // block
    for j in range(blocks):
        here = slice(j * block, (j + 1) * block)
        place = pl.ds(pl.multiple_of(half_ref[0] * n + j * block, block), block)
        high, mid = split_pieces(feat_ref[:, place] * FEATURE_SCALE, 2)
        power = jnp.dot(operand(high, mid, True).T, cen_ref[...], preferred_element_type=F32)
        tile = jnp.exp2(power).astype(BF16)
        tile_ref[here] = tile
        fit_ref[here] = jnp.dot(tile, coef_ref[...], preferred_element_type=F32).astype(fit_ref.dtype)


def tile_forward(half, feat, operands, fit_type):
    n = feat.shape[1] // 2
    first = len(operands) == 1
    if first:
        parts, depth, width = operands[0].shape
        m = parts * width
        more = [
            jax.ShapeDtypeStruct((256, m), BF16),
            jax.ShapeDtypeStruct((parts * (depth - 2 * FEAT), OUTS), BF16),
        ]
    else:
        m = operands[0].shape[1]
        more = []
    return pl.pallas_call(
        functools.partial(tile_kernel, first=first),
        in_specs=[SMEM, VMEM] + [VMEM] * len(operands),
        out_specs=[VMEM] * (2 + len(more)),
        out_shape=[jax.ShapeDtypeStruct((n, m), BF16), jax.ShapeDtypeStruct((n, OUTS), fit_type), *more],
        compiler_params=params(),
        cost_estimate=cost(2 * n * m * 384, 2 * n * m, n * m),
        name="tile_forward",
    )(half, feat, *operands)


def back_kernel(*refs, last):
    tile_ref, fit_ref, *before, out_ref, turned = refs
    parts, share, _ = fit_ref.shape
    for j in range(parts):
        turned[:, j * share : (j + 1) * share] = fit_ref[j].T
    part = jnp.dot(turned[...], tile_ref[...], preferred_element_type=F32)
    if last:
        out_ref[...] = (part + before[0][...]).T.astype(BF16)
    else:
        out_ref[...] = part


def backward(tile, fitted, before=None):
    n, m = tile.shape
    last = before is not None
    return pl.pallas_call(
        functools.partial(back_kernel, last=last),
        in_specs=[VMEM, VMEM] + [VMEM] * last,
        out_specs=VMEM,
        out_shape=jax.ShapeDtypeStruct((m, OUTS), BF16) if last else jax.ShapeDtypeStruct((OUTS, m), F32),
        scratch_shapes=[pltpu.VMEM((OUTS, n), BF16)],
        compiler_params=params(),
        cost_estimate=cost(2 * n * m * OUTS, 2 * n * m),
        name="tile_backward",
    )(tile, fitted, *([before] if last else []))


def core_columns(pre_ref, here, core, width, count):
    return jnp.concatenate(
        [pre_ref[here, pl.ds(pl.multiple_of((2 * j + core) * width, width), width)] for j in range(count)], axis=1
    )


def field_first_kernel(core_ref, pre_hbm, dir_ref, out_ref, pre_ref, sems):
    blocks = sems.shape[0]
    block = pre_ref.shape[0] // blocks
    copies = [
        pltpu.make_async_copy(pre_hbm.at[pl.ds(j * block, block)], pre_ref.at[pl.ds(j * block, block)], sems.at[j])
        for j in range(blocks)
    ]
    for copy in copies:
        copy.start()
    count, width, outs = dir_ref.shape
    direction = dir_ref[...].reshape(count * width, outs)
    for j in range(blocks):
        copies[j].wait()
        here = slice(j * block, (j + 1) * block)
        columns = core_columns(pre_ref, here, core_ref[0], width, count)
        out_ref[here] = jnp.dot(columns, direction, preferred_element_type=F32)


def field_first(core, precond, direction, blocks=4):
    n, m = precond.shape
    return pl.pallas_call(
        field_first_kernel,
        in_specs=[SMEM, HBM, VMEM],
        out_specs=[VMEM, VMEM],
        out_shape=[jax.ShapeDtypeStruct((n, OUTS), F32), jax.ShapeDtypeStruct((n, m), BF16)],
        scratch_shapes=[pltpu.SemaphoreType.DMA((blocks,))],
        compiler_params=params(),
        cost_estimate=cost(n * m * OUTS, 4 * n * m),
        name="precond_first",
    )(core, in_hbm(precond), direction)


def field_second_kernel(core_ref, pre_ref, dir_ref, before_ref, feat_ref, out_ref):
    parts = out_ref.shape[0]
    share = out_ref.shape[1] - 2 * FEAT
    count, width, outs = dir_ref.shape
    direction = dir_ref[...].reshape(count * width, outs)
    block = 256
    for j in range(pre_ref.shape[0] // block):
        here = slice(j * block, (j + 1) * block)
        columns = core_columns(pre_ref, here, core_ref[0], width, count)
        part = jnp.dot(columns, direction, preferred_element_type=F32) + before_ref[here]
        part = part.astype(BF16)
        for k in range(block // share):
            out_ref[j * (block // share) + k, :share] = part[k * share : (k + 1) * share]
    for j in range(parts):
        out_ref[j, share:] = feat_ref[j]


def field_second(core, precond, direction, before, feat_parts):
    n, m = precond.shape
    parts = feat_parts.shape[0]
    return pl.pallas_call(
        field_second_kernel,
        in_specs=[SMEM, VMEM, VMEM, VMEM, VMEM],
        out_specs=VMEM,
        out_shape=jax.ShapeDtypeStruct((parts, n // parts + 2 * FEAT, OUTS), BF16),
        compiler_params=params(),
        cost_estimate=cost(n * m * OUTS, n * m),
        name="precond_second",
    )(core, precond, direction, before, feat_parts)


def image_kernel(core_ref, pre_ref, grad_ref, out_ref):
    core = core_ref[0]
    chips, width, _ = out_ref.shape
    grad = grad_ref[...].T
    for j in range(0, chips, 2):
        pair = [pre_ref[:, pl.ds(pl.multiple_of((2 * k + core) * width, width), width)] for k in (j, j + 1)]
        part = jnp.dot(grad, jnp.concatenate(pair, axis=1), preferred_element_type=F32).T
        out_ref[j] = part[:width]
        out_ref[j + 1] = part[width:]


def image_part(core, precond, grad, share):
    n, m = precond.shape
    return pl.pallas_call(
        image_kernel,
        in_specs=[SMEM, VMEM, VMEM],
        out_specs=VMEM,
        out_shape=jax.ShapeDtypeStruct((m // share // 2, share, OUTS), F32),
        compiler_params=params(),
        cost_estimate=cost(n * m * OUTS, n * m),
        name="precond_backward",
    )(core, precond, grad)


def numbers_kernel(part_ref, dir_ref, res_ref, image_ref, out_ref):
    direction, residual = dir_ref[...], res_ref[...]
    image = jnp.sum(part_ref[...].astype(F32), axis=0) + ridge_weight * direction
    image_ref[...] = image
    top = jnp.max(jnp.max(jnp.abs(image), axis=0, keepdims=True), axis=1, keepdims=True)
    top = jnp.where(top > 0, top, 1.0)
    scaled = image / top

    def total(value):
        return jnp.sum(jnp.sum(value, axis=0, keepdims=True), axis=1, keepdims=True)

    numbers = [total(residual * residual), total(direction * image), total(residual * scaled), total(scaled * scaled), top]
    lane = lax.broadcasted_iota(jnp.int32, (1, 128), 1)
    packed = jnp.zeros((1, 128), F32)
    for place, number in enumerate(numbers):
        packed = jnp.where(lane == place, number, packed)
    out_ref[...] = jnp.broadcast_to(packed, out_ref.shape)


def numbers(parts, direction, residual, devices):
    shape = jax.ShapeDtypeStruct(direction.shape, F32)
    return pl.pallas_call(
        numbers_kernel,
        out_shape=[shape, jax.ShapeDtypeStruct((devices, 128), F32)],
        compiler_params=params(),
        name="image_numbers",
    )(parts, direction, residual)


def finish_kernel(all_ref, image_ref, coef_ref, res_ref, dir_ref, coef_out, res_out, dir_out):
    every = all_ref[...]
    lane = lax.broadcasted_iota(jnp.int32, every.shape, 1)

    def column(place):
        return jnp.sum(jnp.where(lane == place, every, 0.0), axis=1, keepdims=True)

    tops = column(4)
    most = jnp.max(tops, axis=0, keepdims=True)
    ratio = tops / most
    norm_old = jnp.sum(column(0), axis=0, keepdims=True)
    curvature = jnp.sum(column(1), axis=0, keepdims=True)
    cross = jnp.sum(column(2) * ratio, axis=0, keepdims=True)
    square = jnp.sum(column(3) * ratio * ratio, axis=0, keepdims=True)
    step_size = norm_old / curvature
    reach = step_size * most
    norm_new = norm_old - 2.0 * reach * cross + reach * reach * square
    direction = dir_ref[...]
    coef_out[...] = coef_ref[...] + step_size * direction
    residual_next = res_ref[...] - step_size * image_ref[...]
    res_out[...] = residual_next
    dir_out[...] = residual_next + norm_new / norm_old * direction


def finish(every, image, coefficients, residual, direction):
    shape = jax.ShapeDtypeStruct(direction.shape, F32)
    return pl.pallas_call(
        finish_kernel,
        out_shape=[shape, shape, shape],
        compiler_params=params(),
        name="finish",
    )(every, image, coefficients, residual, direction)


def spread(part, axes):
    return lax.all_to_all(part, axes, 0, 0, tiled=True)


def sum_kernel(parts_ref, out_ref, *, scale):
    total = jnp.sum(parts_ref[...].astype(F32), axis=0)
    if scale is not None:
        total = total * scale
    out_ref[...] = jnp.broadcast_to(total.astype(BF16)[None], out_ref.shape)


def all_summed(parts, axes, scale=None):
    own = spread(parts, axes)
    copies = pl.pallas_call(
        functools.partial(sum_kernel, scale=scale),
        out_shape=jax.ShapeDtypeStruct(parts.shape, BF16),
        compiler_params=params(8),
        name="sum_copies",
    )(own)
    return spread(copies, axes)


def swapped(part):
    return lax.ppermute(part, "core", SWAP)


def on_device(train_rows, centre_index, precond, coefficients, residual, direction):
    rows_here = train_rows.shape[0]
    cen_here = centre_index.shape[0]
    row_devices = lax.axis_size("yh") * lax.axis_size("z")
    cen_devices = lax.axis_size("yl") * lax.axis_size("x") * lax.axis_size("core")
    me = lax.axis_index("core").astype(jnp.int32)[None]
    start_row = (lax.axis_index(ROWS) * rows_here).astype(jnp.int32)
    share = cen_here // row_devices

    other = 1 - me
    dir_mine = spread(copies_of(direction, cen_devices // 2), CHIPS)

    feat = train_rows.T
    picked = pick(start_row[None], centre_index[None], feat, row_devices)
    dir_mine, picked, other = lax.optimization_barrier((dir_mine, picked, other))
    dir_came = swapped(dir_mine)
    first, precond = field_first(me, precond, dir_mine)
    first, dir_came = lax.optimization_barrier((first, dir_came))
    got = all_summed(field_second(other, precond, dir_came, first, picked), ROWS)

    chips_shape = (cen_devices // 2, rows_here // cen_devices, OUTS)
    tile_other, fit_other, cen_op, coef = tile_forward(other, feat, [got], BF16)
    fit_came = swapped(fit_other)
    tile_mine, fit_mine = tile_forward(me, feat, [cen_op, coef], F32)
    fit_mine, fit_came = lax.optimization_barrier((fit_mine, fit_came))
    half = (fit_mine + fit_came.astype(F32)).astype(BF16).reshape(chips_shape)
    fitted = all_summed(half, CHIPS)
    fitted_came = swapped(fitted)
    grad_mine = backward(tile_mine, fitted)
    grad_mine, fitted_came = lax.optimization_barrier((grad_mine, fitted_came))
    grad_part = backward(tile_other, fitted_came, grad_mine).reshape(row_devices, share, OUTS)

    grad_low = all_summed(grad_part, ROWS, float(rows_here * row_devices) ** (-0.5)).reshape(cen_here, OUTS)

    image_came = swapped(image_part(other, precond, grad_low, direction.shape[0]))
    image_mine = image_part(me, precond, grad_low, direction.shape[0])
    image_mine, image_came = lax.optimization_barrier((image_mine, image_came))
    half = (image_mine + image_came).astype(BF16)
    image, row = numbers(spread(half, CHIPS), direction, residual, row_devices * cen_devices)
    every = spread(row, (*ROWS, *CENT))
    return tuple(finish(every, image, coefficients, residual, direction))


def solution(mesh):
    fine = Mesh(np.asarray(mesh.devices).reshape([size for _, size in FINE]), [name for name, _ in FINE])
    every = P((*ROWS, *CENT), None)
    return jax.shard_map(
        on_device,
        mesh=fine,
        in_specs=(P(ROWS, None), P(CENT), P(CENT, ROWS), every, every, every),
        out_specs=(every, every, every),
        check_vma=False,
    )
```

```python
import functools
import math

import jax
import jax.numpy as jnp
import numpy as np
from jax import lax
from jax.experimental import pallas as pl
from jax.experimental.pallas import tpu as pltpu
from jax.sharding import Mesh
from jax.sharding import PartitionSpec as P

FEAT = 64
OUTS = 128
ridge_weight = 0.1
F32, BF16 = jnp.float32, jnp.bfloat16

FINE = (("yh", 2), ("z", 4), ("yl", 2), ("x", 4), ("core", 2))
ROWS = ("yh", "z")
ROW_RING = ("z", "yh")
CHIPS = ("x", "yl")
CENT = ("yl", "x", "core")
FEATURE_SCALE = math.sqrt(2.0 * (2.0 / FEAT) * math.log2(math.e))
SWAP = [(0, 1), (1, 0)]


VMEM = pl.BlockSpec(memory_space=pltpu.VMEM)
SMEM = pl.BlockSpec(memory_space=pltpu.SMEM)
HBM = pl.BlockSpec(memory_space=pltpu.HBM)


def params(limit=16):
    return pltpu.CompilerParams(vmem_limit_bytes=limit * 1024 * 1024)


def cost(flops, nbytes, exps=0):
    return pl.CostEstimate(flops=flops, bytes_accessed=nbytes, transcendentals=exps)


def in_hbm(value):
    return pltpu.with_memory_space_constraint(value, pltpu.HBM)


def split_pieces(value, count):
    out = []
    for _ in range(count):
        top = value.astype(BF16)
        out.append(top)
        value = value - top.astype(F32)
    return out


def operand(high, mid, row_side):
    n = high.shape[1]
    value = high.astype(F32) + mid.astype(F32)
    norm = -0.5 * jnp.sum(value * value, axis=0, keepdims=True)
    line = lax.broadcasted_iota(jnp.int32, (FEAT, n), 0)
    tail = jnp.zeros((FEAT, n), F32)
    first_norm, first_one = (0, 3) if row_side else (3, 0)
    for place, piece in enumerate(split_pieces(norm, 3)):
        tail = jnp.where(line == first_norm + place, piece.astype(F32), tail)
    tail = jnp.where((line >= first_one) & (line < first_one + 3), 1.0, tail).astype(BF16)
    middle = (high, mid) if row_side else (mid, high)
    return jnp.concatenate([high, *middle, tail], axis=0)


def pick_kernel(start_ref, index_ref, feat_ref, out_ref, total_ref):
    step = pl.program_id(0)
    block = feat_ref.shape[1]

    @pl.when(step == 0)
    def _():
        total_ref[...] = jnp.zeros_like(total_ref)

    table = jnp.concatenate(split_pieces(feat_ref[...] * FEATURE_SCALE, 2), axis=0)
    wanted = index_ref[...] - (start_ref[0] + step * block)
    place = lax.broadcasted_iota(jnp.int32, (block, wanted.shape[1]), 0)
    choice = jnp.where(place == wanted, 1.0, 0.0).astype(BF16)
    total_ref[...] += jnp.dot(table, choice, preferred_element_type=F32)

    @pl.when(step == pl.num_programs(0) - 1)
    def _():
        for j in range(out_ref.shape[0]):
            width = out_ref.shape[2]
            out_ref[j] = total_ref[:, j * width : (j + 1) * width].astype(BF16)


def pick(start, index, feat, parts, block=512):
    depth, n = feat.shape
    m = index.shape[1]
    return pl.pallas_call(
        pick_kernel,
        grid=(n // block,),
        in_specs=[
            pl.BlockSpec(memory_space=pltpu.SMEM),
            pl.BlockSpec((1, m), lambda i: (0, 0)),
            pl.BlockSpec((depth, block), lambda i: (0, i)),
        ],
        out_specs=pl.BlockSpec((parts, 2 * depth, m // parts), lambda i: (0, 0, 0)),
        out_shape=jax.ShapeDtypeStruct((parts, 2 * depth, m // parts), BF16),
        scratch_shapes=[pltpu.VMEM((2 * depth, m), F32)],
        compiler_params=params(),
        cost_estimate=cost(2 * n * m * 128 * 4, n * depth * 4),
        name="pick_centres",
    )(start, index, feat)


def send_kernel(dir_hbm, out_hbm, dir_ref, low_ref, sems):
    load = pltpu.make_async_copy(dir_hbm, dir_ref, sems.at[0])
    load.start()
    load.wait()
    low_ref[...] = dir_ref[...].astype(BF16)
    stores = [pltpu.make_async_copy(low_ref, out_hbm.at[j], sems.at[1 + j]) for j in range(out_hbm.shape[0])]
    for store in stores:
        store.start()
    for store in stores:
        store.wait()


def copies_of(direction, count):
    return pl.pallas_call(
        send_kernel,
        in_specs=[HBM],
        out_specs=HBM,
        out_shape=pltpu.HBM((count, *direction.shape), BF16),
        scratch_shapes=[
            pltpu.VMEM(direction.shape, F32),
            pltpu.VMEM(direction.shape, BF16),
            pltpu.SemaphoreType.DMA((1 + count,)),
        ],
        compiler_params=params(8),
        name="direction_copies",
    )(in_hbm(direction))


def tile_kernel(*refs, first):
    if first:
        half_ref, feat_ref, got_ref, tile_ref, fit_ref, cen_ref, coef_ref = refs
        parts, depth, width = got_ref.shape
        share = depth - 2 * FEAT
        for j in range(parts):
            both = got_ref[j, share:]
            cen_ref[:, j * width : (j + 1) * width] = operand(both[:FEAT], both[FEAT:], False)
            coef_ref[j * share : (j + 1) * share] = got_ref[j, :share]
    else:
        half_ref, feat_ref, cen_ref, coef_ref, tile_ref, fit_ref = refs
    n = fit_ref.shape[0]
    block = 256
    blocks = n // block
    for j in range(blocks):
        here = slice(j * block, (j + 1) * block)
        place = pl.ds(pl.multiple_of(half_ref[0] * n + j * block, block), block)
        high, mid = split_pieces(feat_ref[:, place] * FEATURE_SCALE, 2)
        power = jnp.dot(operand(high, mid, True).T, cen_ref[...], preferred_element_type=F32)
        tile = jnp.exp2(power).astype(BF16)
        tile_ref[here] = tile
        fit_ref[here] = jnp.dot(tile, coef_ref[...], preferred_element_type=F32).astype(fit_ref.dtype)


def tile_forward(half, feat, operands, fit_type):
    n = feat.shape[1] // 2
    first = len(operands) == 1
    if first:
        parts, depth, width = operands[0].shape
        m = parts * width
        more = [
            jax.ShapeDtypeStruct((256, m), BF16),
            jax.ShapeDtypeStruct((parts * (depth - 2 * FEAT), OUTS), BF16),
        ]
    else:
        m = operands[0].shape[1]
        more = []
    return pl.pallas_call(
        functools.partial(tile_kernel, first=first),
        in_specs=[SMEM, VMEM] + [VMEM] * len(operands),
        out_specs=[VMEM] * (2 + len(more)),
        out_shape=[jax.ShapeDtypeStruct((n, m), BF16), jax.ShapeDtypeStruct((n, OUTS), fit_type), *more],
        compiler_params=params(),
        cost_estimate=cost(2 * n * m * 384, 2 * n * m, n * m),
        name="tile_forward",
    )(half, feat, *operands)


def back_kernel(*refs, last):
    tile_ref, fit_ref, *before, out_ref, turned = refs
    parts, share, _ = fit_ref.shape
    for j in range(parts):
        turned[:, j * share : (j + 1) * share] = fit_ref[j].T
    part = jnp.dot(turned[...], tile_ref[...], preferred_element_type=F32)
    if last:
        out_ref[...] = (part + before[0][...]).T.astype(BF16)
    else:
        out_ref[...] = part


def backward(tile, fitted, before=None):
    n, m = tile.shape
    last = before is not None
    return pl.pallas_call(
        functools.partial(back_kernel, last=last),
        in_specs=[VMEM, VMEM] + [VMEM] * last,
        out_specs=VMEM,
        out_shape=jax.ShapeDtypeStruct((m, OUTS), BF16) if last else jax.ShapeDtypeStruct((OUTS, m), F32),
        scratch_shapes=[pltpu.VMEM((OUTS, n), BF16)],
        compiler_params=params(),
        cost_estimate=cost(2 * n * m * OUTS, 2 * n * m),
        name="tile_backward",
    )(tile, fitted, *([before] if last else []))


def chip_at(place, count):
    return place % 2 * (count // 2) + place // 2


def core_columns(pre_ref, here, core, width, count):
    return jnp.concatenate(
        [
            pre_ref[here, pl.ds(pl.multiple_of((2 * chip_at(j, count) + core) * width, width), width)]
            for j in range(count)
        ],
        axis=1,
    )


def field_first_kernel(core_ref, pre_hbm, dir_ref, out_ref, pre_ref, sems):
    blocks = sems.shape[0]
    block = pre_ref.shape[0] // blocks
    copies = [
        pltpu.make_async_copy(pre_hbm.at[pl.ds(j * block, block)], pre_ref.at[pl.ds(j * block, block)], sems.at[j])
        for j in range(blocks)
    ]
    for copy in copies:
        copy.start()
    count, width, outs = dir_ref.shape
    direction = dir_ref[...].reshape(count * width, outs)
    for j in range(blocks):
        copies[j].wait()
        here = slice(j * block, (j + 1) * block)
        columns = core_columns(pre_ref, here, core_ref[0], width, count)
        out_ref[here] = jnp.dot(columns, direction, preferred_element_type=F32)


def field_first(core, precond, direction, blocks=4):
    n, m = precond.shape
    return pl.pallas_call(
        field_first_kernel,
        in_specs=[SMEM, HBM, VMEM],
        out_specs=[VMEM, VMEM],
        out_shape=[jax.ShapeDtypeStruct((n, OUTS), F32), jax.ShapeDtypeStruct((n, m), BF16)],
        scratch_shapes=[pltpu.SemaphoreType.DMA((blocks,))],
        compiler_params=params(),
        cost_estimate=cost(n * m * OUTS, 4 * n * m),
        name="precond_first",
    )(core, in_hbm(precond), direction)


def field_second_kernel(core_ref, pre_ref, dir_ref, before_ref, feat_ref, out_ref):
    parts = out_ref.shape[0]
    share = out_ref.shape[1] - 2 * FEAT
    count, width, outs = dir_ref.shape
    direction = dir_ref[...].reshape(count * width, outs)
    block = 256
    for j in range(pre_ref.shape[0] // block):
        here = slice(j * block, (j + 1) * block)
        columns = core_columns(pre_ref, here, core_ref[0], width, count)
        part = jnp.dot(columns, direction, preferred_element_type=F32) + before_ref[here]
        part = part.astype(BF16)
        for k in range(block // share):
            out_ref[j * (block // share) + k, :share] = part[k * share : (k + 1) * share]
    for j in range(parts):
        out_ref[j, share:] = feat_ref[j]


def field_second(core, precond, direction, before, feat_parts):
    n, m = precond.shape
    parts = feat_parts.shape[0]
    return pl.pallas_call(
        field_second_kernel,
        in_specs=[SMEM, VMEM, VMEM, VMEM, VMEM],
        out_specs=VMEM,
        out_shape=jax.ShapeDtypeStruct((parts, n // parts + 2 * FEAT, OUTS), BF16),
        compiler_params=params(),
        cost_estimate=cost(n * m * OUTS, n * m),
        name="precond_second",
    )(core, precond, direction, before, feat_parts)


def image_kernel(core_ref, pre_ref, grad_ref, out_ref):
    core = core_ref[0]
    chips, width, _ = out_ref.shape
    grad = grad_ref[...].T
    for j in range(0, chips, 2):
        pair = [
            pre_ref[:, pl.ds(pl.multiple_of((2 * chip_at(k, chips) + core) * width, width), width)] for k in (j, j + 1)
        ]
        part = jnp.dot(grad, jnp.concatenate(pair, axis=1), preferred_element_type=F32).T
        out_ref[j] = part[:width]
        out_ref[j + 1] = part[width:]


def image_part(core, precond, grad, share):
    n, m = precond.shape
    return pl.pallas_call(
        image_kernel,
        in_specs=[SMEM, VMEM, VMEM],
        out_specs=VMEM,
        out_shape=jax.ShapeDtypeStruct((m // share // 2, share, OUTS), F32),
        compiler_params=params(),
        cost_estimate=cost(n * m * OUTS, n * m),
        name="precond_backward",
    )(core, precond, grad)


def numbers_kernel(part_ref, dir_ref, res_ref, image_ref, out_ref):
    direction, residual = dir_ref[...], res_ref[...]
    image = jnp.sum(part_ref[...].astype(F32), axis=0) + ridge_weight * direction
    image_ref[...] = image
    top = jnp.max(jnp.max(jnp.abs(image), axis=0, keepdims=True), axis=1, keepdims=True)
    top = jnp.where(top > 0, top, 1.0)
    scaled = image / top

    def total(value):
        return jnp.sum(jnp.sum(value, axis=0, keepdims=True), axis=1, keepdims=True)

    numbers = [total(residual * residual), total(direction * image), total(residual * scaled), total(scaled * scaled), top]
    lane = lax.broadcasted_iota(jnp.int32, (1, 128), 1)
    packed = jnp.zeros((1, 128), F32)
    for place, number in enumerate(numbers):
        packed = jnp.where(lane == place, number, packed)
    out_ref[...] = jnp.broadcast_to(packed, out_ref.shape)


def numbers(parts, direction, residual, devices):
    shape = jax.ShapeDtypeStruct(direction.shape, F32)
    return pl.pallas_call(
        numbers_kernel,
        out_shape=[shape, jax.ShapeDtypeStruct((devices, 128), F32)],
        compiler_params=params(),
        name="image_numbers",
    )(parts, direction, residual)


def finish_kernel(all_ref, image_ref, coef_ref, res_ref, dir_ref, coef_out, res_out, dir_out):
    every = all_ref[...]
    lane = lax.broadcasted_iota(jnp.int32, every.shape, 1)

    def column(place):
        return jnp.sum(jnp.where(lane == place, every, 0.0), axis=1, keepdims=True)

    tops = column(4)
    most = jnp.max(tops, axis=0, keepdims=True)
    ratio = tops / most
    norm_old = jnp.sum(column(0), axis=0, keepdims=True)
    curvature = jnp.sum(column(1), axis=0, keepdims=True)
    cross = jnp.sum(column(2) * ratio, axis=0, keepdims=True)
    square = jnp.sum(column(3) * ratio * ratio, axis=0, keepdims=True)
    step_size = norm_old / curvature
    reach = step_size * most
    norm_new = norm_old - 2.0 * reach * cross + reach * reach * square
    direction = dir_ref[...]
    coef_out[...] = coef_ref[...] + step_size * direction
    residual_next = res_ref[...] - step_size * image_ref[...]
    res_out[...] = residual_next
    dir_out[...] = residual_next + norm_new / norm_old * direction


def finish(every, image, coefficients, residual, direction):
    shape = jax.ShapeDtypeStruct(direction.shape, F32)
    return pl.pallas_call(
        finish_kernel,
        out_shape=[shape, shape, shape],
        compiler_params=params(),
        name="finish",
    )(every, image, coefficients, residual, direction)


def spread(part, axes):
    return lax.all_to_all(part, axes, 0, 0, tiled=True)


def sum_kernel(parts_ref, out_ref, *, scale):
    total = jnp.sum(parts_ref[...].astype(F32), axis=0)
    if scale is not None:
        total = total * scale
    out_ref[...] = jnp.broadcast_to(total.astype(BF16)[None], out_ref.shape)


def all_summed(parts, axes, scale=None):
    own = spread(parts, axes)
    copies = pl.pallas_call(
        functools.partial(sum_kernel, scale=scale),
        out_shape=jax.ShapeDtypeStruct(parts.shape, BF16),
        compiler_params=params(8),
        name="sum_copies",
    )(own)
    return spread(copies, axes)


def swapped(part):
    return lax.ppermute(part, "core", SWAP)


def on_device(train_rows, centre_index, precond, coefficients, residual, direction):
    rows_here = train_rows.shape[0]
    cen_here = centre_index.shape[0]
    row_devices = lax.axis_size("yh") * lax.axis_size("z")
    cen_devices = lax.axis_size("yl") * lax.axis_size("x") * lax.axis_size("core")
    me = lax.axis_index("core").astype(jnp.int32)[None]
    start_row = (lax.axis_index(ROWS) * rows_here).astype(jnp.int32)
    share = cen_here // row_devices

    other = 1 - me
    dir_mine = spread(copies_of(direction, cen_devices // 2), CHIPS)

    feat = train_rows.T
    picked = pick(start_row[None], centre_index[None], feat, row_devices)
    dir_mine, picked, other = lax.optimization_barrier((dir_mine, picked, other))
    dir_came = swapped(dir_mine)
    first, precond_here = field_first(me, precond, dir_mine)
    first, dir_came = lax.optimization_barrier((first, dir_came))
    got = all_summed(field_second(other, precond_here, dir_came, first, picked), ROW_RING)

    chips_shape = (cen_devices // 2, rows_here // cen_devices, OUTS)
    tile_other, fit_other, cen_op, coef = tile_forward(other, feat, [got], F32)
    fit_came = swapped(fit_other)
    tile_mine, fit_mine = tile_forward(me, feat, [cen_op, coef], F32)
    fit_mine, fit_came = lax.optimization_barrier((fit_mine, fit_came))
    half = (fit_mine + fit_came).astype(BF16).reshape(chips_shape)
    fitted = all_summed(half, CHIPS)
    fitted_came = swapped(fitted)
    grad_mine = backward(tile_mine, fitted)
    grad_mine, fitted_came = lax.optimization_barrier((grad_mine, fitted_came))
    grad_part = backward(tile_other, fitted_came, grad_mine).reshape(row_devices, share, OUTS)

    grad_low = all_summed(grad_part, ROW_RING, float(rows_here * row_devices) ** (-0.5)).reshape(cen_here, OUTS)

    image_came = swapped(image_part(other, precond, grad_low, direction.shape[0]))
    image_mine = image_part(me, precond, grad_low, direction.shape[0])
    image_mine, image_came = lax.optimization_barrier((image_mine, image_came))
    half = (image_mine + image_came).astype(BF16)
    image, row = numbers(spread(half, CHIPS), direction, residual, row_devices * cen_devices)
    every = spread(row, (*ROWS, *CENT))
    return tuple(finish(every, image, coefficients, residual, direction))


def solution(mesh):
    fine = Mesh(np.asarray(mesh.devices).reshape([size for _, size in FINE]), [name for name, _ in FINE])
    every = P((*ROWS, *CENT), None)
    return jax.shard_map(
        on_device,
        mesh=fine,
        in_specs=(P(ROWS, None), P(CENT), P(CENT, ROWS), every, every, every),
        out_specs=(every, every, every),
        check_vma=False,
    )
```

```python
import functools
import math

import jax
import jax.numpy as jnp
import numpy as np
from jax import lax
from jax.experimental import pallas as pl
from jax.experimental.pallas import tpu as pltpu
from jax.sharding import Mesh
from jax.sharding import PartitionSpec as P

FEAT = 64
OUTS = 128
ridge_weight = 0.1
F32, BF16 = jnp.float32, jnp.bfloat16

FINE = (("yh", 2), ("z", 4), ("yl", 2), ("x", 4), ("core", 2))
ROWS = ("yh", "z")
ROW_RING = ("z", "yh")
CHIPS = ("x", "yl")
CENT = ("yl", "x", "core")
FEATURE_SCALE = math.sqrt(2.0 * (2.0 / FEAT) * math.log2(math.e))
SWAP = [(0, 1), (1, 0)]


VMEM = pl.BlockSpec(memory_space=pltpu.VMEM)
SMEM = pl.BlockSpec(memory_space=pltpu.SMEM)
HBM = pl.BlockSpec(memory_space=pltpu.HBM)


def params(limit=16):
    return pltpu.CompilerParams(vmem_limit_bytes=limit * 1024 * 1024)


def cost(flops, nbytes, exps=0):
    return pl.CostEstimate(flops=flops, bytes_accessed=nbytes, transcendentals=exps)


def in_hbm(value):
    return pltpu.with_memory_space_constraint(value, pltpu.HBM)


def split_pieces(value, count):
    out = []
    for _ in range(count):
        top = value.astype(BF16)
        out.append(top)
        value = value - top.astype(F32)
    return out


def operand(high, mid, row_side):
    n = high.shape[1]
    value = high.astype(F32) + mid.astype(F32)
    norm = -0.5 * jnp.sum(value * value, axis=0, keepdims=True)
    line = lax.broadcasted_iota(jnp.int32, (FEAT, n), 0)
    tail = jnp.zeros((FEAT, n), F32)
    first_norm, first_one = (0, 3) if row_side else (3, 0)
    for place, piece in enumerate(split_pieces(norm, 3)):
        tail = jnp.where(line == first_norm + place, piece.astype(F32), tail)
    tail = jnp.where((line >= first_one) & (line < first_one + 3), 1.0, tail).astype(BF16)
    middle = (high, mid) if row_side else (mid, high)
    return jnp.concatenate([high, *middle, tail], axis=0)


def pick_kernel(start_ref, index_ref, feat_ref, out_ref, total_ref):
    step = pl.program_id(0)
    block = feat_ref.shape[1]

    @pl.when(step == 0)
    def _():
        total_ref[...] = jnp.zeros_like(total_ref)

    table = jnp.concatenate(split_pieces(feat_ref[...] * FEATURE_SCALE, 2), axis=0)
    wanted = index_ref[...] - (start_ref[0] + step * block)
    place = lax.broadcasted_iota(jnp.int32, (block, wanted.shape[1]), 0)
    choice = jnp.where(place == wanted, 1.0, 0.0).astype(BF16)
    total_ref[...] += jnp.dot(table, choice, preferred_element_type=F32)

    @pl.when(step == pl.num_programs(0) - 1)
    def _():
        for j in range(out_ref.shape[0]):
            width = out_ref.shape[2]
            out_ref[j] = total_ref[:, j * width : (j + 1) * width].astype(BF16)


def pick(start, index, feat, parts, block=512):
    depth, n = feat.shape
    m = index.shape[1]
    return pl.pallas_call(
        pick_kernel,
        grid=(n // block,),
        in_specs=[
            pl.BlockSpec(memory_space=pltpu.SMEM),
            pl.BlockSpec((1, m), lambda i: (0, 0)),
            pl.BlockSpec((depth, block), lambda i: (0, i)),
        ],
        out_specs=pl.BlockSpec((parts, 2 * depth, m // parts), lambda i: (0, 0, 0)),
        out_shape=jax.ShapeDtypeStruct((parts, 2 * depth, m // parts), BF16),
        scratch_shapes=[pltpu.VMEM((2 * depth, m), F32)],
        compiler_params=params(),
        cost_estimate=cost(2 * n * m * 128 * 4, n * depth * 4),
        name="pick_centres",
    )(start, index, feat)


def send_kernel(dir_hbm, out_hbm, dir_ref, low_ref, sems):
    load = pltpu.make_async_copy(dir_hbm, dir_ref, sems.at[0])
    load.start()
    load.wait()
    low_ref[...] = dir_ref[...].astype(BF16)
    stores = [pltpu.make_async_copy(low_ref, out_hbm.at[j], sems.at[1 + j]) for j in range(out_hbm.shape[0])]
    for store in stores:
        store.start()
    for store in stores:
        store.wait()


def copies_of(direction, count):
    return pl.pallas_call(
        send_kernel,
        in_specs=[HBM],
        out_specs=HBM,
        out_shape=pltpu.HBM((count, *direction.shape), BF16),
        scratch_shapes=[
            pltpu.VMEM(direction.shape, F32),
            pltpu.VMEM(direction.shape, BF16),
            pltpu.SemaphoreType.DMA((1 + count,)),
        ],
        compiler_params=params(8),
        name="direction_copies",
    )(in_hbm(direction))


def tile_kernel(*refs, first):
    if first:
        half_ref, feat_ref, got_ref, tile_ref, fit_ref, cen_ref, coef_ref = refs
        parts, depth, width = got_ref.shape
        share = depth - 2 * FEAT
        for j in range(parts):
            both = got_ref[j, share:]
            cen_ref[:, j * width : (j + 1) * width] = operand(both[:FEAT], both[FEAT:], False)
            coef_ref[j * share : (j + 1) * share] = got_ref[j, :share]
    else:
        half_ref, feat_ref, cen_ref, coef_ref, tile_ref, fit_ref = refs
    n = fit_ref.shape[0]
    block = 256
    blocks = n // block
    for j in range(blocks):
        here = slice(j * block, (j + 1) * block)
        place = pl.ds(pl.multiple_of(half_ref[0] * n + j * block, block), block)
        high, mid = split_pieces(feat_ref[:, place] * FEATURE_SCALE, 2)
        power = jnp.dot(operand(high, mid, True).T, cen_ref[...], preferred_element_type=F32)
        tile = jnp.exp2(power).astype(BF16)
        tile_ref[here] = tile
        fit_ref[here] = jnp.dot(tile, coef_ref[...], preferred_element_type=F32).astype(fit_ref.dtype)


def tile_forward(half, feat, operands, fit_type):
    n = feat.shape[1] // 2
    first = len(operands) == 1
    if first:
        parts, depth, width = operands[0].shape
        m = parts * width
        more = [
            jax.ShapeDtypeStruct((256, m), BF16),
            jax.ShapeDtypeStruct((parts * (depth - 2 * FEAT), OUTS), BF16),
        ]
    else:
        m = operands[0].shape[1]
        more = []
    return pl.pallas_call(
        functools.partial(tile_kernel, first=first),
        in_specs=[SMEM, VMEM] + [VMEM] * len(operands),
        out_specs=[VMEM] * (2 + len(more)),
        out_shape=[jax.ShapeDtypeStruct((n, m), BF16), jax.ShapeDtypeStruct((n, OUTS), fit_type), *more],
        compiler_params=params(),
        cost_estimate=cost(2 * n * m * 384, 2 * n * m, n * m),
        name="tile_forward",
    )(half, feat, *operands)


def side_by_side(parts_ref):
    return jnp.concatenate([parts_ref[j] for j in range(parts_ref.shape[0])], axis=1)


def back_kernel(*refs, last):
    tile_ref, fit_ref, *before, out_ref = refs
    part = jnp.dot(side_by_side(fit_ref), tile_ref[...], preferred_element_type=F32)
    if last:
        part = (part + before[0][...]).astype(BF16)
        share = out_ref.shape[2]
        for j in range(out_ref.shape[0]):
            out_ref[j] = part[:, j * share : (j + 1) * share]
    else:
        out_ref[...] = part


def backward(tile, fitted, parts, before=None):
    n, m = tile.shape
    last = before is not None
    whole = jax.ShapeDtypeStruct((parts, OUTS, m // parts), BF16)
    return pl.pallas_call(
        functools.partial(back_kernel, last=last),
        in_specs=[VMEM, VMEM] + [VMEM] * last,
        out_specs=VMEM,
        out_shape=whole if last else jax.ShapeDtypeStruct((OUTS, m), F32),
        compiler_params=params(),
        cost_estimate=cost(2 * n * m * OUTS, 2 * n * m),
        name="tile_backward",
    )(tile, fitted, *([before] if last else []))


def chip_at(place, count):
    return place % 2 * (count // 2) + place // 2


def core_columns(pre_ref, here, core, width, count):
    return jnp.concatenate(
        [
            pre_ref[here, pl.ds(pl.multiple_of((2 * chip_at(j, count) + core) * width, width), width)]
            for j in range(count)
        ],
        axis=1,
    )


def field_first_kernel(core_ref, pre_hbm, dir_ref, out_ref, pre_ref, sems):
    blocks = sems.shape[0]
    block = pre_ref.shape[0] // blocks
    copies = [
        pltpu.make_async_copy(pre_hbm.at[pl.ds(j * block, block)], pre_ref.at[pl.ds(j * block, block)], sems.at[j])
        for j in range(blocks)
    ]
    for copy in copies:
        copy.start()
    count, width, outs = dir_ref.shape
    direction = dir_ref[...].reshape(count * width, outs)
    for j in range(blocks):
        copies[j].wait()
        here = slice(j * block, (j + 1) * block)
        columns = core_columns(pre_ref, here, core_ref[0], width, count)
        out_ref[here] = jnp.dot(columns, direction, preferred_element_type=F32)


def field_first(core, precond, direction, blocks=4):
    n, m = precond.shape
    return pl.pallas_call(
        field_first_kernel,
        in_specs=[SMEM, HBM, VMEM],
        out_specs=[VMEM, VMEM],
        out_shape=[jax.ShapeDtypeStruct((n, OUTS), F32), jax.ShapeDtypeStruct((n, m), BF16)],
        scratch_shapes=[pltpu.SemaphoreType.DMA((blocks,))],
        compiler_params=params(),
        cost_estimate=cost(n * m * OUTS, 4 * n * m),
        name="precond_first",
    )(core, in_hbm(precond), direction)


def field_second_kernel(core_ref, pre_ref, dir_ref, before_ref, feat_ref, out_ref):
    parts = out_ref.shape[0]
    share = out_ref.shape[1] - 2 * FEAT
    count, width, outs = dir_ref.shape
    direction = dir_ref[...].reshape(count * width, outs)
    block = 256
    for j in range(pre_ref.shape[0] // block):
        here = slice(j * block, (j + 1) * block)
        columns = core_columns(pre_ref, here, core_ref[0], width, count)
        part = jnp.dot(columns, direction, preferred_element_type=F32) + before_ref[here]
        part = part.astype(BF16)
        for k in range(block // share):
            out_ref[j * (block // share) + k, :share] = part[k * share : (k + 1) * share]
    for j in range(parts):
        out_ref[j, share:] = feat_ref[j]


def field_second(core, precond, direction, before, feat_parts):
    n, m = precond.shape
    parts = feat_parts.shape[0]
    return pl.pallas_call(
        field_second_kernel,
        in_specs=[SMEM, VMEM, VMEM, VMEM, VMEM],
        out_specs=VMEM,
        out_shape=jax.ShapeDtypeStruct((parts, n // parts + 2 * FEAT, OUTS), BF16),
        compiler_params=params(),
        cost_estimate=cost(n * m * OUTS, n * m),
        name="precond_second",
    )(core, precond, direction, before, feat_parts)


def image_kernel(core_ref, pre_ref, grad_ref, out_ref):
    core = core_ref[0]
    chips, width, _ = out_ref.shape
    grad = side_by_side(grad_ref)
    for j in range(0, chips, 2):
        pair = [
            pre_ref[:, pl.ds(pl.multiple_of((2 * chip_at(k, chips) + core) * width, width), width)] for k in (j, j + 1)
        ]
        part = jnp.dot(grad, jnp.concatenate(pair, axis=1), preferred_element_type=F32).T
        out_ref[j] = part[:width]
        out_ref[j + 1] = part[width:]


def image_part(core, precond, grad, share):
    n, m = precond.shape
    return pl.pallas_call(
        image_kernel,
        in_specs=[SMEM, VMEM, VMEM],
        out_specs=VMEM,
        out_shape=jax.ShapeDtypeStruct((m // share // 2, share, OUTS), F32),
        compiler_params=params(),
        cost_estimate=cost(n * m * OUTS, n * m),
        name="precond_backward",
    )(core, precond, grad)


def numbers_kernel(part_ref, dir_ref, res_ref, image_ref, out_ref):
    direction, residual = dir_ref[...], res_ref[...]
    image = jnp.sum(part_ref[...].astype(F32), axis=0) + ridge_weight * direction
    image_ref[...] = image
    top = jnp.max(jnp.max(jnp.abs(image), axis=0, keepdims=True), axis=1, keepdims=True)
    top = jnp.where(top > 0, top, 1.0)
    scaled = image / top

    def total(value):
        return jnp.sum(jnp.sum(value, axis=0, keepdims=True), axis=1, keepdims=True)

    numbers = [total(residual * residual), total(direction * image), total(residual * scaled), total(scaled * scaled), top]
    lane = lax.broadcasted_iota(jnp.int32, (1, 128), 1)
    packed = jnp.zeros((1, 128), F32)
    for place, number in enumerate(numbers):
        packed = jnp.where(lane == place, number, packed)
    out_ref[...] = jnp.broadcast_to(packed, out_ref.shape)


def numbers(parts, direction, residual, devices):
    shape = jax.ShapeDtypeStruct(direction.shape, F32)
    return pl.pallas_call(
        numbers_kernel,
        out_shape=[shape, jax.ShapeDtypeStruct((devices, 128), F32)],
        compiler_params=params(),
        name="image_numbers",
    )(parts, direction, residual)


def finish_kernel(all_ref, image_ref, coef_ref, res_ref, dir_ref, coef_out, res_out, dir_out):
    every = all_ref[...]
    lane = lax.broadcasted_iota(jnp.int32, every.shape, 1)

    def column(place):
        return jnp.sum(jnp.where(lane == place, every, 0.0), axis=1, keepdims=True)

    tops = column(4)
    most = jnp.max(tops, axis=0, keepdims=True)
    ratio = tops / most
    norm_old = jnp.sum(column(0), axis=0, keepdims=True)
    curvature = jnp.sum(column(1), axis=0, keepdims=True)
    cross = jnp.sum(column(2) * ratio, axis=0, keepdims=True)
    square = jnp.sum(column(3) * ratio * ratio, axis=0, keepdims=True)
    step_size = norm_old / curvature
    reach = step_size * most
    norm_new = norm_old - 2.0 * reach * cross + reach * reach * square
    direction = dir_ref[...]
    coef_out[...] = coef_ref[...] + step_size * direction
    residual_next = res_ref[...] - step_size * image_ref[...]
    res_out[...] = residual_next
    dir_out[...] = residual_next + norm_new / norm_old * direction


def finish(every, image, coefficients, residual, direction):
    shape = jax.ShapeDtypeStruct(direction.shape, F32)
    return pl.pallas_call(
        finish_kernel,
        out_shape=[shape, shape, shape],
        compiler_params=params(),
        name="finish",
    )(every, image, coefficients, residual, direction)


def spread(part, axes):
    return lax.all_to_all(part, axes, 0, 0, tiled=True)


def sum_kernel(parts_ref, out_ref, *, scale, turn):
    total = jnp.sum(parts_ref[...].astype(F32), axis=0)
    if scale is not None:
        total = total * scale
    if turn:
        total = total.T
    out_ref[...] = jnp.broadcast_to(total.astype(BF16)[None], out_ref.shape)


def all_summed(parts, axes, scale=None, turn=False):
    count, first, second = parts.shape
    copies = pl.pallas_call(
        functools.partial(sum_kernel, scale=scale, turn=turn),
        out_shape=jax.ShapeDtypeStruct((count, second, first) if turn else parts.shape, BF16),
        compiler_params=params(8),
        name="sum_copies",
    )(spread(parts, axes))
    return spread(copies, axes)


def swapped(part):
    return lax.ppermute(part, "core", SWAP)


def on_device(train_rows, centre_index, precond, coefficients, residual, direction):
    rows_here = train_rows.shape[0]
    cen_here = centre_index.shape[0]
    row_devices = lax.axis_size("yh") * lax.axis_size("z")
    cen_devices = lax.axis_size("yl") * lax.axis_size("x") * lax.axis_size("core")
    me = lax.axis_index("core").astype(jnp.int32)[None]
    start_row = (lax.axis_index(ROWS) * rows_here).astype(jnp.int32)
    share = cen_here // row_devices

    other = 1 - me
    dir_mine = spread(copies_of(direction, cen_devices // 2), CHIPS)

    feat = train_rows.T
    picked = pick(start_row[None], centre_index[None], feat, row_devices)
    dir_mine, picked, other = lax.optimization_barrier((dir_mine, picked, other))
    dir_came = swapped(dir_mine)
    first, precond_here = field_first(me, precond, dir_mine)
    first, dir_came = lax.optimization_barrier((first, dir_came))
    got = all_summed(field_second(other, precond_here, dir_came, first, picked), ROW_RING)

    chips_shape = (cen_devices // 2, rows_here // cen_devices, OUTS)
    tile_other, fit_other, cen_op, coef = tile_forward(other, feat, [got], F32)
    fit_came = swapped(fit_other)
    tile_mine, fit_mine = tile_forward(me, feat, [cen_op, coef], F32)
    fit_mine, fit_came = lax.optimization_barrier((fit_mine, fit_came))
    half = (fit_mine + fit_came).astype(BF16).reshape(chips_shape)
    fitted = all_summed(half, CHIPS, turn=True)
    fitted_came = swapped(fitted)
    grad_mine = backward(tile_mine, fitted, row_devices)
    grad_mine, fitted_came = lax.optimization_barrier((grad_mine, fitted_came))
    grad_part = backward(tile_other, fitted_came, row_devices, grad_mine)
    grad_low = all_summed(grad_part, ROW_RING, float(rows_here * row_devices) ** (-0.5))

    image_came = swapped(image_part(other, precond, grad_low, direction.shape[0]))
    image_mine = image_part(me, precond, grad_low, direction.shape[0])
    image_mine, image_came = lax.optimization_barrier((image_mine, image_came))
    half = (image_mine + image_came).astype(BF16)
    image, row = numbers(spread(half, CHIPS), direction, residual, row_devices * cen_devices)
    every = spread(row, (*ROWS, *CENT))
    return tuple(finish(every, image, coefficients, residual, direction))


def solution(mesh):
    fine = Mesh(np.asarray(mesh.devices).reshape([size for _, size in FINE]), [name for name, _ in FINE])
    every = P((*ROWS, *CENT), None)
    return jax.shard_map(
        on_device,
        mesh=fine,
        in_specs=(P(ROWS, None), P(CENT), P(CENT, ROWS), every, every, every),
        out_specs=(every, every, every),
        check_vma=False,
    )
```

```python
import functools
import math

import jax
import jax.numpy as jnp
import numpy as np
from jax import lax
from jax.experimental import pallas as pl
from jax.experimental.pallas import tpu as pltpu
from jax.sharding import Mesh
from jax.sharding import PartitionSpec as P

FEAT = 64
OUTS = 128
ridge_weight = 0.1
F32, BF16 = jnp.float32, jnp.bfloat16

FINE = (("yh", 2), ("z", 4), ("yl", 2), ("x", 4), ("core", 2))
ROWS = ("yh", "z")
ROW_RING = ("z", "yh")
CHIPS = ("x", "yl")
CENT = ("yl", "x", "core")
FEATURE_SCALE = math.sqrt(2.0 * (2.0 / FEAT) * math.log2(math.e))
SWAP = [(0, 1), (1, 0)]


VMEM = pl.BlockSpec(memory_space=pltpu.VMEM)
SMEM = pl.BlockSpec(memory_space=pltpu.SMEM)
HBM = pl.BlockSpec(memory_space=pltpu.HBM)


def params(limit=16):
    return pltpu.CompilerParams(vmem_limit_bytes=limit * 1024 * 1024)


def cost(flops, nbytes, exps=0):
    return pl.CostEstimate(flops=flops, bytes_accessed=nbytes, transcendentals=exps)


def in_hbm(value):
    return pltpu.with_memory_space_constraint(value, pltpu.HBM)


def split_pieces(value, count):
    out = []
    for _ in range(count):
        top = value.astype(BF16)
        out.append(top)
        value = value - top.astype(F32)
    return out


def operand(high, mid, row_side):
    n = high.shape[1]
    value = high.astype(F32) + mid.astype(F32)
    norm = -0.5 * jnp.sum(value * value, axis=0, keepdims=True)
    line = lax.broadcasted_iota(jnp.int32, (FEAT, n), 0)
    tail = jnp.zeros((FEAT, n), F32)
    first_norm, first_one = (0, 3) if row_side else (3, 0)
    for place, piece in enumerate(split_pieces(norm, 3)):
        tail = jnp.where(line == first_norm + place, piece.astype(F32), tail)
    tail = jnp.where((line >= first_one) & (line < first_one + 3), 1.0, tail).astype(BF16)
    middle = (high, mid) if row_side else (mid, high)
    return jnp.concatenate([high, *middle, tail], axis=0)


def pick_kernel(start_ref, index_ref, feat_ref, out_ref, total_ref):
    step = pl.program_id(0)
    block = feat_ref.shape[1]

    @pl.when(step == 0)
    def _():
        total_ref[...] = jnp.zeros_like(total_ref)

    table = jnp.concatenate(split_pieces(feat_ref[...] * FEATURE_SCALE, 2), axis=0)
    wanted = index_ref[...] - (start_ref[0] + step * block)
    place = lax.broadcasted_iota(jnp.int32, (block, wanted.shape[1]), 0)
    choice = jnp.where(place == wanted, 1.0, 0.0).astype(BF16)
    total_ref[...] += jnp.dot(table, choice, preferred_element_type=F32)

    @pl.when(step == pl.num_programs(0) - 1)
    def _():
        for j in range(out_ref.shape[0]):
            width = out_ref.shape[2]
            out_ref[j] = total_ref[:, j * width : (j + 1) * width].astype(BF16)


def pick(start, index, feat, parts, block=512):
    depth, n = feat.shape
    m = index.shape[1]
    return pl.pallas_call(
        pick_kernel,
        grid=(n // block,),
        in_specs=[
            pl.BlockSpec(memory_space=pltpu.SMEM),
            pl.BlockSpec((1, m), lambda i: (0, 0)),
            pl.BlockSpec((depth, block), lambda i: (0, i)),
        ],
        out_specs=pl.BlockSpec((parts, 2 * depth, m // parts), lambda i: (0, 0, 0)),
        out_shape=jax.ShapeDtypeStruct((parts, 2 * depth, m // parts), BF16),
        scratch_shapes=[pltpu.VMEM((2 * depth, m), F32)],
        compiler_params=params(),
        cost_estimate=cost(2 * n * m * 128 * 4, n * depth * 4),
        name="pick_centres",
    )(start, index, feat)


def send_kernel(dir_hbm, out_hbm, dir_ref, low_ref, sems):
    load = pltpu.make_async_copy(dir_hbm, dir_ref, sems.at[0])
    load.start()
    load.wait()
    low_ref[...] = dir_ref[...].astype(BF16)
    stores = [pltpu.make_async_copy(low_ref, out_hbm.at[j], sems.at[1 + j]) for j in range(out_hbm.shape[0])]
    for store in stores:
        store.start()
    for store in stores:
        store.wait()


def copies_of(direction, count):
    return pl.pallas_call(
        send_kernel,
        in_specs=[HBM],
        out_specs=HBM,
        out_shape=pltpu.HBM((count, *direction.shape), BF16),
        scratch_shapes=[
            pltpu.VMEM(direction.shape, F32),
            pltpu.VMEM(direction.shape, BF16),
            pltpu.SemaphoreType.DMA((1 + count,)),
        ],
        compiler_params=params(8),
        name="direction_copies",
    )(in_hbm(direction))


def tile_kernel(*refs, first):
    if first:
        half_ref, feat_ref, got_ref, tile_ref, fit_ref, cen_ref, coef_ref = refs
        parts, depth, width = got_ref.shape
        share = depth - 2 * FEAT
        for j in range(parts):
            both = got_ref[j, share:]
            cen_ref[:, j * width : (j + 1) * width] = operand(both[:FEAT], both[FEAT:], False)
            coef_ref[j * share : (j + 1) * share] = got_ref[j, :share]
    else:
        half_ref, feat_ref, cen_ref, coef_ref, tile_ref, fit_ref = refs
    n = fit_ref.shape[0]
    block = 256
    blocks = n // block
    for j in range(blocks):
        here = slice(j * block, (j + 1) * block)
        place = pl.ds(pl.multiple_of(half_ref[0] * n + j * block, block), block)
        high, mid = split_pieces(feat_ref[:, place] * FEATURE_SCALE, 2)
        power = jnp.dot(operand(high, mid, True).T, cen_ref[...], preferred_element_type=F32)
        tile = jnp.exp2(power).astype(BF16)
        tile_ref[here] = tile
        fit_ref[here] = jnp.dot(tile, coef_ref[...], preferred_element_type=F32).astype(fit_ref.dtype)


def tile_forward(half, feat, operands, fit_type):
    n = feat.shape[1] // 2
    first = len(operands) == 1
    if first:
        parts, depth, width = operands[0].shape
        m = parts * width
        more = [
            jax.ShapeDtypeStruct((256, m), BF16),
            jax.ShapeDtypeStruct((parts * (depth - 2 * FEAT), OUTS), BF16),
        ]
    else:
        m = operands[0].shape[1]
        more = []
    return pl.pallas_call(
        functools.partial(tile_kernel, first=first),
        in_specs=[SMEM, VMEM] + [VMEM] * len(operands),
        out_specs=[VMEM] * (2 + len(more)),
        out_shape=[jax.ShapeDtypeStruct((n, m), BF16), jax.ShapeDtypeStruct((n, OUTS), fit_type), *more],
        compiler_params=params(),
        cost_estimate=cost(2 * n * m * 384, 2 * n * m, n * m),
        name="tile_forward",
    )(half, feat, *operands)


def side_by_side(parts_ref):
    return jnp.concatenate([parts_ref[j] for j in range(parts_ref.shape[0])], axis=1)


def back_kernel(*refs, last):
    tile_ref, fit_ref, *before, out_ref = refs
    part = jnp.dot(side_by_side(fit_ref), tile_ref[...], preferred_element_type=F32)
    if last:
        part = (part + before[0][...]).astype(BF16)
        share = out_ref.shape[2]
        for j in range(out_ref.shape[0]):
            out_ref[j] = part[:, j * share : (j + 1) * share]
    else:
        out_ref[...] = part


def backward(tile, fitted, parts, before=None):
    n, m = tile.shape
    last = before is not None
    whole = jax.ShapeDtypeStruct((parts, OUTS, m // parts), BF16)
    return pl.pallas_call(
        functools.partial(back_kernel, last=last),
        in_specs=[VMEM, VMEM] + [VMEM] * last,
        out_specs=VMEM,
        out_shape=whole if last else jax.ShapeDtypeStruct((OUTS, m), F32),
        compiler_params=params(),
        cost_estimate=cost(2 * n * m * OUTS, 2 * n * m),
        name="tile_backward",
    )(tile, fitted, *([before] if last else []))


def chip_at(place, count):
    return place % 2 * (count // 2) + place // 2


def core_columns(pre_ref, here, core, width, count):
    return jnp.concatenate(
        [
            pre_ref[here, pl.ds(pl.multiple_of((2 * chip_at(j, count) + core) * width, width), width)]
            for j in range(count)
        ],
        axis=1,
    )


def field_first_kernel(core_ref, pre_hbm, dir_ref, out_ref, pre_ref, sems):
    blocks = sems.shape[0]
    block = pre_ref.shape[0] // blocks
    copies = [
        pltpu.make_async_copy(pre_hbm.at[pl.ds(j * block, block)], pre_ref.at[pl.ds(j * block, block)], sems.at[j])
        for j in range(blocks)
    ]
    for copy in copies:
        copy.start()
    count, width, outs = dir_ref.shape
    direction = dir_ref[...].reshape(count * width, outs)
    for j in range(blocks):
        copies[j].wait()
        here = slice(j * block, (j + 1) * block)
        columns = core_columns(pre_ref, here, core_ref[0], width, count)
        out_ref[here] = jnp.dot(columns, direction, preferred_element_type=F32)


def field_first(core, precond, direction, blocks=4):
    n, m = precond.shape
    return pl.pallas_call(
        field_first_kernel,
        in_specs=[SMEM, HBM, VMEM],
        out_specs=[VMEM, VMEM],
        out_shape=[jax.ShapeDtypeStruct((n, OUTS), F32), jax.ShapeDtypeStruct((n, m), BF16)],
        scratch_shapes=[pltpu.SemaphoreType.DMA((blocks,))],
        compiler_params=params(),
        cost_estimate=cost(n * m * OUTS, 4 * n * m),
        name="precond_first",
    )(core, in_hbm(precond), direction)


def field_second_kernel(core_ref, pre_ref, dir_ref, before_ref, feat_ref, out_ref):
    parts = out_ref.shape[0]
    share = out_ref.shape[1] - 2 * FEAT
    count, width, outs = dir_ref.shape
    direction = dir_ref[...].reshape(count * width, outs)
    block = 256
    for j in range(pre_ref.shape[0] // block):
        here = slice(j * block, (j + 1) * block)
        columns = core_columns(pre_ref, here, core_ref[0], width, count)
        part = jnp.dot(columns, direction, preferred_element_type=F32) + before_ref[here]
        part = part.astype(BF16)
        for k in range(block // share):
            out_ref[j * (block // share) + k, :share] = part[k * share : (k + 1) * share]
    for j in range(parts):
        out_ref[j, share:] = feat_ref[j]


def field_second(core, precond, direction, before, feat_parts):
    n, m = precond.shape
    parts = feat_parts.shape[0]
    return pl.pallas_call(
        field_second_kernel,
        in_specs=[SMEM, VMEM, VMEM, VMEM, VMEM],
        out_specs=VMEM,
        out_shape=jax.ShapeDtypeStruct((parts, n // parts + 2 * FEAT, OUTS), BF16),
        compiler_params=params(),
        cost_estimate=cost(n * m * OUTS, n * m),
        name="precond_second",
    )(core, precond, direction, before, feat_parts)


def image_kernel(core_ref, pre_ref, grad_ref, out_ref):
    core = core_ref[0]
    chips, width, _ = out_ref.shape
    grad = side_by_side(grad_ref)
    for j in range(0, chips, 2):
        pair = [
            pre_ref[:, pl.ds(pl.multiple_of((2 * chip_at(k, chips) + core) * width, width), width)] for k in (j, j + 1)
        ]
        part = jnp.dot(grad, jnp.concatenate(pair, axis=1), preferred_element_type=F32).T
        out_ref[j] = part[:width]
        out_ref[j + 1] = part[width:]


def image_part(core, precond, grad, share):
    n, m = precond.shape
    return pl.pallas_call(
        image_kernel,
        in_specs=[SMEM, VMEM, VMEM],
        out_specs=VMEM,
        out_shape=jax.ShapeDtypeStruct((m // share // 2, share, OUTS), F32),
        compiler_params=params(),
        cost_estimate=cost(n * m * OUTS, n * m),
        name="precond_backward",
    )(core, precond, grad)


def numbers_kernel(part_ref, dir_ref, res_ref, image_ref, out_ref):
    direction, residual = dir_ref[...], res_ref[...]
    image = jnp.sum(part_ref[...].astype(F32), axis=0) + ridge_weight * direction
    image_ref[...] = image
    top = jnp.max(jnp.max(jnp.abs(image), axis=0, keepdims=True), axis=1, keepdims=True)
    top = jnp.where(top > 0, top, 1.0)
    scaled = image / top

    def total(value):
        return jnp.sum(jnp.sum(value, axis=0, keepdims=True), axis=1, keepdims=True)

    numbers = [total(residual * residual), total(direction * image), total(residual * scaled), total(scaled * scaled), top]
    lane = lax.broadcasted_iota(jnp.int32, (1, 128), 1)
    packed = jnp.zeros((1, 128), F32)
    for place, number in enumerate(numbers):
        packed = jnp.where(lane == place, number, packed)
    out_ref[...] = jnp.broadcast_to(packed, out_ref.shape)


def numbers(parts, direction, residual, devices):
    shape = jax.ShapeDtypeStruct(direction.shape, F32)
    return pl.pallas_call(
        numbers_kernel,
        out_shape=[shape, jax.ShapeDtypeStruct((devices, 128), F32)],
        compiler_params=params(),
        name="image_numbers",
    )(parts, direction, residual)


def finish_kernel(all_ref, image_ref, coef_ref, res_ref, dir_ref, coef_out, res_out, dir_out):
    every = all_ref[...]
    lane = lax.broadcasted_iota(jnp.int32, every.shape, 1)

    def column(place):
        return jnp.sum(jnp.where(lane == place, every, 0.0), axis=1, keepdims=True)

    tops = column(4)
    most = jnp.max(tops, axis=0, keepdims=True)
    ratio = tops / most
    norm_old = jnp.sum(column(0), axis=0, keepdims=True)
    curvature = jnp.sum(column(1), axis=0, keepdims=True)
    cross = jnp.sum(column(2) * ratio, axis=0, keepdims=True)
    square = jnp.sum(column(3) * ratio * ratio, axis=0, keepdims=True)
    step_size = norm_old / curvature
    reach = step_size * most
    norm_new = norm_old - 2.0 * reach * cross + reach * reach * square
    direction = dir_ref[...]
    coef_out[...] = coef_ref[...] + step_size * direction
    residual_next = res_ref[...] - step_size * image_ref[...]
    res_out[...] = residual_next
    dir_out[...] = residual_next + norm_new / norm_old * direction


def finish(every, image, coefficients, residual, direction):
    shape = jax.ShapeDtypeStruct(direction.shape, F32)
    return pl.pallas_call(
        finish_kernel,
        out_shape=[shape, shape, shape],
        compiler_params=params(),
        name="finish",
    )(every, image, coefficients, residual, direction)


def spread(part, axes):
    return lax.all_to_all(part, axes, 0, 0, tiled=True)


def sum_kernel(parts_ref, out_ref, *, scale, turn):
    total = jnp.sum(parts_ref[...].astype(F32), axis=0)
    if scale is not None:
        total = total * scale
    if turn:
        total = total.T
    out_ref[...] = jnp.broadcast_to(total.astype(BF16)[None], out_ref.shape)


def all_summed(parts, axes, scale=None, turn=False):
    count, first, second = parts.shape
    copies = pl.pallas_call(
        functools.partial(sum_kernel, scale=scale, turn=turn),
        out_shape=jax.ShapeDtypeStruct((count, second, first) if turn else parts.shape, BF16),
        compiler_params=params(8),
        name="sum_copies",
    )(spread(parts, axes))
    return spread(copies, axes)


def swapped(part):
    return lax.ppermute(part, "core", SWAP)


def on_device(train_rows, centre_index, precond, coefficients, residual, direction):
    rows_here = train_rows.shape[0]
    cen_here = centre_index.shape[0]
    row_devices = lax.axis_size("yh") * lax.axis_size("z")
    cen_devices = lax.axis_size("yl") * lax.axis_size("x") * lax.axis_size("core")
    me = lax.axis_index("core").astype(jnp.int32)[None]
    start_row = (lax.axis_index(ROWS) * rows_here).astype(jnp.int32)
    share = cen_here // row_devices

    other = 1 - me
    dir_mine = spread(copies_of(direction, cen_devices // 2), CHIPS)

    feat = train_rows.T
    picked = pick(start_row[None], centre_index[None], feat, row_devices)
    dir_mine, picked, other = lax.optimization_barrier((dir_mine, picked, other))
    dir_came = swapped(dir_mine)
    first, precond_here = field_first(me, precond, dir_mine)
    first, dir_came = lax.optimization_barrier((first, dir_came))
    got = all_summed(field_second(other, precond_here, dir_came, first, picked), ROW_RING)

    chips_shape = (cen_devices // 2, rows_here // cen_devices, OUTS)
    tile_other, fit_other, cen_op, coef = tile_forward(other, feat, [got], F32)
    fit_came = swapped(fit_other)
    tile_mine, fit_mine = tile_forward(me, feat, [cen_op, coef], F32)
    fit_mine, fit_came = lax.optimization_barrier((fit_mine, fit_came))
    half = (fit_mine + fit_came).astype(BF16).reshape(chips_shape)
    fitted = all_summed(half, CHIPS, turn=True)
    fitted_came = swapped(fitted)
    grad_mine = backward(tile_mine, fitted, row_devices)
    grad_mine, fitted_came = lax.optimization_barrier((grad_mine, fitted_came))
    grad_part = backward(tile_other, fitted_came, row_devices, grad_mine)
    grad_low = all_summed(grad_part, ROW_RING, float(rows_here * row_devices) ** (-0.5))

    image_came = swapped(image_part(other, precond, grad_low, direction.shape[0]))
    image_mine = image_part(me, precond, grad_low, direction.shape[0])
    image_mine, image_came = lax.optimization_barrier((image_mine, image_came))
    half = (image_mine + image_came).astype(BF16)
    image, row = numbers(spread(half, CHIPS), direction, residual, row_devices * cen_devices)
    every = spread(row, ("core", *ROW_RING, *CHIPS))
    return tuple(finish(every, image, coefficients, residual, direction))


def solution(mesh):
    fine = Mesh(np.asarray(mesh.devices).reshape([size for _, size in FINE]), [name for name, _ in FINE])
    every = P((*ROWS, *CENT), None)
    return jax.shard_map(
        on_device,
        mesh=fine,
        in_specs=(P(ROWS, None), P(CENT), P(CENT, ROWS), every, every, every),
        out_specs=(every, every, every),
        check_vma=False,
    )
```
